32 devices in a mesh: req: 4 (over z), seq: 2 (over core), exp: 4 (over y, x).
Axes of the slice: x: 2, y: 2, z: 4, core: 2. Of those that a mesh axis runs over, the one named last changes fastest.
Arguments:
- residual: bfloat16 [64, 7168], P(('req', 'seq', 'exp')), may hold values from -6 to 6
- queries: bfloat16 [4, 16, 128, 576], P('req', None, 'exp'), may hold values from -60 to 60
- latent_cache: bfloat16 [4, 384, 576], P('req', 'seq'), may hold values from -20 to 20
- blocks: int32 [4, 2, 2], P('req', 'seq'), may hold values from 0 to 2, as said below
- lengths: int32 [4], P('req'), may hold values from 208 to 384, as said below
- value_up: bfloat16 [128, 512, 128], P('exp'), may hold values from -0.25 to 0.25
- out_proj: bfloat16 [16384, 7168], P('exp', ('req', 'seq')), may hold values from -0.046875 to 0.046875
- norm_gain: bfloat16 [7168], replicated, may hold values from 0.099609375 to 1.8984375
- router: bfloat16 [7168, 4], replicated, may hold values from -0.0625 to 0.0625
- expert_ids: int32 [64, 2], P(('req', 'seq', 'exp')), may hold values from 0 to 3, all different within a row; in each aligned block of 2 rows (0 to 1, 2 to 3, ...) at most 2 rows name the same one
- w_gate: bfloat16 [4, 7168, 2048], P('req', None, ('seq', 'exp')), may hold values from -0.0625 to 0.0625
- w_up: bfloat16 [4, 7168, 2048], P('req', None, ('seq', 'exp')), may hold values from -0.0625 to 0.0625
- w_down: bfloat16 [4, 2048, 7168], P('req', ('seq', 'exp')), may hold values from -0.125 to 0.125
Outputs:
- layer_out: bfloat16 [64, 7168], P(('req', 'seq', 'exp'))
The draws below stay inside these ranges and needn't reach their ends.
Inputs may be any that keep to these rules, and one draw needn't show every extreme that they name: `blocks`: each request and shard lists 2 different block numbers of that shard. `lengths`: some request has exactly 384, some exactly 208. `expert_ids`: each row names 2 different experts; among the rows of one device (aligned blocks of 2 rows) no expert is named more than 2 times, a bound that some block reaches.
All inputs are finite; a program needn't handle non-finite values.
Results may differ from the reference program's by a relative error of at most 0.019.
Values may be sent and summed in bfloat16 or wider, within the bound.
A program may use at most 128 MiB of HBM per device.

```python
import math
import jax
import jax.numpy as jnp
import numpy as np
from jax import lax

D = 7168
H = 128
DL = 512
DR = 64
DV = 128
FF = 2048
BLOCK = 64
SHARD_BLOCKS = 3
NSEL = 2
NT = 2
QT = 16
CAP = 2
REQUESTS = 4
TOKENS = 64
EXPERTS = 4
TOPK = 2
CTX_HALF = 192
CTX = 384
N_SEQ = 2
N_EXP = 4


def pick_blocks(key):
    scores = jax.random.randint(jax.random.fold_in(key, 22), (REQUESTS, N_SEQ, SHARD_BLOCKS), 0, 1 << 20)
    scores = scores * SHARD_BLOCKS + jnp.arange(SHARD_BLOCKS, dtype=jnp.int32)
    order = jnp.argsort(scores, axis=-1, stable=True)
    return order[..., :NSEL].astype(jnp.int32)


def cache_values(key):
    normal_part = jnp.clip(jax.random.normal(jax.random.fold_in(key, 11), (REQUESTS, CTX, DL + DR), jnp.float32), -4.0, 4.0)
    return normal_part


def draw_latent_cache(key, part):
    return cache_values(key).astype(jnp.bfloat16)


def draw_blocks(key, part):
    return pick_blocks(key)


def draw_lengths(key, part):
    drawn = jax.random.randint(jax.random.fold_in(key, 33), (REQUESTS,), CTX_HALF + QT, CTX + 1)
    return drawn.at[0].set(CTX).at[1].set(CTX_HALF + QT).astype(jnp.int32)


def draw_queries(key, part):
    normal_part = jnp.clip(jax.random.normal(jax.random.fold_in(key, 44), (REQUESTS, QT, H, DL + DR), jnp.float32), -4.0, 4.0)
    return normal_part.astype(jnp.bfloat16)


def block_levels(rng, dims, shards, least, largest):
    loudness = 1.0
    for dim, shards_of in shards:
        heights = jax.random.uniform(jax.random.fold_in(jax.random.fold_in(rng, 6), dim), (shards_of,), jnp.float32, least / len(shards), largest / len(shards))
        loudness = loudness * jnp.repeat(jnp.exp(heights), dims[dim] // shards_of).reshape((-1,) + (1,) * (len(dims) - 1 - dim))
    return loudness


def shared_out(rng, own, number, rows, amount, top, limit, skew):
    order = jax.random.permutation(rng, amount)
    heavy_load, usual = load_shares(amount, rows * top, limit, skew, True), load_shares(amount, rows * top, limit, skew, False)
    places = jnp.arange(amount)

    def named(tallies, turn):
        used = int((tallies > 0).sum())
        fixed = max(1, used // 4)
        moved = fixed + (places - fixed + turn * (used - fixed)) % max(1, amount - fixed)
        return jnp.zeros((amount,), jnp.int32).at[order[jnp.where(places < fixed, places, moved)]].set(jnp.asarray(tallies, jnp.int32))

    tallies = jnp.where(number % 4 == 0, named(heavy_load, number // 4), named(usual, number - number // 4 - 1))
    mixed = jax.random.permutation(jax.random.fold_in(own, 3), amount)
    source_of, sink = mixed[0:amount // 2 * 2:2], mixed[1:amount // 2 * 2:2]
    margin = jnp.minimum(tallies[source_of] - 1, limit - tallies[sink]) // 2
    margin = jnp.where((source_of == order[0]) | (sink == order[0]) | (tallies[sink] == 0), 0, jnp.maximum(margin, 0))
    moved = jax.random.randint(jax.random.fold_in(own, 4), (amount // 2,), 0, 1 << 20) % (margin + 1)
    tallies = tallies.at[source_of].add(-moved).at[sink].add(moved)
    items = jnp.searchsorted(jnp.cumsum(tallies), jnp.arange(rows * top), side="right").astype(jnp.int32)
    listing = items.reshape(top, rows).T
    listing = listing[jax.random.permutation(jax.random.fold_in(own, 1), rows)]
    turn = jax.random.randint(jax.random.fold_in(own, 2), (rows, 1), 0, top)
    return jnp.take_along_axis(listing, (jnp.arange(top)[None, :] + turn) % top, axis=1)


def load_shares(amount, total, bound, skew, full):
    portions = [(1 << 20) // math.isqrt(rank ** skew) + 1 for rank in range(1, amount + 1)]
    largest = bound if full else min(bound, max(-(-total // amount), total * portions[0] // sum(portions)))
    least = 1 if total - largest >= amount - 1 else 0
    counts, surplus = [largest] + [least] * (amount - 1), total - largest - least * (amount - 1)
    while surplus > 0:
        candidates = [i for i in range(1, amount) if counts[i] < largest] or [i for i in range(1, amount) if counts[i] < bound]
        whole, remaining = sum([portions[i] for i in candidates]), surplus
        for i in candidates:
            more = min(bound - counts[i], max(1, remaining * portions[i] // whole), surplus)
            counts[i] = counts[i] + more
            surplus = surplus - more
    return np.array(counts)


def bell_draw(stream_key, extent, spread, bound, cuts=(), held_as=jnp.bfloat16):
    factor_of = block_levels(stream_key, extent, cuts, -0.22, 0.18) if cuts else 1.0
    values = jax.random.normal(stream_key, extent, jnp.float32) * spread * factor_of
    return jnp.minimum(jnp.maximum(values, -bound), bound).astype(held_as)


def setup_inputs(seed: int = 0) -> dict:
    arg_keys = jax.random.split(jax.random.key(seed), 14)
    residual = bell_draw(arg_keys[0], (TOKENS, D), 1.0, 6.0, ((0, 32),))
    queries = draw_queries(jax.random.fold_in(arg_keys[13], 71), 0)
    latent_cache = draw_latent_cache(jax.random.fold_in(arg_keys[13], 71), 0)
    blocks = draw_blocks(jax.random.fold_in(arg_keys[13], 71), 0)
    lengths = draw_lengths(jax.random.fold_in(arg_keys[13], 71), 0)
    value_up = bell_draw(arg_keys[5], (H, DL, DV), DL ** -0.5, 0.25, ((0, 4),))
    out_proj = bell_draw(arg_keys[6], (H * DV, D), (H * DV) ** -0.5, 0.046875, ((0, 4), (1, 8)))
    norm_gain = jnp.clip(1.0 + 0.18 * jax.random.normal(arg_keys[7], (D,), jnp.float32), 0.099609375, 1.8984375).astype(jnp.bfloat16)
    router = bell_draw(arg_keys[8], (D, EXPERTS), D ** -0.5, 0.0625)
    expert_ids_keys = jax.random.split(jax.random.fold_in(arg_keys[9], 1), TOKENS // NT)
    expert_ids_turns = jax.random.permutation(jax.random.fold_in(arg_keys[9], 3), TOKENS // NT)
    expert_ids = jax.vmap(lambda own, number: shared_out(jax.random.fold_in(arg_keys[9], 2), own, number, NT, EXPERTS, TOPK, CAP, 2))(expert_ids_keys, expert_ids_turns).reshape((TOKENS, TOPK))
    w_gate = bell_draw(arg_keys[10], (EXPERTS, D, FF), D ** -0.5, 0.0625, ((0, 4), (2, 8)))
    w_up = bell_draw(arg_keys[11], (EXPERTS, D, FF), D ** -0.5, 0.0625, ((0, 4), (2, 8)))
    w_down = bell_draw(arg_keys[12], (EXPERTS, FF, D), FF ** -0.5, 0.125, ((0, 4), (1, 8)))
    return dict(residual=residual, queries=queries, latent_cache=latent_cache, blocks=blocks, lengths=lengths, value_up=value_up, out_proj=out_proj, norm_gain=norm_gain, router=router, expert_ids=expert_ids, w_gate=w_gate, w_up=w_up, w_down=w_down)


def pick_rows(block_rows, picks):
    return block_rows[picks]

def shard_partial(queries32, latent_cache, blocks, lengths, shard):
    region = latent_cache[:, shard * CTX_HALF:(shard + 1) * CTX_HALF]
    region = region.reshape(REQUESTS, SHARD_BLOCKS, BLOCK, DL + DR)
    picked = jax.vmap(pick_rows)(region, blocks[:, shard]).reshape(REQUESTS, NSEL * BLOCK, DL + DR)
    positions = shard * CTX_HALF + blocks[:, shard, :, None] * BLOCK + jnp.arange(BLOCK, dtype=jnp.int32)
    positions = positions.reshape(REQUESTS, NSEL * BLOCK)
    limits = lengths[:, None] - (QT - 1) + jnp.arange(QT, dtype=jnp.int32)[None, :]
    usable = positions[:, None, None, :] < limits[:, :, None, None]
    key_rows = picked.astype(jnp.float32)
    scores = jnp.einsum('bqhk,bjk->bqhj', queries32, key_rows) * (DV + DR) ** (-0.5)
    row_max = lax.optimization_barrier(jnp.max(jnp.where(usable, scores, -1e+30), axis=-1))
    weights = jnp.where(usable, jnp.exp(scores - row_max[..., None]), 0.0).astype(jnp.bfloat16).astype(jnp.float32)
    row_sum = lax.optimization_barrier(jnp.sum(weights, -1))
    weighted = jnp.einsum('bqhj,bjd->bqhd', weights, key_rows[..., :DL])
    return (row_max, row_sum, weighted)

def reference(residual, queries, latent_cache, blocks, lengths, value_up, out_proj, norm_gain, router, expert_ids, w_gate, w_up, w_down):
    queries32 = queries.astype(jnp.float32)
    pieces_list = [shard_partial(queries32, latent_cache, blocks, lengths, shard) for shard in range(N_SEQ)]
    overall = pieces_list[0][0]
    for entry in pieces_list[1:]:
        overall = jnp.maximum(overall, entry[0])
    totals = jnp.zeros_like(overall)
    numers = jnp.zeros(pieces_list[0][2].shape, jnp.float32)
    for entry in pieces_list:
        factor = jnp.exp(entry[0] - overall)
        totals = totals + factor * entry[1]
        numers = numers + factor[..., None] * entry[2]
    latent = (numers / totals[..., None]).astype(jnp.bfloat16)
    head_values = jnp.einsum('bqhd,hdv->bqhv', latent.astype(jnp.float32), value_up.astype(jnp.float32)).astype(jnp.bfloat16)
    attended = jnp.dot(head_values.reshape(TOKENS, H * DV), out_proj, preferred_element_type=jnp.float32).astype(jnp.bfloat16)
    hidden_sum = (residual.astype(jnp.float32) + attended.astype(jnp.float32)).astype(jnp.bfloat16)
    hidden32 = hidden_sum.astype(jnp.float32)
    normed = (hidden32 * lax.rsqrt(lax.optimization_barrier(jnp.mean(hidden32 * hidden32, -1, keepdims=True)) + 1e-06) * norm_gain.astype(jnp.float32)).astype(jnp.bfloat16)
    gate_probs = jax.nn.sigmoid(jnp.dot(normed, router, preferred_element_type=jnp.float32))
    chosen = jnp.take_along_axis(gate_probs, expert_ids, axis=1)
    gate_weights = chosen / lax.optimization_barrier(jnp.sum(chosen, -1, keepdims=True)) * 2.5
    groups = N_SEQ * N_EXP
    group_width = FF // groups

    def run_expert(weights_triple):
        gate_mat, up_mat, down_mat = weights_triple
        gate_act = jnp.dot(normed, gate_mat, preferred_element_type=jnp.float32)
        up_act = jnp.dot(normed, up_mat, preferred_element_type=jnp.float32)
        activated = (jax.nn.silu(gate_act) * up_act).astype(jnp.bfloat16)
        parts = jnp.einsum('bsf,sfd->bsd', activated.reshape(TOKENS, groups, group_width).astype(jnp.float32), down_mat.reshape(groups, group_width, D).astype(jnp.float32))
        parts = parts.astype(jnp.bfloat16).astype(jnp.float32)
        return lax.optimization_barrier(jnp.sum(parts, 1)).astype(jnp.bfloat16)
    expert_out = lax.map(run_expert, (w_gate, w_up, w_down))
    token_index = jnp.arange(TOKENS, dtype=jnp.int32)[:, None]
    selected = expert_out[expert_ids, token_index].astype(jnp.float32)
    routed = lax.optimization_barrier(jnp.sum(gate_weights[..., None] * selected, 1))
    return (hidden32 + routed).astype(jnp.bfloat16)
```

```python
import functools

import jax
import jax.numpy as jnp
from jax import lax
from jax.experimental import pallas as pl
from jax.experimental.pallas import tpu as pltpu
from jax.sharding import PartitionSpec as P

DL = 512
DR = 64
DV = 128
BLOCK = 64


def merge_parts(former, latter):
    row_max = jnp.maximum(former[0], latter[0])
    left_scale = jnp.exp(former[0] - row_max)
    right_scale = jnp.exp(latter[0] - row_max)
    return (
        row_max,
        left_scale * former[1] + right_scale * latter[1],
        left_scale[..., None] * former[2] + right_scale[..., None] * latter[2],
    )


def pick_rows(block_rows, picks):
    return block_rows[picks]


def shard_softmax(queries, picked, usable):
    scores = jnp.einsum("bqhk,bjk->bqhj", queries, picked, preferred_element_type=jnp.float32) * (
        DV + DR
    ) ** (-0.5)
    row_max = jnp.max(jnp.where(usable, scores, -1e30), axis=-1)
    weights = jnp.where(usable, jnp.exp(scores - row_max[..., None]), 0.0).astype(jnp.bfloat16)
    row_sum = jnp.sum(weights.astype(jnp.float32), -1)
    weighted = jnp.einsum(
        "bqhj,bjd->bqhd", weights, picked[..., :DL], preferred_element_type=jnp.float32
    )
    return (row_max, row_sum, weighted)


def expert_rows(arrived, w_gate, w_up, w_down):
    model_width = w_gate.shape[1]
    flat_rows = arrived.reshape(-1, model_width)
    gate_act = jnp.dot(flat_rows, w_gate[0], preferred_element_type=jnp.float32)
    up_act = jnp.dot(flat_rows, w_up[0], preferred_element_type=jnp.float32)
    activated = (jax.nn.silu(gate_act) * up_act).astype(jnp.bfloat16)
    partial_value = jnp.dot(activated, w_down[0], preferred_element_type=jnp.float32).astype(
        jnp.bfloat16
    )
    return partial_value.reshape(arrived.shape)


def per_device(
    residual,
    queries,
    latent_cache,
    blocks,
    lengths,
    value_up,
    out_proj,
    norm_gain,
    router,
    expert_ids,
    w_gate,
    w_up,
    w_down,
):
    local_reqs, drafts, head_count, qk_width = queries.shape
    shard_len = latent_cache.shape[1]
    picks_count = blocks.shape[2]
    seq_index = lax.axis_index("seq")
    block_view = latent_cache.reshape(local_reqs, shard_len // BLOCK, BLOCK, qk_width)
    picked = jax.vmap(pick_rows)(block_view, blocks[:, 0]).reshape(
        local_reqs, picks_count * BLOCK, qk_width
    )
    positions = (
        seq_index * shard_len + blocks[:, 0, :, None] * BLOCK + jnp.arange(BLOCK, dtype=jnp.int32)
    )
    positions = positions.reshape(local_reqs, picks_count * BLOCK)
    limits = lengths[:, None] - (drafts - 1) + jnp.arange(drafts, dtype=jnp.int32)[None, :]
    usable = positions[:, None, None, :] < limits[:, :, None, None]
    usable_mark = usable[:, :, 0, :].astype(jnp.bfloat16)
    all_keys, all_marks = (
        lax.all_gather(picked[None], "seq", axis=0, tiled=True),
        lax.all_gather(usable_mark[None], "seq", axis=0, tiled=True),
    )
    combined = None
    for shard in range(lax.axis_size("seq")):
        shard_usable = (all_marks[shard] > 0)[:, :, None, :]
        partial_value = shard_softmax(queries, all_keys[shard], shard_usable)
        combined = partial_value if combined is None else merge_parts(combined, partial_value)
    latent = (combined[2] / combined[1][..., None]).astype(jnp.bfloat16)
    head_values = jnp.einsum(
        "bqhd,hdv->bqhv", latent, value_up, preferred_element_type=jnp.float32
    ).astype(jnp.bfloat16)
    flat_values = head_values.reshape(local_reqs * drafts, head_count * DV)
    col_terms = jnp.dot(
        lax.all_gather(flat_values, "req", axis=0, tiled=True),
        out_proj,
        preferred_element_type=jnp.float32,
    )
    token_terms = lax.all_to_all(
        col_terms[None].astype(jnp.bfloat16),
        ("req", "seq", "exp"),
        split_axis=1,
        concat_axis=0,
        tiled=True,
    ).astype(jnp.float32)
    exp_count = lax.axis_size("exp")
    col_blocks = token_terms.shape[0] // exp_count
    rows_here = token_terms.shape[1]
    col_sums = jnp.sum(
        token_terms.reshape(col_blocks, exp_count, rows_here, token_terms.shape[2]), 1
    )
    attended = jnp.transpose(col_sums, (1, 0, 2)).reshape(rows_here, -1).astype(jnp.bfloat16)
    hidden_sum = (residual.astype(jnp.float32) + attended.astype(jnp.float32)).astype(jnp.bfloat16)
    hidden32 = hidden_sum.astype(jnp.float32)
    normed = (
        hidden32
        * lax.rsqrt(jnp.mean(hidden32 * hidden32, -1, keepdims=True) + 1e-06)
        * norm_gain.astype(jnp.float32)
    ).astype(jnp.bfloat16)
    gate_probs = jax.nn.sigmoid(jnp.dot(normed, router, preferred_element_type=jnp.float32))
    expert_count = router.shape[1]
    top_count = expert_ids.shape[1]
    one_hot = (expert_ids[:, :, None] == jnp.arange(expert_count, dtype=jnp.int32)).astype(
        jnp.int32
    )
    pair_hot = one_hot.reshape(rows_here * top_count, expert_count)
    slot_index = jnp.sum((jnp.cumsum(pair_hot, 0) - pair_hot) * pair_hot, -1)
    slot_hot = (slot_index[:, None] == jnp.arange(rows_here, dtype=jnp.int32)).astype(jnp.int32)
    placement = (pair_hot[:, :, None] * slot_hot[:, None, :]).reshape(
        rows_here, top_count, expert_count * rows_here
    )
    chosen = jnp.sum(one_hot.astype(jnp.float32) * gate_probs[:, None, :], -1)
    gate_weights = chosen / jnp.sum(chosen, -1, keepdims=True) * 2.5
    dispatch = jnp.sum(placement, 1).astype(jnp.bfloat16)
    outgoing = jnp.dot(dispatch.T, normed, preferred_element_type=jnp.float32).astype(jnp.bfloat16)
    outgoing = outgoing.reshape(expert_count, rows_here, outgoing.shape[1])
    combine = jnp.sum(gate_weights[:, :, None] * placement.astype(jnp.float32), 1)
    copies = lax.axis_size("seq") * exp_count
    fanned = jnp.broadcast_to(outgoing[:, None], (expert_count, copies) + outgoing.shape[1:])
    fanned = fanned.reshape((expert_count * copies,) + outgoing.shape[1:])
    returned = lax.all_to_all(
        expert_rows(
            lax.all_to_all(fanned, ("req", "seq", "exp"), split_axis=0, concat_axis=0, tiled=True),
            w_gate,
            w_up,
            w_down,
        ),
        ("req", "seq", "exp"),
        split_axis=0,
        concat_axis=0,
        tiled=True,
    )
    returned = returned.reshape((expert_count, copies) + outgoing.shape[1:]).astype(jnp.float32)
    expert_out = jnp.sum(returned, 1).astype(jnp.bfloat16)
    slot_rows = expert_out.reshape(expert_count * rows_here, expert_out.shape[2]).astype(
        jnp.float32
    )
    routed = jnp.dot(combine, slot_rows, precision=lax.Precision.HIGHEST)
    return (hidden32 + routed).astype(jnp.bfloat16)


MESH = pl.DeviceIdType.MESH


def fused_kernel(
    dims,
    residual_ref,
    queries_hbm,
    cache_ref,
    blocks_ref,
    lengths_ref,
    value_up_hbm,
    out_proj_hbm,
    gain_ref,
    router_hbm,
    ids_ref,
    w_gate_hbm,
    w_up_hbm,
    w_down_hbm,
    out_ref,
    q_v,
    vu_v,
    op_v,
    rt_v,
    wg_v,
    wu_v,
    wd_v,
    keys_rx,
    marks,
    res_tx,
    res_rx,
    lat,
    hv,
    acc,
    part_tx,
    part_rx,
    res_sum,
    xs,
    ys,
    y_tx,
    y_rx,
    z_sum,
    z_tx,
    z_rx,
    f_tx,
    f_rx,
    load_sem,
    key_sem,
    mark_sem,
    res_ssem,
    res_rsem,
    hz_ssem,
    hz_rsem,
    hs_ssem,
    hs_rsem,
    ps_ssem,
    ps_rsem,
    az_ssem,
    az_rsem,
    ae_ssem,
    ae_rsem,
    as_ssem,
    as_rsem,
    ys_ssem,
    ys_rsem,
    ye_ssem,
    ye_rsem,
    yz_ssem,
    yz_rsem,
):
    R, S, E = dims
    f32, b16 = jnp.float32, jnp.bfloat16
    r, s, e = lax.axis_index("req"), lax.axis_index("seq"), lax.axis_index("exp")
    other = 1 - s
    sibling = (r, other, e)
    drafts, half_heads, _ = q_v.shape
    keys_len = cache_ref.shape[0]
    width = op_v.shape[1]
    chunks = R * S
    nt = residual_ref.shape[0]
    devices = R * S * E
    mine = r * S + s
    at_home = (e == r).astype(jnp.int32)

    head_from = pl.multiple_of(s * half_heads, half_heads)
    loads = [
        pltpu.make_async_copy(queries_hbm.at[:, pl.ds(head_from, half_heads), :], q_v, load_sem.at[0]),
        pltpu.make_async_copy(value_up_hbm.at[pl.ds(head_from, half_heads)], vu_v, load_sem.at[1]),
        pltpu.make_async_copy(out_proj_hbm, op_v, load_sem.at[2]),
        pltpu.make_async_copy(router_hbm, rt_v, load_sem.at[3]),
        pltpu.make_async_copy(w_gate_hbm, wg_v, load_sem.at[4]),
        pltpu.make_async_copy(w_up_hbm, wu_v, load_sem.at[5]),
        pltpu.make_async_copy(w_down_hbm, wd_v, load_sem.at[6]),
    ]
    for load in loads:
        load.start()

    def z_peer(d):
        return (lax.rem(r + d, R), s, e)

    def e_peer(d):
        return (r, s, lax.rem(e + d, E))

    barrier = pltpu.get_barrier_semaphore()
    for peer in [sibling] + [z_peer(d) for d in range(1, R)] + [e_peer(d) for d in range(1, E)]:
        pl.semaphore_signal(barrier, inc=1, device_id=peer, device_id_type=MESH)
    for ss in range(S):
        for ee in range(E):

            @pl.when(jnp.logical_not((e == r) & (s == ss) & (e == ee)))
            def _():
                pl.semaphore_signal(barrier, inc=1, device_id=(e, ss, ee), device_id_type=MESH)

    block_of = lax.broadcasted_iota(jnp.int32, marks.shape[1:], 1) // BLOCK
    hit = block_of == blocks_ref[0]
    for i in range(1, blocks_ref.shape[0]):
        hit = hit | (block_of == blocks_ref[i])
    marks[0] = hit.astype(f32)
    lane = lax.broadcasted_iota(jnp.int32, (1, 128), 1)
    for t in range(nt):
        hot = lane == ids_ref[t, 0]
        for k in range(1, ids_ref.shape[1]):
            hot = hot | (lane == ids_ref[t, k])
        for c in range(chunks):
            res_tx[c, t : t + 1, width:] = hot.astype(f32)
    for c in range(chunks):
        res_tx[c, :, :width] = residual_ref[:, c * width : (c + 1) * width].astype(f32)

    pl.semaphore_wait(barrier, 1 + (R - 1) + (E - 1) + S * E - at_home)

    def remote(src, dst, ssem, rsem, peer):
        return pltpu.make_async_remote_copy(
            src_ref=src, dst_ref=dst, send_sem=ssem, recv_sem=rsem, device_id=peer, device_id_type=MESH
        )

    sent = []
    key_copy = remote(cache_ref, keys_rx, key_sem.at[0], key_sem.at[1], sibling)
    mark_copy = remote(marks.at[0], marks.at[1], mark_sem.at[0], mark_sem.at[1], sibling)
    key_copy.start()
    mark_copy.start()
    sent += [key_copy, mark_copy]
    slot = s * E + e
    for c in range(chunks):
        to = (c // S, c % S, r)
        here = (r == c // S) & (s == c % S) & (e == r)

        @pl.when(jnp.logical_not(here))
        def _():
            remote(res_tx.at[c], res_rx.at[slot], res_ssem.at[c], res_rsem.at[slot], to).start()

        @pl.when(here)
        def _():
            pltpu.make_async_copy(res_tx.at[c], res_rx.at[slot], res_rsem.at[slot]).start()

    loads[0].wait()
    q2 = q_v[...].reshape(drafts * half_heads, q_v.shape[2])
    rows = drafts * half_heads
    limit = lengths_ref[0] - (drafts - 1) + lax.broadcasted_iota(jnp.int32, (rows, 1), 0) // half_heads

    def scores_of(keys, mark, shard):
        sc = lax.dot_general(q2, keys, (((1,), (1,)), ((), ())), preferred_element_type=f32)
        pos = shard * keys_len + lax.broadcasted_iota(jnp.int32, (rows, keys_len), 1)
        usable = (pos < limit) & (mark > 0)
        return jnp.where(usable, sc * (DV + DR) ** (-0.5), -1e30), usable

    near, near_ok = scores_of(cache_ref[...], marks[0, :1, :keys_len], s)
    key_copy.wait_recv()
    mark_copy.wait_recv()
    far, far_ok = scores_of(keys_rx[...], marks[1, :1, :keys_len], other)
    top = jnp.maximum(jnp.max(near, -1, keepdims=True), jnp.max(far, -1, keepdims=True))
    near_p = jnp.where(near_ok, jnp.exp(near - top), 0.0).astype(b16)
    far_p = jnp.where(far_ok, jnp.exp(far - top), 0.0).astype(b16)
    total = jnp.sum(near_p.astype(f32), -1, keepdims=True) + jnp.sum(far_p.astype(f32), -1, keepdims=True)
    weighted = jnp.dot(near_p, cache_ref[:, :DL], preferred_element_type=f32)
    weighted += jnp.dot(far_p, keys_rx[:, :DL], preferred_element_type=f32)
    latent = weighted / total
    for k in range(lat.shape[0]):
        lat[k] = latent[:, k * 128 : (k + 1) * 128]

    loads[1].wait()
    for h in range(half_heads):
        one = [lat[k, pl.ds(h, drafts, stride=half_heads), :] for k in range(lat.shape[0])]
        one = jnp.concatenate(one, axis=1).astype(b16)
        hv[s, r, :, h * DV : (h + 1) * DV] = jnp.dot(one, vu_v[h], preferred_element_type=f32).astype(b16)

    hz = [
        remote(hv.at[s, r], hv.at[s, r], hz_ssem.at[d - 1], hz_rsem.at[d - 1], z_peer(d)) for d in range(1, R)
    ]
    for copy in hz:
        copy.start()
    hs = []
    for d in range(R):
        if d:
            hz[d - 1].wait_recv()
        origin = lax.rem(r + R - d, R)
        copy = remote(hv.at[s, origin], hv.at[s, origin], hs_ssem.at[d], hs_rsem.at[d], sibling)
        copy.start()
        hs.append(copy)
    sent += hz + hs

    loads[2].wait()
    half = half_heads * DV

    def out_part(side):
        head_rows = hv[side].reshape(R * drafts, half)
        return jnp.dot(head_rows, op_v[pl.ds(pl.multiple_of(side * half, half), half), :], preferred_element_type=f32)

    acc[...] = out_part(s).reshape(acc.shape)
    for j in range(S * E):
        pltpu.make_async_copy(res_rx.at[j], res_rx.at[j], res_rsem.at[j]).wait()
        res_sum[j * nt : (j + 1) * nt, :] = res_rx[j]
    for copy in hs:
        copy.wait_recv()
    acc[...] += out_part(other).reshape(acc.shape)
    part_tx[...] = acc[...].astype(b16)
    ps = [
        remote(part_tx.at[lax.rem(e + d, E)], part_rx.at[d - 1], ps_ssem.at[d - 1], ps_rsem.at[d - 1], e_peer(d))
        for d in range(1, E)
    ]
    for copy in ps:
        copy.start()
    attended = acc[e]
    for d in range(1, E):
        ps[d - 1].wait_recv()
        attended += part_rx[d - 1].astype(f32)
    sent += ps
    hidden = res_sum[:, :width] + attended.astype(b16).astype(f32)
    xs[mine, e, :, :width] = hidden.astype(b16)
    xs[mine, e, :, width:] = res_sum[:, width:].astype(b16)

    az = [
        remote(xs.at[mine, e], xs.at[mine, e], az_ssem.at[d - 1], az_rsem.at[d - 1], z_peer(d)) for d in range(1, R)
    ]
    for copy in az:
        copy.start()
    ae = []
    for dz in range(R):
        if dz:
            az[dz - 1].wait_recv()
        chunk = lax.rem(r + R - dz, R) * S + s
        row = [
            remote(xs.at[chunk, e], xs.at[chunk, e], ae_ssem.at[dz, d - 1], ae_rsem.at[dz, d - 1], e_peer(d))
            for d in range(1, E)
        ]
        for copy in row:
            copy.start()
        ae.append(row)
    for load in loads[3:6]:
        load.wait()

    tokens = E * xs.shape[2]

    def expert_part(state, chunk):
        squares, gate, up, logits = state
        hid = xs[chunk].reshape(tokens, xs.shape[3])[:, :width].astype(f32)
        cols = pl.ds(pl.multiple_of(chunk * width, width), width)
        scaled = (hid * gain_ref[:, cols].astype(f32)).astype(b16)
        return (
            squares + jnp.sum(hid * hid, -1, keepdims=True),
            gate + jnp.dot(scaled, wg_v[cols, :], preferred_element_type=f32),
            up + jnp.dot(scaled, wu_v[cols, :], preferred_element_type=f32),
            logits + lax.dot_general(scaled, rt_v[:, cols], (((1,), (1,)), ((), ())), preferred_element_type=f32),
        )

    state = (
        jnp.zeros((tokens, 1), f32),
        jnp.zeros((tokens, wg_v.shape[1]), f32),
        jnp.zeros((tokens, wg_v.shape[1]), f32),
        jnp.zeros((tokens, rt_v.shape[0]), f32),
    )
    across = []
    for dz in range(R):
        for copy in ae[dz]:
            copy.wait_recv()
        chunk = lax.rem(r + R - dz, R) * S + s
        copy = remote(xs.at[chunk], xs.at[chunk], as_ssem.at[dz], as_rsem.at[dz], sibling)
        copy.start()
        across.append(copy)
        state = expert_part(state, chunk)
    for dz in range(R):
        across[dz].wait_recv()
        state = expert_part(state, lax.rem(r + R - dz, R) * S + other)
    sent += az + [copy for row in ae for copy in row] + across
    squares, gate, up, logits = state
    scale = lax.rsqrt(squares / (chunks * width) + 1e-06)
    experts = rt_v.shape[0]
    hots = xs[mine].reshape(tokens, xs.shape[3])[:, width : width + experts].astype(f32)
    chosen = hots * jax.nn.sigmoid(logits * scale)
    this_expert = lax.broadcasted_iota(jnp.int32, (1, experts), 1) == r
    weight = jnp.sum(jnp.where(this_expert, chosen, 0.0), -1, keepdims=True)
    weight = weight / jnp.sum(chosen, -1, keepdims=True) * 2.5
    activated = (jax.nn.silu(gate * scale) * (up * scale) * weight).astype(b16)

    to_row = lax.broadcasted_iota(jnp.int32, (tokens, tokens), 0)
    from_row = lax.broadcasted_iota(jnp.int32, (tokens, tokens), 1)
    owner = to_row % devices
    wanted = ((owner % R) * (S * E) + owner // R) * nt + to_row // devices
    ordered = jnp.dot((wanted == from_row).astype(b16), activated, preferred_element_type=f32).astype(b16)
    loads[6].wait()
    per_owner = nt * chunks
    planes = width // 128
    for c in range(chunks):
        down = jnp.dot(ordered, wd_v[:, c * width : (c + 1) * width], preferred_element_type=f32)
        for t in range(nt):
            part = down[t * devices : (t + 1) * devices]
            for k in range(planes):
                ys[k, pl.ds(c * nt + t, devices, stride=per_owner), :] = part[:, k * 128 : (k + 1) * 128]

    span = R * per_owner
    order = list(range(1, E)) + [0]
    yc = {}

    def summed(side, group):
        at = pl.ds(pl.multiple_of((side * E + group) * span, span), span)
        return jnp.concatenate([ys[k, at, :] for k in range(planes)], axis=1)

    for d in order:
        group = lax.rem(e + d, E)
        y_tx[d] = summed(other, group).astype(b16)
        yc[d] = remote(y_tx.at[d], y_rx.at[d], ys_ssem.at[d], ys_rsem.at[d], sibling)
        yc[d].start()
    ye = []
    for d in order:
        group = lax.rem(e + d, E)
        yc[d].wait_recv()
        both = summed(s, group) + y_rx[d].astype(f32)
        if d:
            z_tx[d - 1] = both.astype(b16)
            copy = remote(z_tx.at[d - 1], z_rx.at[d - 1], ye_ssem.at[d - 1], ye_rsem.at[d - 1], e_peer(d))
            copy.start()
            ye.append(copy)
        else:
            z_all = both
    for d in range(1, E):
        ye[d - 1].wait_recv()
        z_all += z_rx[d - 1].astype(f32)
    z_sum[...] = z_all.reshape(z_sum.shape)
    f_tx[...] = z_sum[...].astype(b16)
    yz = [
        remote(f_tx.at[lax.rem(r + d, R)], f_rx.at[d - 1], yz_ssem.at[d - 1], yz_rsem.at[d - 1], z_peer(d))
        for d in range(1, R)
    ]
    for copy in yz:
        copy.start()
    sent += list(yc.values()) + ye + yz
    pick = lax.broadcasted_iota(jnp.int32, (8, tokens), 0) + (mine * E + e) * nt
    pick = (pick == lax.broadcasted_iota(jnp.int32, (8, tokens), 1)).astype(b16)
    own = [
        jnp.dot(pick, xs[c].reshape(tokens, xs.shape[3])[:, :width], preferred_element_type=f32)
        for c in range(chunks)
    ]
    routed = z_sum[r]
    for d in range(1, R):
        yz[d - 1].wait_recv()
        routed += f_rx[d - 1].astype(f32)
    for c in range(chunks):
        out_ref[:, c * width : (c + 1) * width] = (own[c][:nt] + routed[c * nt : (c + 1) * nt]).astype(b16)

    for copy in sent:
        copy.wait_send()
    for c in range(chunks):
        here = (r == c // S) & (s == c % S) & (e == r)

        @pl.when(jnp.logical_not(here))
        def _():
            remote(res_tx.at[c], res_rx.at[slot], res_ssem.at[c], res_rsem.at[slot], (c // S, c % S, r)).wait_send()


def fused(
    dims, residual, queries, cache, blocks, lengths, value_up, out_proj, gain, router, ids, w_gate, w_up, w_down
):
    R, S, E = dims
    f32, b16 = jnp.float32, jnp.bfloat16
    drafts, heads, qk = queries.shape
    half_heads = heads // S
    width = out_proj.shape[1]
    nt, model = residual.shape
    keys_len = cache.shape[0]
    chunks = R * S
    lanes = -(-keys_len // 128) * 128
    ff = w_gate.shape[1]
    per_owner = nt * chunks
    dma = pltpu.SemaphoreType.DMA
    vmem, smem, hbm = (pl.BlockSpec(memory_space=m) for m in (pltpu.VMEM, pltpu.SMEM, pl.ANY))
    scratch = [
        pltpu.VMEM((drafts, half_heads, qk), b16),
        pltpu.VMEM((half_heads,) + value_up.shape[1:], b16),
        pltpu.VMEM(out_proj.shape, b16),
        pltpu.VMEM(router.shape, b16),
        pltpu.VMEM(w_gate.shape, b16),
        pltpu.VMEM(w_up.shape, b16),
        pltpu.VMEM(w_down.shape, b16),
        pltpu.VMEM(cache.shape, b16),
        pltpu.VMEM((2, 8, lanes), f32),
        pltpu.VMEM((chunks, nt, width + 128), f32),
        pltpu.VMEM((S * E, nt, width + 128), f32),
        pltpu.VMEM((DL // 128, drafts * half_heads, 128), f32),
        pltpu.VMEM((S, R, drafts, half_heads * DV), b16),
        pltpu.VMEM((E, drafts, width), f32),
        pltpu.VMEM((E, drafts, width), b16),
        pltpu.VMEM((E - 1, drafts, width), b16),
        pltpu.VMEM((drafts, width + 128), f32),
        pltpu.VMEM((chunks, E, drafts, width + 128), b16),
        pltpu.VMEM((width // 128, R * S * E * per_owner, 128), f32),
        pltpu.VMEM((E, R * per_owner, width), b16),
        pltpu.VMEM((E, R * per_owner, width), b16),
        pltpu.VMEM((R, per_owner, width), f32),
        pltpu.VMEM((E - 1, R * per_owner, width), b16),
        pltpu.VMEM((E - 1, R * per_owner, width), b16),
        pltpu.VMEM((R, per_owner, width), b16),
        pltpu.VMEM((R - 1, per_owner, width), b16),
        dma((7,)),
        dma((2,)),
        dma((2,)),
        dma((chunks,)),
        dma((S * E,)),
        dma((R - 1,)),
        dma((R - 1,)),
        dma((R,)),
        dma((R,)),
        dma((E - 1,)),
        dma((E - 1,)),
        dma((R - 1,)),
        dma((R - 1,)),
        dma((R, E - 1)),
        dma((R, E - 1)),
        dma((R,)),
        dma((R,)),
        dma((E,)),
        dma((E,)),
        dma((E - 1,)),
        dma((E - 1,)),
        dma((R - 1,)),
        dma((R - 1,)),
    ]
    return pl.pallas_call(
        functools.partial(fused_kernel, dims),
        out_shape=jax.ShapeDtypeStruct((nt, model), b16),
        in_specs=[vmem, hbm, vmem, smem, smem, hbm, hbm, vmem, hbm, smem, hbm, hbm, hbm],
        out_specs=vmem,
        scratch_shapes=scratch,
        compiler_params=pltpu.CompilerParams(
            collective_id=0, has_side_effects=True, vmem_limit_bytes=56 * 1024 * 1024
        ),
        cost_estimate=pl.CostEstimate(
            flops=2 * R * drafts * (out_proj.size + 3 * w_gate.size),
            bytes_accessed=2 * (value_up.size + out_proj.size + 3 * w_gate.size),
            transcendentals=0,
        ),
    )(residual, queries, cache, blocks, lengths, value_up, out_proj, gain, router, ids, w_gate, w_up, w_down)


def per_device_fused(dims, *args):
    (residual, queries, cache, blocks, lengths, value_up, out_proj, gain, router, ids, w_gate, w_up, w_down) = args
    return fused(
        dims,
        residual,
        queries[0],
        cache[0],
        blocks[0, 0],
        lengths,
        value_up,
        out_proj,
        gain[None],
        router.T,
        ids,
        w_gate[0],
        w_up[0],
        w_down[0],
    )


def fits_fused(dims, shapes):
    R, S, E = dims
    residual, queries, cache, router = shapes[0], shapes[1], shapes[2], shapes[8]
    drafts, heads, model = queries[1], queries[2], residual[1]
    return (
        S == 2
        and R == E
        and queries[0] == R
        and router[1] == R
        and drafts % 16 == 0
        and residual[0] == R * drafts
        and heads % (E * S * 16) == 0
        and model % (R * S * 128) == 0
        and (residual[0] // E) % 16 == 0
        and (drafts // (S * E) * R * S) % 16 == 0
        and cache[1] // S % BLOCK == 0
    )


def solution(mesh):
    in_specs = (
        P(("req", "seq", "exp"), None),
        P("req", None, "exp", None),
        P("req", "seq", None),
        P("req", "seq", None),
        P("req"),
        P("exp", None, None),
        P("exp", ("req", "seq")),
        P(),
        P(),
        P(("req", "seq", "exp"), None),
        P("req", None, ("seq", "exp")),
        P("req", None, ("seq", "exp")),
        P("req", ("seq", "exp"), None),
    )
    out_specs = P(("req", "seq", "exp"), None)
    dims = (mesh.shape["req"], mesh.shape["seq"], mesh.shape["exp"])

    def layer(*args):
        fast = fits_fused(dims, [a.shape for a in args])
        body = functools.partial(per_device_fused, dims) if fast else per_device
        return jax.shard_map(body, mesh=mesh, in_specs=in_specs, out_specs=out_specs, check_vma=False)(*args)

    return layer
```

```python
import functools

import jax
import jax.numpy as jnp
from jax import lax
from jax.experimental import pallas as pl
from jax.experimental.pallas import tpu as pltpu
from jax.sharding import PartitionSpec as P

DL = 512
DR = 64
DV = 128
BLOCK = 64


def merge_parts(former, latter):
    row_max = jnp.maximum(former[0], latter[0])
    left_scale = jnp.exp(former[0] - row_max)
    right_scale = jnp.exp(latter[0] - row_max)
    return (
        row_max,
        left_scale * former[1] + right_scale * latter[1],
        left_scale[..., None] * former[2] + right_scale[..., None] * latter[2],
    )


def pick_rows(block_rows, picks):
    return block_rows[picks]


def shard_softmax(queries, picked, usable):
    scores = jnp.einsum("bqhk,bjk->bqhj", queries, picked, preferred_element_type=jnp.float32) * (
        DV + DR
    ) ** (-0.5)
    row_max = jnp.max(jnp.where(usable, scores, -1e30), axis=-1)
    weights = jnp.where(usable, jnp.exp(scores - row_max[..., None]), 0.0).astype(jnp.bfloat16)
    row_sum = jnp.sum(weights.astype(jnp.float32), -1)
    weighted = jnp.einsum(
        "bqhj,bjd->bqhd", weights, picked[..., :DL], preferred_element_type=jnp.float32
    )
    return (row_max, row_sum, weighted)


def expert_rows(arrived, w_gate, w_up, w_down):
    model_width = w_gate.shape[1]
    flat_rows = arrived.reshape(-1, model_width)
    gate_act = jnp.dot(flat_rows, w_gate[0], preferred_element_type=jnp.float32)
    up_act = jnp.dot(flat_rows, w_up[0], preferred_element_type=jnp.float32)
    activated = (jax.nn.silu(gate_act) * up_act).astype(jnp.bfloat16)
    partial_value = jnp.dot(activated, w_down[0], preferred_element_type=jnp.float32).astype(
        jnp.bfloat16
    )
    return partial_value.reshape(arrived.shape)


def per_device(
    residual,
    queries,
    latent_cache,
    blocks,
    lengths,
    value_up,
    out_proj,
    norm_gain,
    router,
    expert_ids,
    w_gate,
    w_up,
    w_down,
):
    local_reqs, drafts, head_count, qk_width = queries.shape
    shard_len = latent_cache.shape[1]
    picks_count = blocks.shape[2]
    seq_index = lax.axis_index("seq")
    block_view = latent_cache.reshape(local_reqs, shard_len // BLOCK, BLOCK, qk_width)
    picked = jax.vmap(pick_rows)(block_view, blocks[:, 0]).reshape(
        local_reqs, picks_count * BLOCK, qk_width
    )
    positions = (
        seq_index * shard_len + blocks[:, 0, :, None] * BLOCK + jnp.arange(BLOCK, dtype=jnp.int32)
    )
    positions = positions.reshape(local_reqs, picks_count * BLOCK)
    limits = lengths[:, None] - (drafts - 1) + jnp.arange(drafts, dtype=jnp.int32)[None, :]
    usable = positions[:, None, None, :] < limits[:, :, None, None]
    usable_mark = usable[:, :, 0, :].astype(jnp.bfloat16)
    all_keys, all_marks = (
        lax.all_gather(picked[None], "seq", axis=0, tiled=True),
        lax.all_gather(usable_mark[None], "seq", axis=0, tiled=True),
    )
    combined = None
    for shard in range(lax.axis_size("seq")):
        shard_usable = (all_marks[shard] > 0)[:, :, None, :]
        partial_value = shard_softmax(queries, all_keys[shard], shard_usable)
        combined = partial_value if combined is None else merge_parts(combined, partial_value)
    latent = (combined[2] / combined[1][..., None]).astype(jnp.bfloat16)
    head_values = jnp.einsum(
        "bqhd,hdv->bqhv", latent, value_up, preferred_element_type=jnp.float32
    ).astype(jnp.bfloat16)
    flat_values = head_values.reshape(local_reqs * drafts, head_count * DV)
    col_terms = jnp.dot(
        lax.all_gather(flat_values, "req", axis=0, tiled=True),
        out_proj,
        preferred_element_type=jnp.float32,
    )
    token_terms = lax.all_to_all(
        col_terms[None].astype(jnp.bfloat16),
        ("req", "seq", "exp"),
        split_axis=1,
        concat_axis=0,
        tiled=True,
    ).astype(jnp.float32)
    exp_count = lax.axis_size("exp")
    col_blocks = token_terms.shape[0] // exp_count
    rows_here = token_terms.shape[1]
    col_sums = jnp.sum(
        token_terms.reshape(col_blocks, exp_count, rows_here, token_terms.shape[2]), 1
    )
    attended = jnp.transpose(col_sums, (1, 0, 2)).reshape(rows_here, -1).astype(jnp.bfloat16)
    hidden_sum = (residual.astype(jnp.float32) + attended.astype(jnp.float32)).astype(jnp.bfloat16)
    hidden32 = hidden_sum.astype(jnp.float32)
    normed = (
        hidden32
        * lax.rsqrt(jnp.mean(hidden32 * hidden32, -1, keepdims=True) + 1e-06)
        * norm_gain.astype(jnp.float32)
    ).astype(jnp.bfloat16)
    gate_probs = jax.nn.sigmoid(jnp.dot(normed, router, preferred_element_type=jnp.float32))
    expert_count = router.shape[1]
    top_count = expert_ids.shape[1]
    one_hot = (expert_ids[:, :, None] == jnp.arange(expert_count, dtype=jnp.int32)).astype(
        jnp.int32
    )
    pair_hot = one_hot.reshape(rows_here * top_count, expert_count)
    slot_index = jnp.sum((jnp.cumsum(pair_hot, 0) - pair_hot) * pair_hot, -1)
    slot_hot = (slot_index[:, None] == jnp.arange(rows_here, dtype=jnp.int32)).astype(jnp.int32)
    placement = (pair_hot[:, :, None] * slot_hot[:, None, :]).reshape(
        rows_here, top_count, expert_count * rows_here
    )
    chosen = jnp.sum(one_hot.astype(jnp.float32) * gate_probs[:, None, :], -1)
    gate_weights = chosen / jnp.sum(chosen, -1, keepdims=True) * 2.5
    dispatch = jnp.sum(placement, 1).astype(jnp.bfloat16)
    outgoing = jnp.dot(dispatch.T, normed, preferred_element_type=jnp.float32).astype(jnp.bfloat16)
    outgoing = outgoing.reshape(expert_count, rows_here, outgoing.shape[1])
    combine = jnp.sum(gate_weights[:, :, None] * placement.astype(jnp.float32), 1)
    copies = lax.axis_size("seq") * exp_count
    fanned = jnp.broadcast_to(outgoing[:, None], (expert_count, copies) + outgoing.shape[1:])
    fanned = fanned.reshape((expert_count * copies,) + outgoing.shape[1:])
    returned = lax.all_to_all(
        expert_rows(
            lax.all_to_all(fanned, ("req", "seq", "exp"), split_axis=0, concat_axis=0, tiled=True),
            w_gate,
            w_up,
            w_down,
        ),
        ("req", "seq", "exp"),
        split_axis=0,
        concat_axis=0,
        tiled=True,
    )
    returned = returned.reshape((expert_count, copies) + outgoing.shape[1:]).astype(jnp.float32)
    expert_out = jnp.sum(returned, 1).astype(jnp.bfloat16)
    slot_rows = expert_out.reshape(expert_count * rows_here, expert_out.shape[2]).astype(
        jnp.float32
    )
    routed = jnp.dot(combine, slot_rows, precision=lax.Precision.HIGHEST)
    return (hidden32 + routed).astype(jnp.bfloat16)


MESH = pl.DeviceIdType.MESH


def column_cuts(width):
    return [(0, width - 256), (width - 256, width)]


def column_groups(width):
    cuts = column_cuts(width)
    return [(lo, min(lo + 256, cuts[0][1])) for lo in range(0, cuts[0][1], 256)] + cuts[1:]


def fused_kernel(
    dims,
    residual_ref,
    queries_hbm,
    cache_ref,
    blocks_ref,
    lengths_ref,
    value_up_hbm,
    out_proj_hbm,
    gain_ref,
    router_hbm,
    ids_ref,
    w_gate_hbm,
    w_up_hbm,
    w_down_hbm,
    out_ref,
    q_v,
    vu_v,
    op_v,
    rt_v,
    wg_v,
    wu_v,
    wd_v,
    keys_rx,
    marks,
    res_tx,
    res_rx,
    gains,
    lat,
    hv,
    acc,
    res_sum,
    hots,
    ys,
    parts_tx,
    parts_rx,
    xs,
    y_tx,
    y_rx,
    both,
    mid_tx,
    mid_rx,
    mid_sum,
    end_tx,
    end_rx,
    load_sem,
    key_sem,
    mark_sem,
    res_ssem,
    res_rsem,
    hz_sem,
    hs_sem,
    hot_sem,
    ps_sem,
    first_sem,
    second_sem,
    across_sem,
    ys_sem,
    mid_sem,
    end_sem,
):
    R, S, E = dims
    f32, b16 = jnp.float32, jnp.bfloat16
    r, s, e = lax.axis_index("req"), lax.axis_index("seq"), lax.axis_index("exp")
    other = 1 - s
    sibling = (r, other, e)
    drafts, half_heads, _ = q_v.shape
    keys_len = cache_ref.shape[0]
    width = op_v.shape[1]
    chunks = R * S
    nt = residual_ref.shape[0]
    devices = R * S * E
    mine = r * S + s
    at_home = (e == r).astype(jnp.int32)

    head_from = pl.multiple_of(s * half_heads, half_heads)
    loads = [
        pltpu.make_async_copy(queries_hbm.at[:, pl.ds(head_from, half_heads), :], q_v, load_sem.at[0]),
        pltpu.make_async_copy(value_up_hbm.at[pl.ds(head_from, half_heads)], vu_v, load_sem.at[1]),
        pltpu.make_async_copy(out_proj_hbm, op_v, load_sem.at[2]),
        pltpu.make_async_copy(router_hbm, rt_v, load_sem.at[3]),
        pltpu.make_async_copy(w_gate_hbm, wg_v, load_sem.at[4]),
        pltpu.make_async_copy(w_up_hbm, wu_v, load_sem.at[5]),
        pltpu.make_async_copy(w_down_hbm, wd_v, load_sem.at[6]),
    ]
    for load in loads:
        load.start()

    def z_peer(d):
        return (lax.rem(r + d, R), s, e)

    def e_peer(d):
        return (r, s, lax.rem(e + d, E))

    barrier = pltpu.get_barrier_semaphore()
    for peer in [sibling] + [z_peer(d) for d in range(1, R)] + [e_peer(d) for d in range(1, E)]:
        pl.semaphore_signal(barrier, inc=1, device_id=peer, device_id_type=MESH)
    for ss in range(S):
        for ee in range(E):

            @pl.when(jnp.logical_not((e == r) & (s == ss) & (e == ee)))
            def _():
                pl.semaphore_signal(barrier, inc=1, device_id=(e, ss, ee), device_id_type=MESH)

    gains[...] = gain_ref[...].astype(f32).reshape(gains.shape)
    block_of = lax.broadcasted_iota(jnp.int32, marks.shape[1:], 1) // BLOCK
    hit = block_of == blocks_ref[0]
    for i in range(1, blocks_ref.shape[0]):
        hit = hit | (block_of == blocks_ref[i])
    marks[0] = hit.astype(f32)
    lane = lax.broadcasted_iota(jnp.int32, (1, 128), 1)
    for t in range(nt):
        hot = lane == ids_ref[t, 0]
        for k in range(1, ids_ref.shape[1]):
            hot = hot | (lane == ids_ref[t, k])
        for c in range(chunks):
            res_tx[c, t : t + 1, width:] = hot.astype(f32)
    for c in range(chunks):
        res_tx[c, :, :width] = residual_ref[:, c * width : (c + 1) * width].astype(f32)

    pl.semaphore_wait(barrier, 1 + (R - 1) + (E - 1) + S * E - at_home)

    def remote(src, dst, ssem, rsem, peer):
        return pltpu.make_async_remote_copy(
            src_ref=src, dst_ref=dst, send_sem=ssem, recv_sem=rsem, device_id=peer, device_id_type=MESH
        )

    sent = []
    key_copy = remote(cache_ref, keys_rx, key_sem.at[0], key_sem.at[1], sibling)
    mark_copy = remote(marks.at[0], marks.at[1], mark_sem.at[0], mark_sem.at[1], sibling)
    key_copy.start()
    mark_copy.start()
    sent += [key_copy, mark_copy]
    slot = s * E + e
    for c in range(chunks):
        to = (c // S, c % S, r)
        here = (r == c // S) & (s == c % S) & (e == r)

        @pl.when(jnp.logical_not(here))
        def _():
            remote(res_tx.at[c], res_rx.at[slot], res_ssem.at[c], res_rsem.at[slot], to).start()

        @pl.when(here)
        def _():
            pltpu.make_async_copy(res_tx.at[c], res_rx.at[slot], res_rsem.at[slot]).start()

    loads[0].wait()
    q2 = q_v[...].reshape(drafts * half_heads, q_v.shape[2])
    rows = drafts * half_heads
    limit = lengths_ref[0] - (drafts - 1) + lax.broadcasted_iota(jnp.int32, (rows, 1), 0) // half_heads

    def scores_of(keys, mark, shard):
        sc = lax.dot_general(q2, keys, (((1,), (1,)), ((), ())), preferred_element_type=f32)
        pos = shard * keys_len + lax.broadcasted_iota(jnp.int32, (rows, keys_len), 1)
        usable = (pos < limit) & (mark > 0)
        return jnp.where(usable, sc * (DV + DR) ** (-0.5), -1e30), usable

    near, near_ok = scores_of(cache_ref[...], marks[0, :1, :keys_len], s)
    key_copy.wait_recv()
    mark_copy.wait_recv()
    far, far_ok = scores_of(keys_rx[...], marks[1, :1, :keys_len], other)
    top = jnp.maximum(jnp.max(near, -1, keepdims=True), jnp.max(far, -1, keepdims=True))
    near_p = jnp.where(near_ok, jnp.exp(near - top), 0.0).astype(b16)
    far_p = jnp.where(far_ok, jnp.exp(far - top), 0.0).astype(b16)
    total = jnp.sum(near_p.astype(f32), -1, keepdims=True) + jnp.sum(far_p.astype(f32), -1, keepdims=True)
    weighted = jnp.dot(near_p, cache_ref[:, :DL], preferred_element_type=f32)
    weighted += jnp.dot(far_p, keys_rx[:, :DL], preferred_element_type=f32)
    latent = weighted / total
    for k in range(lat.shape[0]):
        lat[k] = latent[:, k * 128 : (k + 1) * 128]

    loads[1].wait()
    for h in range(half_heads):
        one = [lat[k, pl.ds(h, drafts, stride=half_heads), :] for k in range(lat.shape[0])]
        one = jnp.concatenate(one, axis=1).astype(b16)
        hv[s, r, :, h * DV : (h + 1) * DV] = jnp.dot(one, vu_v[h], preferred_element_type=f32).astype(b16)

    hz = [
        remote(hv.at[s, r], hv.at[s, r], hz_sem.at[0, d - 1], hz_sem.at[1, d - 1], z_peer(d)) for d in range(1, R)
    ]
    for copy in hz:
        copy.start()
    hs = []
    for d in range(R):
        if d:
            hz[d - 1].wait_recv()
        origin = lax.rem(r + R - d, R)
        copy = remote(hv.at[s, origin], hv.at[s, origin], hs_sem.at[0, d], hs_sem.at[1, d], sibling)
        copy.start()
        hs.append(copy)
    sent += hz + hs

    loads[2].wait()
    half = half_heads * DV

    def out_part(side, lo, hi):
        head_rows = hv[side].reshape(R * drafts, half)
        depth = pl.ds(pl.multiple_of(side * half, half), half)
        part = jnp.dot(head_rows, op_v[depth, lo:hi], preferred_element_type=f32)
        return part.reshape(E, drafts, hi - lo)

    cuts = column_cuts(width)
    for lo, hi in cuts:
        acc[:, :, lo:hi] = out_part(s, lo, hi)
    for j in range(S * E):
        pltpu.make_async_copy(res_rx.at[j], res_rx.at[j], res_rsem.at[j]).wait()
        res_sum[j * nt : (j + 1) * nt, :] = res_rx[j]
    hots[e] = res_sum[:, width:].astype(b16)
    hot_copies = [
        remote(hots.at[e], hots.at[e], hot_sem.at[0, d - 1], hot_sem.at[1, d - 1], e_peer(d)) for d in range(1, E)
    ]
    for copy in hot_copies:
        copy.start()
    sent += hot_copies
    for copy in hs:
        copy.wait_recv()
    ps = [None, None]
    for i in (1, 0):
        lo, hi = cuts[i]
        acc[:, :, lo:hi] += out_part(other, lo, hi)
        parts_tx[i][...] = acc[:, :, lo:hi].astype(b16)
        ps[i] = [
            remote(
                parts_tx[i].at[lax.rem(e + d, E)],
                parts_rx[i].at[d - 1],
                ps_sem.at[0, i, d - 1],
                ps_sem.at[1, i, d - 1],
                e_peer(d),
            )
            for d in range(1, E)
        ]
        for copy in ps[i]:
            copy.start()
        sent += ps[i]

    def chunk_at(d):
        return lax.rem(r + R - d, R) * S + s

    def group_at(d):
        return lax.rem(e + E - d, E)

    first = [None, None]
    for i in (1, 0):
        lo, hi = cuts[i]
        attended = acc[e, :, lo:hi]
        for d in range(1, E):
            ps[i][d - 1].wait_recv()
            attended += parts_rx[i][d - 1].astype(f32)
        xs[i][mine, e] = (res_sum[:, lo:hi] + attended.astype(b16).astype(f32)).astype(b16)
        block = xs[i].at[mine, e]
        first[i] = [
            remote(block, block, first_sem.at[0, i, d - 1], first_sem.at[1, i, d - 1], (e_peer if i else z_peer)(d))
            for d in range(1, E if i else R)
        ]
        for copy in first[i]:
            copy.start()
        sent += first[i]
    second = [[], []]
    for hop in range(max(R, E)):
        for i in (1, 0):
            if hop >= (E if i else R):
                continue
            if hop:
                first[i][hop - 1].wait_recv()
            block = xs[i].at[mine, group_at(hop)] if i else xs[i].at[chunk_at(hop), e]
            row = [
                remote(
                    block,
                    block,
                    second_sem.at[0, i, hop, d - 1],
                    second_sem.at[1, i, hop, d - 1],
                    (z_peer if i else e_peer)(d),
                )
                for d in range(1, R if i else E)
            ]
            for copy in row:
                copy.start()
            second[i].append(row)
            sent += row
    for load in loads[3:6]:
        load.wait()

    tokens = E * drafts

    def expert_part(state, chunk, i):
        squares, gate, up, logits = state
        lo, hi = cuts[i]
        hid = xs[i][chunk].reshape(tokens, hi - lo).astype(f32)
        cols = pl.ds(pl.multiple_of(chunk * width + lo, 128), hi - lo)
        scaled = (hid * gains[:, cols]).astype(b16)
        return (
            squares + jnp.sum(hid * hid, -1, keepdims=True),
            gate + jnp.dot(scaled, wg_v[cols, :], preferred_element_type=f32),
            up + jnp.dot(scaled, wu_v[cols, :], preferred_element_type=f32),
            logits + lax.dot_general(scaled, rt_v[:, cols], (((1,), (1,)), ((), ())), preferred_element_type=f32),
        )

    state = (
        jnp.zeros((tokens, 1), f32),
        jnp.zeros((tokens, wg_v.shape[1]), f32),
        jnp.zeros((tokens, wg_v.shape[1]), f32),
        jnp.zeros((tokens, rt_v.shape[0]), f32),
    )
    across = []
    for d in range(R):
        for i in (0, 1):
            if i == 0:
                waits = second[0][d]
            elif d == 0:
                waits = []
            else:
                waits = [row[d - 1] for row in second[1]]
            for copy in waits:
                copy.wait_recv()
            whole = xs[i].at[chunk_at(d)]
            copy = remote(whole, whole, across_sem.at[0, i, d], across_sem.at[1, i, d], sibling)
            copy.start()
            across.append(copy)
            state = expert_part(state, chunk_at(d), i)
    for d in range(R):
        for i in (0, 1):
            across[2 * d + i].wait_recv()
            state = expert_part(state, lax.rem(r + R - d, R) * S + other, i)
    sent += across
    squares, gate, up, logits = state
    scale = lax.rsqrt(squares / (chunks * width) + 1e-06)
    experts = rt_v.shape[0]
    for copy in hot_copies:
        copy.wait_recv()
    chosen = hots[...].reshape(tokens, 128)[:, :experts].astype(f32) * jax.nn.sigmoid(logits * scale)
    this_expert = lax.broadcasted_iota(jnp.int32, (1, experts), 1) == r
    weight = jnp.sum(jnp.where(this_expert, chosen, 0.0), -1, keepdims=True)
    weight = weight / jnp.sum(chosen, -1, keepdims=True) * 2.5
    activated = (jax.nn.silu(gate * scale) * (up * scale) * weight).astype(b16)

    to_row = lax.broadcasted_iota(jnp.int32, (tokens, tokens), 0)
    from_row = lax.broadcasted_iota(jnp.int32, (tokens, tokens), 1)
    owner = to_row % devices
    wanted = ((owner % R) * (S * E) + owner // R) * nt + to_row // devices
    ordered = jnp.dot((wanted == from_row).astype(b16), activated, preferred_element_type=f32).astype(b16)
    loads[6].wait()
    per_owner = nt * chunks
    groups = column_groups(width)
    order = [len(groups) - 1] + list(range(len(groups) - 1))
    half_rows = R * E * per_owner

    def summed(side, lo, hi):
        at = pl.ds(pl.multiple_of(side * half_rows, half_rows), half_rows)
        part = jnp.concatenate([ys[k, at, :] for k in range(lo // 128, hi // 128)], axis=1)
        return part.reshape(E, R, per_owner, hi - lo)

    with_core, mid, end = {}, {}, {}

    def peers_of(g):
        return (z_peer, r, R, e_peer, e, E) if g == len(groups) - 1 else (e_peer, e, E, z_peer, r, R)

    def begin(g):
        lo, hi = groups[g]
        for c in range(chunks):
            down = jnp.dot(ordered, wd_v[:, c * width + lo : c * width + hi], preferred_element_type=f32)
            for t in range(nt):
                part = down[t * devices : (t + 1) * devices]
                for k in range(lo // 128, hi // 128):
                    column = part[:, k * 128 - lo : (k + 1) * 128 - lo]
                    ys[k, pl.ds(c * nt + t, devices, stride=per_owner), :] = column
        y_tx[g][...] = summed(other, lo, hi).astype(b16)
        with_core[g] = remote(y_tx[g], y_rx[g], ys_sem.at[0, g], ys_sem.at[1, g], sibling)
        with_core[g].start()

    def middle(g):
        lo, hi = groups[g]
        peer, me, count = peers_of(g)[:3]
        with_core[g].wait_recv()
        both[g][...] = summed(s, lo, hi) + y_rx[g][...].astype(f32)
        mid[g] = []
        for d in range(1, count):
            to = lax.rem(me + d, count)
            block = both[g][:, to] if g == len(groups) - 1 else both[g][to]
            mid_tx[g][d - 1] = block.astype(b16)
            copy = remote(
                mid_tx[g].at[d - 1], mid_rx[g].at[d - 1], mid_sem.at[0, g, d - 1], mid_sem.at[1, g, d - 1], peer(d)
            )
            copy.start()
            mid[g].append(copy)

    for n, g in enumerate(order):
        begin(g)
        if n:
            middle(order[n - 1])
    middle(order[-1])
    for g in order:
        peer, me, count = peers_of(g)[3:]
        total_g = both[g][:, r] if g == len(groups) - 1 else both[g][e]
        for d, copy in enumerate(mid[g]):
            copy.wait_recv()
            total_g += mid_rx[g][d].astype(f32)
        mid_sum[g][...] = total_g
        end_tx[g][...] = total_g.astype(b16)
        end[g] = []
        for d in range(1, count):
            to = lax.rem(me + d, count)
            copy = remote(
                end_tx[g].at[to], end_rx[g].at[d - 1], end_sem.at[0, g, d - 1], end_sem.at[1, g, d - 1], peer(d)
            )
            copy.start()
            end[g].append(copy)
        sent += [with_core[g]] + mid[g] + end[g]
    pick = lax.broadcasted_iota(jnp.int32, (8, tokens), 0) + (mine * E + e) * nt
    pick = (pick == lax.broadcasted_iota(jnp.int32, (8, tokens), 1)).astype(b16)
    own = []
    for c in range(chunks):
        sides = [
            jnp.dot(pick, xs[i][c].reshape(tokens, hi - lo), preferred_element_type=f32)
            for i, (lo, hi) in enumerate(cuts)
        ]
        own.append(jnp.concatenate(sides, axis=1))
    for g in order:
        lo, hi = groups[g]
        routed = mid_sum[g][peers_of(g)[4]]
        for d, copy in enumerate(end[g]):
            copy.wait_recv()
            routed += end_rx[g][d].astype(f32)
        for c in range(chunks):
            value = own[c][:nt, lo:hi] + routed[c * nt : (c + 1) * nt]
            out_ref[:, c * width + lo : c * width + hi] = value.astype(b16)

    for copy in sent:
        copy.wait_send()
    for c in range(chunks):
        here = (r == c // S) & (s == c % S) & (e == r)

        @pl.when(jnp.logical_not(here))
        def _():
            remote(res_tx.at[c], res_rx.at[slot], res_ssem.at[c], res_rsem.at[slot], (c // S, c % S, r)).wait_send()


def fused(
    dims, residual, queries, cache, blocks, lengths, value_up, out_proj, gain, router, ids, w_gate, w_up, w_down
):
    R, S, E = dims
    f32, b16 = jnp.float32, jnp.bfloat16
    drafts, heads, qk = queries.shape
    half_heads = heads // S
    width = out_proj.shape[1]
    nt, model = residual.shape
    keys_len = cache.shape[0]
    chunks = R * S
    lanes = -(-keys_len // 128) * 128
    ff = w_gate.shape[1]
    per_owner = nt * chunks
    cuts, groups = column_cuts(width), column_groups(width)
    dma = pltpu.SemaphoreType.DMA
    vmem, smem, hbm = (pl.BlockSpec(memory_space=m) for m in (pltpu.VMEM, pltpu.SMEM, pl.ANY))
    scratch = [
        pltpu.VMEM((drafts, half_heads, qk), b16),
        pltpu.VMEM((half_heads,) + value_up.shape[1:], b16),
        pltpu.VMEM(out_proj.shape, b16),
        pltpu.VMEM(router.shape, b16),
        pltpu.VMEM(w_gate.shape, b16),
        pltpu.VMEM(w_up.shape, b16),
        pltpu.VMEM(w_down.shape, b16),
        pltpu.VMEM(cache.shape, b16),
        pltpu.VMEM((2, 8, lanes), f32),
        pltpu.VMEM((chunks, nt, width + 128), f32),
        pltpu.VMEM((S * E, nt, width + 128), f32),
        pltpu.VMEM((1, model), f32),
        pltpu.VMEM((DL // 128, drafts * half_heads, 128), f32),
        pltpu.VMEM((S, R, drafts, half_heads * DV), b16),
        pltpu.VMEM((E, drafts, width), f32),
        pltpu.VMEM((drafts, width + 128), f32),
        pltpu.VMEM((E, drafts, 128), b16),
        pltpu.VMEM((width // 128, R * S * E * per_owner, 128), f32),
        [pltpu.VMEM((E, drafts, hi - lo), b16) for lo, hi in cuts],
        [pltpu.VMEM((E - 1, drafts, hi - lo), b16) for lo, hi in cuts],
        [pltpu.VMEM((chunks, E, drafts, hi - lo), b16) for lo, hi in cuts],
        [pltpu.VMEM((E, R, per_owner, hi - lo), b16) for lo, hi in groups],
        [pltpu.VMEM((E, R, per_owner, hi - lo), b16) for lo, hi in groups],
        [pltpu.VMEM((E, R, per_owner, hi - lo), f32) for lo, hi in groups],
        [pltpu.VMEM((E - 1, R, per_owner, hi - lo), b16) for lo, hi in groups],
        [pltpu.VMEM((E - 1, R, per_owner, hi - lo), b16) for lo, hi in groups],
        [pltpu.VMEM((R, per_owner, hi - lo), f32) for lo, hi in groups],
        [pltpu.VMEM((R, per_owner, hi - lo), b16) for lo, hi in groups],
        [pltpu.VMEM((R - 1, per_owner, hi - lo), b16) for lo, hi in groups],
        dma((7,)),
        dma((2,)),
        dma((2,)),
        dma((chunks,)),
        dma((S * E,)),
        dma((2, R - 1)),
        dma((2, R)),
        dma((2, E - 1)),
        dma((2, 2, E - 1)),
        dma((2, 2, R - 1)),
        dma((2, 2, R, E - 1)),
        dma((2, 2, R)),
        dma((2, len(groups))),
        dma((2, len(groups), E - 1)),
        dma((2, len(groups), E - 1)),
    ]
    return pl.pallas_call(
        functools.partial(fused_kernel, dims),
        out_shape=jax.ShapeDtypeStruct((nt, model), b16),
        in_specs=[vmem, hbm, vmem, smem, smem, hbm, hbm, vmem, hbm, smem, hbm, hbm, hbm],
        out_specs=vmem,
        scratch_shapes=scratch,
        compiler_params=pltpu.CompilerParams(
            collective_id=0, has_side_effects=True, vmem_limit_bytes=56 * 1024 * 1024
        ),
        cost_estimate=pl.CostEstimate(
            flops=2 * R * drafts * (out_proj.size + 3 * w_gate.size),
            bytes_accessed=2 * (value_up.size + out_proj.size + 3 * w_gate.size),
            transcendentals=0,
        ),
    )(residual, queries, cache, blocks, lengths, value_up, out_proj, gain, router, ids, w_gate, w_up, w_down)


def per_device_fused(dims, *args):
    (residual, queries, cache, blocks, lengths, value_up, out_proj, gain, router, ids, w_gate, w_up, w_down) = args
    return fused(
        dims,
        residual,
        queries[0],
        cache[0],
        blocks[0, 0],
        lengths,
        value_up,
        out_proj,
        gain,
        router.T,
        ids,
        w_gate[0],
        w_up[0],
        w_down[0],
    )


def fits_fused(dims, shapes):
    R, S, E = dims
    residual, queries, cache, router = shapes[0], shapes[1], shapes[2], shapes[8]
    drafts, heads, model = queries[1], queries[2], residual[1]
    return (
        S == 2
        and R == E
        and queries[0] == R
        and router[1] == R
        and drafts % 16 == 0
        and residual[0] == R * drafts
        and heads % (E * S * 16) == 0
        and model % (R * S * 128) == 0
        and model // (R * S) >= 384
        and (residual[0] // E) % 16 == 0
        and (drafts // (S * E) * R * S) % 16 == 0
        and cache[1] // S % BLOCK == 0
    )


def solution(mesh):
    in_specs = (
        P(("req", "seq", "exp"), None),
        P("req", None, "exp", None),
        P("req", "seq", None),
        P("req", "seq", None),
        P("req"),
        P("exp", None, None),
        P("exp", ("req", "seq")),
        P(),
        P(),
        P(("req", "seq", "exp"), None),
        P("req", None, ("seq", "exp")),
        P("req", None, ("seq", "exp")),
        P("req", ("seq", "exp"), None),
    )
    out_specs = P(("req", "seq", "exp"), None)
    dims = (mesh.shape["req"], mesh.shape["seq"], mesh.shape["exp"])

    def layer(*args):
        fast = fits_fused(dims, [a.shape for a in args])
        body = functools.partial(per_device_fused, dims) if fast else per_device
        return jax.shard_map(body, mesh=mesh, in_specs=in_specs, out_specs=out_specs, check_vma=False)(*args)

    return layer
```

```python
import functools

import jax
import jax.numpy as jnp
from jax import lax
from jax.experimental import pallas as pl
from jax.experimental.pallas import tpu as pltpu
from jax.sharding import PartitionSpec as P

DL = 512
DR = 64
DV = 128
BLOCK = 64


def merge_parts(former, latter):
    row_max = jnp.maximum(former[0], latter[0])
    left_scale = jnp.exp(former[0] - row_max)
    right_scale = jnp.exp(latter[0] - row_max)
    return (
        row_max,
        left_scale * former[1] + right_scale * latter[1],
        left_scale[..., None] * former[2] + right_scale[..., None] * latter[2],
    )


def pick_rows(block_rows, picks):
    return block_rows[picks]


def shard_softmax(queries, picked, usable):
    scores = jnp.einsum("bqhk,bjk->bqhj", queries, picked, preferred_element_type=jnp.float32) * (
        DV + DR
    ) ** (-0.5)
    row_max = jnp.max(jnp.where(usable, scores, -1e30), axis=-1)
    weights = jnp.where(usable, jnp.exp(scores - row_max[..., None]), 0.0).astype(jnp.bfloat16)
    row_sum = jnp.sum(weights.astype(jnp.float32), -1)
    weighted = jnp.einsum(
        "bqhj,bjd->bqhd", weights, picked[..., :DL], preferred_element_type=jnp.float32
    )
    return (row_max, row_sum, weighted)


def expert_rows(arrived, w_gate, w_up, w_down):
    model_width = w_gate.shape[1]
    flat_rows = arrived.reshape(-1, model_width)
    gate_act = jnp.dot(flat_rows, w_gate[0], preferred_element_type=jnp.float32)
    up_act = jnp.dot(flat_rows, w_up[0], preferred_element_type=jnp.float32)
    activated = (jax.nn.silu(gate_act) * up_act).astype(jnp.bfloat16)
    partial_value = jnp.dot(activated, w_down[0], preferred_element_type=jnp.float32).astype(
        jnp.bfloat16
    )
    return partial_value.reshape(arrived.shape)


def per_device(
    residual,
    queries,
    latent_cache,
    blocks,
    lengths,
    value_up,
    out_proj,
    norm_gain,
    router,
    expert_ids,
    w_gate,
    w_up,
    w_down,
):
    local_reqs, drafts, head_count, qk_width = queries.shape
    shard_len = latent_cache.shape[1]
    picks_count = blocks.shape[2]
    seq_index = lax.axis_index("seq")
    block_view = latent_cache.reshape(local_reqs, shard_len // BLOCK, BLOCK, qk_width)
    picked = jax.vmap(pick_rows)(block_view, blocks[:, 0]).reshape(
        local_reqs, picks_count * BLOCK, qk_width
    )
    positions = (
        seq_index * shard_len + blocks[:, 0, :, None] * BLOCK + jnp.arange(BLOCK, dtype=jnp.int32)
    )
    positions = positions.reshape(local_reqs, picks_count * BLOCK)
    limits = lengths[:, None] - (drafts - 1) + jnp.arange(drafts, dtype=jnp.int32)[None, :]
    usable = positions[:, None, None, :] < limits[:, :, None, None]
    usable_mark = usable[:, :, 0, :].astype(jnp.bfloat16)
    all_keys, all_marks = (
        lax.all_gather(picked[None], "seq", axis=0, tiled=True),
        lax.all_gather(usable_mark[None], "seq", axis=0, tiled=True),
    )
    combined = None
    for shard in range(lax.axis_size("seq")):
        shard_usable = (all_marks[shard] > 0)[:, :, None, :]
        partial_value = shard_softmax(queries, all_keys[shard], shard_usable)
        combined = partial_value if combined is None else merge_parts(combined, partial_value)
    latent = (combined[2] / combined[1][..., None]).astype(jnp.bfloat16)
    head_values = jnp.einsum(
        "bqhd,hdv->bqhv", latent, value_up, preferred_element_type=jnp.float32
    ).astype(jnp.bfloat16)
    flat_values = head_values.reshape(local_reqs * drafts, head_count * DV)
    col_terms = jnp.dot(
        lax.all_gather(flat_values, "req", axis=0, tiled=True),
        out_proj,
        preferred_element_type=jnp.float32,
    )
    token_terms = lax.all_to_all(
        col_terms[None].astype(jnp.bfloat16),
        ("req", "seq", "exp"),
        split_axis=1,
        concat_axis=0,
        tiled=True,
    ).astype(jnp.float32)
    exp_count = lax.axis_size("exp")
    col_blocks = token_terms.shape[0] // exp_count
    rows_here = token_terms.shape[1]
    col_sums = jnp.sum(
        token_terms.reshape(col_blocks, exp_count, rows_here, token_terms.shape[2]), 1
    )
    attended = jnp.transpose(col_sums, (1, 0, 2)).reshape(rows_here, -1).astype(jnp.bfloat16)
    hidden_sum = (residual.astype(jnp.float32) + attended.astype(jnp.float32)).astype(jnp.bfloat16)
    hidden32 = hidden_sum.astype(jnp.float32)
    normed = (
        hidden32
        * lax.rsqrt(jnp.mean(hidden32 * hidden32, -1, keepdims=True) + 1e-06)
        * norm_gain.astype(jnp.float32)
    ).astype(jnp.bfloat16)
    gate_probs = jax.nn.sigmoid(jnp.dot(normed, router, preferred_element_type=jnp.float32))
    expert_count = router.shape[1]
    top_count = expert_ids.shape[1]
    one_hot = (expert_ids[:, :, None] == jnp.arange(expert_count, dtype=jnp.int32)).astype(
        jnp.int32
    )
    pair_hot = one_hot.reshape(rows_here * top_count, expert_count)
    slot_index = jnp.sum((jnp.cumsum(pair_hot, 0) - pair_hot) * pair_hot, -1)
    slot_hot = (slot_index[:, None] == jnp.arange(rows_here, dtype=jnp.int32)).astype(jnp.int32)
    placement = (pair_hot[:, :, None] * slot_hot[:, None, :]).reshape(
        rows_here, top_count, expert_count * rows_here
    )
    chosen = jnp.sum(one_hot.astype(jnp.float32) * gate_probs[:, None, :], -1)
    gate_weights = chosen / jnp.sum(chosen, -1, keepdims=True) * 2.5
    dispatch = jnp.sum(placement, 1).astype(jnp.bfloat16)
    outgoing = jnp.dot(dispatch.T, normed, preferred_element_type=jnp.float32).astype(jnp.bfloat16)
    outgoing = outgoing.reshape(expert_count, rows_here, outgoing.shape[1])
    combine = jnp.sum(gate_weights[:, :, None] * placement.astype(jnp.float32), 1)
    copies = lax.axis_size("seq") * exp_count
    fanned = jnp.broadcast_to(outgoing[:, None], (expert_count, copies) + outgoing.shape[1:])
    fanned = fanned.reshape((expert_count * copies,) + outgoing.shape[1:])
    returned = lax.all_to_all(
        expert_rows(
            lax.all_to_all(fanned, ("req", "seq", "exp"), split_axis=0, concat_axis=0, tiled=True),
            w_gate,
            w_up,
            w_down,
        ),
        ("req", "seq", "exp"),
        split_axis=0,
        concat_axis=0,
        tiled=True,
    )
    returned = returned.reshape((expert_count, copies) + outgoing.shape[1:]).astype(jnp.float32)
    expert_out = jnp.sum(returned, 1).astype(jnp.bfloat16)
    slot_rows = expert_out.reshape(expert_count * rows_here, expert_out.shape[2]).astype(
        jnp.float32
    )
    routed = jnp.dot(combine, slot_rows, precision=lax.Precision.HIGHEST)
    return (hidden32 + routed).astype(jnp.bfloat16)


MESH = pl.DeviceIdType.MESH


def column_cuts(width):
    return [(0, width - 256), (width - 256, width)]


def column_groups(width):
    cuts = column_cuts(width)
    return [(lo, min(lo + 256, cuts[0][1])) for lo in range(0, cuts[0][1], 256)] + cuts[1:]


def fused_kernel(
    dims,
    residual_ref,
    queries_hbm,
    cache_ref,
    blocks_ref,
    lengths_ref,
    value_up_hbm,
    out_proj_hbm,
    gain_ref,
    router_hbm,
    ids_ref,
    w_gate_hbm,
    w_up_hbm,
    w_down_hbm,
    out_ref,
    q_v,
    vu_v,
    op_v,
    rt_v,
    wg_v,
    wu_v,
    wd_v,
    keys_rx,
    marks,
    res_tx,
    res_rx,
    gains,
    lat,
    hv,
    acc,
    res_sum,
    hots,
    ys,
    parts_tx,
    parts_rx,
    xs,
    y_tx,
    y_rx,
    both,
    mid_tx,
    mid_rx,
    mid_sum,
    end_tx,
    end_rx,
    load_sem,
    key_sem,
    mark_sem,
    res_ssem,
    res_rsem,
    hz_sem,
    hs_sem,
    hot_sem,
    ps_sem,
    first_sem,
    second_sem,
    across_sem,
    ys_sem,
    mid_sem,
    end_sem,
):
    R, S, E = dims
    f32, b16 = jnp.float32, jnp.bfloat16
    r, s, e = lax.axis_index("req"), lax.axis_index("seq"), lax.axis_index("exp")
    other = 1 - s
    sibling = (r, other, e)
    drafts, half_heads, _ = q_v.shape
    keys_len = cache_ref.shape[0]
    width = op_v.shape[1]
    chunks = R * S
    nt = residual_ref.shape[0]
    devices = R * S * E
    mine = r * S + s
    at_home = (e == r).astype(jnp.int32)

    head_from = pl.multiple_of(s * half_heads, half_heads)
    loads = [
        pltpu.make_async_copy(queries_hbm.at[:, pl.ds(head_from, half_heads), :], q_v, load_sem.at[0]),
        pltpu.make_async_copy(value_up_hbm.at[pl.ds(head_from, half_heads)], vu_v, load_sem.at[1]),
        pltpu.make_async_copy(out_proj_hbm, op_v, load_sem.at[2]),
        pltpu.make_async_copy(router_hbm, rt_v, load_sem.at[3]),
        pltpu.make_async_copy(w_gate_hbm, wg_v, load_sem.at[4]),
        pltpu.make_async_copy(w_up_hbm, wu_v, load_sem.at[5]),
        pltpu.make_async_copy(w_down_hbm, wd_v, load_sem.at[6]),
    ]
    for load in loads:
        load.start()

    def z_peer(d):
        return (lax.rem(r + d, R), s, e)

    def e_peer(d):
        return (r, s, lax.rem(e + d, E))

    barrier = pltpu.get_barrier_semaphore()
    for peer in [sibling] + [z_peer(d) for d in range(1, R)] + [e_peer(d) for d in range(1, E)]:
        pl.semaphore_signal(barrier, inc=1, device_id=peer, device_id_type=MESH)
    for ss in range(S):
        for ee in range(E):

            @pl.when(jnp.logical_not((e == r) & (s == ss) & (e == ee)))
            def _():
                pl.semaphore_signal(barrier, inc=1, device_id=(e, ss, ee), device_id_type=MESH)

    gains[...] = gain_ref[...].astype(f32).reshape(gains.shape)
    block_of = lax.broadcasted_iota(jnp.int32, marks.shape[1:], 1) // BLOCK
    hit = block_of == blocks_ref[0]
    for i in range(1, blocks_ref.shape[0]):
        hit = hit | (block_of == blocks_ref[i])
    marks[0] = hit.astype(f32)
    lane = lax.broadcasted_iota(jnp.int32, (1, 128), 1)
    for t in range(nt):
        hot = lane == ids_ref[t, 0]
        for k in range(1, ids_ref.shape[1]):
            hot = hot | (lane == ids_ref[t, k])
        for c in range(chunks):
            res_tx[c, t : t + 1, width:] = hot.astype(f32)
    for c in range(chunks):
        res_tx[c, :, :width] = residual_ref[:, c * width : (c + 1) * width].astype(f32)

    pl.semaphore_wait(barrier, 1 + (R - 1) + (E - 1) + S * E - at_home)

    def remote(src, dst, ssem, rsem, peer):
        return pltpu.make_async_remote_copy(
            src_ref=src, dst_ref=dst, send_sem=ssem, recv_sem=rsem, device_id=peer, device_id_type=MESH
        )

    sent = []
    key_copy = remote(cache_ref, keys_rx, key_sem.at[0], key_sem.at[1], sibling)
    mark_copy = remote(marks.at[0], marks.at[1], mark_sem.at[0], mark_sem.at[1], sibling)
    key_copy.start()
    mark_copy.start()
    sent += [key_copy, mark_copy]
    slot = s * E + e
    for c in range(chunks):
        to = (c // S, c % S, r)
        here = (r == c // S) & (s == c % S) & (e == r)

        @pl.when(jnp.logical_not(here))
        def _():
            remote(res_tx.at[c], res_rx.at[slot], res_ssem.at[c], res_rsem.at[slot], to).start()

        @pl.when(here)
        def _():
            pltpu.make_async_copy(res_tx.at[c], res_rx.at[slot], res_rsem.at[slot]).start()

    loads[0].wait()
    q2 = q_v[...].reshape(drafts * half_heads, q_v.shape[2])
    rows = drafts * half_heads
    limit = lengths_ref[0] - (drafts - 1) + lax.broadcasted_iota(jnp.int32, (rows, 1), 0) // half_heads

    def scores_of(keys, mark, shard):
        sc = lax.dot_general(q2, keys, (((1,), (1,)), ((), ())), preferred_element_type=f32)
        pos = shard * keys_len + lax.broadcasted_iota(jnp.int32, (rows, keys_len), 1)
        usable = (pos < limit) & (mark > 0)
        return jnp.where(usable, sc * (DV + DR) ** (-0.5), -1e30), usable

    near, near_ok = scores_of(cache_ref[...], marks[0, :1, :keys_len], s)
    key_copy.wait_recv()
    mark_copy.wait_recv()
    far, far_ok = scores_of(keys_rx[...], marks[1, :1, :keys_len], other)
    top = jnp.maximum(jnp.max(near, -1, keepdims=True), jnp.max(far, -1, keepdims=True))
    near_p = jnp.where(near_ok, jnp.exp(near - top), 0.0).astype(b16)
    far_p = jnp.where(far_ok, jnp.exp(far - top), 0.0).astype(b16)
    total = jnp.sum(near_p.astype(f32), -1, keepdims=True) + jnp.sum(far_p.astype(f32), -1, keepdims=True)
    weighted = jnp.dot(near_p, cache_ref[:, :DL], preferred_element_type=f32)
    weighted += jnp.dot(far_p, keys_rx[:, :DL], preferred_element_type=f32)
    latent = weighted / total
    for k in range(lat.shape[0]):
        lat[k] = latent[:, k * 128 : (k + 1) * 128]

    pieces = hv.shape[1]
    piece_heads = half_heads // pieces
    depth = piece_heads * DV
    loads[1].wait()
    hz = []
    for p in range(pieces):
        for n in range(piece_heads):
            h = p * piece_heads + n
            one = [lat[k, pl.ds(h, drafts, stride=half_heads), :] for k in range(lat.shape[0])]
            one = jnp.concatenate(one, axis=1).astype(b16)
            value = jnp.dot(one, vu_v[h], preferred_element_type=f32)
            hv[s, p, r, :, n * DV : (n + 1) * DV] = value.astype(b16)
        block = hv.at[s, p, r]
        hz.append(
            [remote(block, block, hz_sem.at[0, p, d - 1], hz_sem.at[1, p, d - 1], z_peer(d)) for d in range(1, R)]
        )
        for copy in hz[p]:
            copy.start()
        sent += hz[p]

    cuts = column_cuts(width)
    loads[2].wait()

    def out_part(side, p, lo, hi):
        head_rows = hv[side, p].reshape(R * drafts, depth)
        at = pl.ds(pl.multiple_of((side * pieces + p) * depth, depth), depth)
        part = jnp.dot(head_rows, op_v[at, lo:hi], preferred_element_type=f32)
        return part.reshape(E, drafts, hi - lo)

    hs = []
    for p in range(pieces):
        for copy in hz[p]:
            copy.wait_recv()
        whole = hv.at[s, p]
        hs.append(remote(whole, whole, hs_sem.at[0, p], hs_sem.at[1, p], sibling))
        hs[p].start()
        part = out_part(s, p, 0, width)
        if p:
            hs[p - 1].wait_recv()
            part += out_part(other, p - 1, 0, width)
            acc[...] += part
        else:
            acc[...] = part
    sent += hs
    for j in range(S * E):
        pltpu.make_async_copy(res_rx.at[j], res_rx.at[j], res_rsem.at[j]).wait()
        res_sum[j * nt : (j + 1) * nt, :] = res_rx[j]
    hots[e] = res_sum[:, width:].astype(b16)
    hot_copies = [
        remote(hots.at[e], hots.at[e], hot_sem.at[0, d - 1], hot_sem.at[1, d - 1], e_peer(d)) for d in range(1, E)
    ]
    for copy in hot_copies:
        copy.start()
    sent += hot_copies
    hs[-1].wait_recv()
    ps = [None, None]
    for i in (1, 0):
        lo, hi = cuts[i]
        acc[:, :, lo:hi] += out_part(other, pieces - 1, lo, hi)
        parts_tx[i][...] = acc[:, :, lo:hi].astype(b16)
        ps[i] = [
            remote(
                parts_tx[i].at[lax.rem(e + d, E)],
                parts_rx[i].at[d - 1],
                ps_sem.at[0, i, d - 1],
                ps_sem.at[1, i, d - 1],
                e_peer(d),
            )
            for d in range(1, E)
        ]
        for copy in ps[i]:
            copy.start()
        sent += ps[i]

    def chunk_at(d):
        return lax.rem(r + R - d, R) * S + s

    def group_at(d):
        return lax.rem(e + E - d, E)

    first = [None, None]
    for i in (1, 0):
        lo, hi = cuts[i]
        attended = acc[e, :, lo:hi]
        for d in range(1, E):
            ps[i][d - 1].wait_recv()
            attended += parts_rx[i][d - 1].astype(f32)
        xs[i][mine, e] = (res_sum[:, lo:hi] + attended.astype(b16).astype(f32)).astype(b16)
        block = xs[i].at[mine, e]
        first[i] = [
            remote(block, block, first_sem.at[0, i, d - 1], first_sem.at[1, i, d - 1], (e_peer if i else z_peer)(d))
            for d in range(1, E if i else R)
        ]
        for copy in first[i]:
            copy.start()
        sent += first[i]
    second = [[], []]
    for hop in range(max(R, E)):
        for i in (1, 0):
            if hop >= (E if i else R):
                continue
            if hop:
                first[i][hop - 1].wait_recv()
            block = xs[i].at[mine, group_at(hop)] if i else xs[i].at[chunk_at(hop), e]
            row = [
                remote(
                    block,
                    block,
                    second_sem.at[0, i, hop, d - 1],
                    second_sem.at[1, i, hop, d - 1],
                    (z_peer if i else e_peer)(d),
                )
                for d in range(1, R if i else E)
            ]
            for copy in row:
                copy.start()
            second[i].append(row)
            sent += row
    for load in loads[3:6]:
        load.wait()

    tokens = E * drafts

    def expert_part(state, chunk, i):
        squares, gate, up, logits = state
        lo, hi = cuts[i]
        hid = xs[i][chunk].reshape(tokens, hi - lo).astype(f32)
        cols = pl.ds(pl.multiple_of(chunk * width + lo, 128), hi - lo)
        scaled = (hid * gains[:, cols]).astype(b16)
        return (
            squares + jnp.sum(hid * hid, -1, keepdims=True),
            gate + jnp.dot(scaled, wg_v[cols, :], preferred_element_type=f32),
            up + jnp.dot(scaled, wu_v[cols, :], preferred_element_type=f32),
            logits + lax.dot_general(scaled, rt_v[:, cols], (((1,), (1,)), ((), ())), preferred_element_type=f32),
        )

    state = (
        jnp.zeros((tokens, 1), f32),
        jnp.zeros((tokens, wg_v.shape[1]), f32),
        jnp.zeros((tokens, wg_v.shape[1]), f32),
        jnp.zeros((tokens, rt_v.shape[0]), f32),
    )
    across = []

    def arrived(state, d):
        for i in (0, 1):
            across[2 * d + i].wait_recv()
            state = expert_part(state, lax.rem(r + R - d, R) * S + other, i)
        return state

    for d in range(R):
        for i in (0, 1):
            if i == 0:
                waits = second[0][d]
            elif d == 0:
                waits = []
            else:
                waits = [row[d - 1] for row in second[1]]
            for copy in waits:
                copy.wait_recv()
            whole = xs[i].at[chunk_at(d)]
            copy = remote(whole, whole, across_sem.at[0, i, d], across_sem.at[1, i, d], sibling)
            copy.start()
            across.append(copy)
            state = expert_part(state, chunk_at(d), i)
        if d:
            state = arrived(state, d - 1)
    state = arrived(state, R - 1)
    sent += across
    squares, gate, up, logits = state
    scale = lax.rsqrt(squares / (chunks * width) + 1e-06)
    experts = rt_v.shape[0]
    for copy in hot_copies:
        copy.wait_recv()
    chosen = hots[...].reshape(tokens, 128)[:, :experts].astype(f32) * jax.nn.sigmoid(logits * scale)
    this_expert = lax.broadcasted_iota(jnp.int32, (1, experts), 1) == r
    weight = jnp.sum(jnp.where(this_expert, chosen, 0.0), -1, keepdims=True)
    weight = weight / jnp.sum(chosen, -1, keepdims=True) * 2.5
    activated = (jax.nn.silu(gate * scale) * (up * scale) * weight).astype(b16)

    to_row = lax.broadcasted_iota(jnp.int32, (tokens, tokens), 0)
    from_row = lax.broadcasted_iota(jnp.int32, (tokens, tokens), 1)
    owner = to_row % devices
    wanted = ((owner % R) * (S * E) + owner // R) * nt + to_row // devices
    ordered = jnp.dot((wanted == from_row).astype(b16), activated, preferred_element_type=f32).astype(b16)
    loads[6].wait()
    per_owner = nt * chunks
    groups = column_groups(width)
    order = [len(groups) - 1] + list(range(len(groups) - 1))
    half_rows = R * E * per_owner

    def summed(side, lo, hi):
        at = pl.ds(pl.multiple_of(side * half_rows, half_rows), half_rows)
        part = jnp.concatenate([ys[k, at, :] for k in range(lo // 128, hi // 128)], axis=1)
        return part.reshape(E, R, per_owner, hi - lo)

    with_core, mid, end = {}, {}, {}

    def peers_of(g):
        return (z_peer, r, R, e_peer, e, E) if g == len(groups) - 1 else (e_peer, e, E, z_peer, r, R)

    def begin(g):
        lo, hi = groups[g]
        for c in range(chunks):
            down = jnp.dot(ordered, wd_v[:, c * width + lo : c * width + hi], preferred_element_type=f32)
            for t in range(nt):
                part = down[t * devices : (t + 1) * devices]
                for k in range(lo // 128, hi // 128):
                    column = part[:, k * 128 - lo : (k + 1) * 128 - lo]
                    ys[k, pl.ds(c * nt + t, devices, stride=per_owner), :] = column
        y_tx[g][...] = summed(other, lo, hi).astype(b16)
        with_core[g] = remote(y_tx[g], y_rx[g], ys_sem.at[0, g], ys_sem.at[1, g], sibling)
        with_core[g].start()

    def middle(g):
        lo, hi = groups[g]
        peer, me, count = peers_of(g)[:3]
        with_core[g].wait_recv()
        both[g][...] = summed(s, lo, hi) + y_rx[g][...].astype(f32)
        mid[g] = []
        for d in range(1, count):
            to = lax.rem(me + d, count)
            block = both[g][:, to] if g == len(groups) - 1 else both[g][to]
            mid_tx[g][d - 1] = block.astype(b16)
            copy = remote(
                mid_tx[g].at[d - 1], mid_rx[g].at[d - 1], mid_sem.at[0, g, d - 1], mid_sem.at[1, g, d - 1], peer(d)
            )
            copy.start()
            mid[g].append(copy)

    for n, g in enumerate(order):
        begin(g)
        if n:
            middle(order[n - 1])
    middle(order[-1])
    for g in order:
        peer, me, count = peers_of(g)[3:]
        total_g = both[g][:, r] if g == len(groups) - 1 else both[g][e]
        for d, copy in enumerate(mid[g]):
            copy.wait_recv()
            total_g += mid_rx[g][d].astype(f32)
        mid_sum[g][...] = total_g
        end_tx[g][...] = total_g.astype(b16)
        end[g] = []
        for d in range(1, count):
            to = lax.rem(me + d, count)
            copy = remote(
                end_tx[g].at[to], end_rx[g].at[d - 1], end_sem.at[0, g, d - 1], end_sem.at[1, g, d - 1], peer(d)
            )
            copy.start()
            end[g].append(copy)
        sent += [with_core[g]] + mid[g] + end[g]
    pick = lax.broadcasted_iota(jnp.int32, (8, tokens), 0) + (mine * E + e) * nt
    pick = (pick == lax.broadcasted_iota(jnp.int32, (8, tokens), 1)).astype(b16)
    own = []
    for c in range(chunks):
        sides = [
            jnp.dot(pick, xs[i][c].reshape(tokens, hi - lo), preferred_element_type=f32)
            for i, (lo, hi) in enumerate(cuts)
        ]
        own.append(jnp.concatenate(sides, axis=1))
    for g in order:
        lo, hi = groups[g]
        routed = mid_sum[g][peers_of(g)[4]]
        for d, copy in enumerate(end[g]):
            copy.wait_recv()
            routed += end_rx[g][d].astype(f32)
        for c in range(chunks):
            value = own[c][:nt, lo:hi] + routed[c * nt : (c + 1) * nt]
            out_ref[:, c * width + lo : c * width + hi] = value.astype(b16)

    for copy in sent:
        copy.wait_send()
    for c in range(chunks):
        here = (r == c // S) & (s == c % S) & (e == r)

        @pl.when(jnp.logical_not(here))
        def _():
            remote(res_tx.at[c], res_rx.at[slot], res_ssem.at[c], res_rsem.at[slot], (c // S, c % S, r)).wait_send()


def fused(
    dims, residual, queries, cache, blocks, lengths, value_up, out_proj, gain, router, ids, w_gate, w_up, w_down
):
    R, S, E = dims
    f32, b16 = jnp.float32, jnp.bfloat16
    drafts, heads, qk = queries.shape
    half_heads = heads // S
    width = out_proj.shape[1]
    nt, model = residual.shape
    keys_len = cache.shape[0]
    chunks = R * S
    lanes = -(-keys_len // 128) * 128
    ff = w_gate.shape[1]
    per_owner = nt * chunks
    cuts, groups = column_cuts(width), column_groups(width)
    pieces = 4
    dma = pltpu.SemaphoreType.DMA
    vmem, smem, hbm = (pl.BlockSpec(memory_space=m) for m in (pltpu.VMEM, pltpu.SMEM, pl.ANY))
    scratch = [
        pltpu.VMEM((drafts, half_heads, qk), b16),
        pltpu.VMEM((half_heads,) + value_up.shape[1:], b16),
        pltpu.VMEM(out_proj.shape, b16),
        pltpu.VMEM(router.shape, b16),
        pltpu.VMEM(w_gate.shape, b16),
        pltpu.VMEM(w_up.shape, b16),
        pltpu.VMEM(w_down.shape, b16),
        pltpu.VMEM(cache.shape, b16),
        pltpu.VMEM((2, 8, lanes), f32),
        pltpu.VMEM((chunks, nt, width + 128), f32),
        pltpu.VMEM((S * E, nt, width + 128), f32),
        pltpu.VMEM((1, model), f32),
        pltpu.VMEM((DL // 128, drafts * half_heads, 128), f32),
        pltpu.VMEM((S, pieces, R, drafts, half_heads // pieces * DV), b16),
        pltpu.VMEM((E, drafts, width), f32),
        pltpu.VMEM((drafts, width + 128), f32),
        pltpu.VMEM((E, drafts, 128), b16),
        pltpu.VMEM((width // 128, R * S * E * per_owner, 128), f32),
        [pltpu.VMEM((E, drafts, hi - lo), b16) for lo, hi in cuts],
        [pltpu.VMEM((E - 1, drafts, hi - lo), b16) for lo, hi in cuts],
        [pltpu.VMEM((chunks, E, drafts, hi - lo), b16) for lo, hi in cuts],
        [pltpu.VMEM((E, R, per_owner, hi - lo), b16) for lo, hi in groups],
        [pltpu.VMEM((E, R, per_owner, hi - lo), b16) for lo, hi in groups],
        [pltpu.VMEM((E, R, per_owner, hi - lo), f32) for lo, hi in groups],
        [pltpu.VMEM((E - 1, R, per_owner, hi - lo), b16) for lo, hi in groups],
        [pltpu.VMEM((E - 1, R, per_owner, hi - lo), b16) for lo, hi in groups],
        [pltpu.VMEM((R, per_owner, hi - lo), f32) for lo, hi in groups],
        [pltpu.VMEM((R, per_owner, hi - lo), b16) for lo, hi in groups],
        [pltpu.VMEM((R - 1, per_owner, hi - lo), b16) for lo, hi in groups],
        dma((7,)),
        dma((2,)),
        dma((2,)),
        dma((chunks,)),
        dma((S * E,)),
        dma((2, pieces, R - 1)),
        dma((2, pieces)),
        dma((2, E - 1)),
        dma((2, 2, E - 1)),
        dma((2, 2, R - 1)),
        dma((2, 2, R, E - 1)),
        dma((2, 2, R)),
        dma((2, len(groups))),
        dma((2, len(groups), E - 1)),
        dma((2, len(groups), E - 1)),
    ]
    return pl.pallas_call(
        functools.partial(fused_kernel, dims),
        out_shape=jax.ShapeDtypeStruct((nt, model), b16),
        in_specs=[vmem, hbm, vmem, smem, smem, hbm, hbm, vmem, hbm, smem, hbm, hbm, hbm],
        out_specs=vmem,
        scratch_shapes=scratch,
        compiler_params=pltpu.CompilerParams(
            collective_id=0, has_side_effects=True, vmem_limit_bytes=56 * 1024 * 1024
        ),
        cost_estimate=pl.CostEstimate(
            flops=2 * R * drafts * (out_proj.size + 3 * w_gate.size),
            bytes_accessed=2 * (value_up.size + out_proj.size + 3 * w_gate.size),
            transcendentals=0,
        ),
    )(residual, queries, cache, blocks, lengths, value_up, out_proj, gain, router, ids, w_gate, w_up, w_down)


def per_device_fused(dims, *args):
    (residual, queries, cache, blocks, lengths, value_up, out_proj, gain, router, ids, w_gate, w_up, w_down) = args
    return fused(
        dims,
        residual,
        queries[0],
        cache[0],
        blocks[0, 0],
        lengths,
        value_up,
        out_proj,
        gain,
        router.T,
        ids,
        w_gate[0],
        w_up[0],
        w_down[0],
    )


def fits_fused(dims, shapes):
    R, S, E = dims
    residual, queries, cache, router = shapes[0], shapes[1], shapes[2], shapes[8]
    drafts, heads, model = queries[1], queries[2], residual[1]
    return (
        S == 2
        and R == E
        and queries[0] == R
        and router[1] == R
        and drafts % 16 == 0
        and residual[0] == R * drafts
        and heads % (E * S * 16) == 0
        and model % (R * S * 128) == 0
        and model // (R * S) >= 384
        and (residual[0] // E) % 16 == 0
        and (drafts // (S * E) * R * S) % 16 == 0
        and cache[1] // S % BLOCK == 0
    )


def solution(mesh):
    in_specs = (
        P(("req", "seq", "exp"), None),
        P("req", None, "exp", None),
        P("req", "seq", None),
        P("req", "seq", None),
        P("req"),
        P("exp", None, None),
        P("exp", ("req", "seq")),
        P(),
        P(),
        P(("req", "seq", "exp"), None),
        P("req", None, ("seq", "exp")),
        P("req", None, ("seq", "exp")),
        P("req", ("seq", "exp"), None),
    )
    out_specs = P(("req", "seq", "exp"), None)
    dims = (mesh.shape["req"], mesh.shape["seq"], mesh.shape["exp"])

    def layer(*args):
        fast = fits_fused(dims, [a.shape for a in args])
        body = functools.partial(per_device_fused, dims) if fast else per_device
        return jax.shard_map(body, mesh=mesh, in_specs=in_specs, out_specs=out_specs, check_vma=False)(*args)

    return layer
```

```python
import functools

import jax
import jax.numpy as jnp
from jax import lax
from jax.experimental import pallas as pl
from jax.experimental.pallas import tpu as pltpu
from jax.sharding import PartitionSpec as P

DL = 512
DR = 64
DV = 128
BLOCK = 64


def merge_parts(former, latter):
    row_max = jnp.maximum(former[0], latter[0])
    left_scale = jnp.exp(former[0] - row_max)
    right_scale = jnp.exp(latter[0] - row_max)
    return (
        row_max,
        left_scale * former[1] + right_scale * latter[1],
        left_scale[..., None] * former[2] + right_scale[..., None] * latter[2],
    )


def pick_rows(block_rows, picks):
    return block_rows[picks]


def shard_softmax(queries, picked, usable):
    scores = jnp.einsum("bqhk,bjk->bqhj", queries, picked, preferred_element_type=jnp.float32) * (
        DV + DR
    ) ** (-0.5)
    row_max = jnp.max(jnp.where(usable, scores, -1e30), axis=-1)
    weights = jnp.where(usable, jnp.exp(scores - row_max[..., None]), 0.0).astype(jnp.bfloat16)
    row_sum = jnp.sum(weights.astype(jnp.float32), -1)
    weighted = jnp.einsum(
        "bqhj,bjd->bqhd", weights, picked[..., :DL], preferred_element_type=jnp.float32
    )
    return (row_max, row_sum, weighted)


def expert_rows(arrived, w_gate, w_up, w_down):
    model_width = w_gate.shape[1]
    flat_rows = arrived.reshape(-1, model_width)
    gate_act = jnp.dot(flat_rows, w_gate[0], preferred_element_type=jnp.float32)
    up_act = jnp.dot(flat_rows, w_up[0], preferred_element_type=jnp.float32)
    activated = (jax.nn.silu(gate_act) * up_act).astype(jnp.bfloat16)
    partial_value = jnp.dot(activated, w_down[0], preferred_element_type=jnp.float32).astype(
        jnp.bfloat16
    )
    return partial_value.reshape(arrived.shape)


def per_device(
    residual,
    queries,
    latent_cache,
    blocks,
    lengths,
    value_up,
    out_proj,
    norm_gain,
    router,
    expert_ids,
    w_gate,
    w_up,
    w_down,
):
    local_reqs, drafts, head_count, qk_width = queries.shape
    shard_len = latent_cache.shape[1]
    picks_count = blocks.shape[2]
    seq_index = lax.axis_index("seq")
    block_view = latent_cache.reshape(local_reqs, shard_len // BLOCK, BLOCK, qk_width)
    picked = jax.vmap(pick_rows)(block_view, blocks[:, 0]).reshape(
        local_reqs, picks_count * BLOCK, qk_width
    )
    positions = (
        seq_index * shard_len + blocks[:, 0, :, None] * BLOCK + jnp.arange(BLOCK, dtype=jnp.int32)
    )
    positions = positions.reshape(local_reqs, picks_count * BLOCK)
    limits = lengths[:, None] - (drafts - 1) + jnp.arange(drafts, dtype=jnp.int32)[None, :]
    usable = positions[:, None, None, :] < limits[:, :, None, None]
    usable_mark = usable[:, :, 0, :].astype(jnp.bfloat16)
    all_keys, all_marks = (
        lax.all_gather(picked[None], "seq", axis=0, tiled=True),
        lax.all_gather(usable_mark[None], "seq", axis=0, tiled=True),
    )
    combined = None
    for shard in range(lax.axis_size("seq")):
        shard_usable = (all_marks[shard] > 0)[:, :, None, :]
        partial_value = shard_softmax(queries, all_keys[shard], shard_usable)
        combined = partial_value if combined is None else merge_parts(combined, partial_value)
    latent = (combined[2] / combined[1][..., None]).astype(jnp.bfloat16)
    head_values = jnp.einsum(
        "bqhd,hdv->bqhv", latent, value_up, preferred_element_type=jnp.float32
    ).astype(jnp.bfloat16)
    flat_values = head_values.reshape(local_reqs * drafts, head_count * DV)
    col_terms = jnp.dot(
        lax.all_gather(flat_values, "req", axis=0, tiled=True),
        out_proj,
        preferred_element_type=jnp.float32,
    )
    token_terms = lax.all_to_all(
        col_terms[None].astype(jnp.bfloat16),
        ("req", "seq", "exp"),
        split_axis=1,
        concat_axis=0,
        tiled=True,
    ).astype(jnp.float32)
    exp_count = lax.axis_size("exp")
    col_blocks = token_terms.shape[0] // exp_count
    rows_here = token_terms.shape[1]
    col_sums = jnp.sum(
        token_terms.reshape(col_blocks, exp_count, rows_here, token_terms.shape[2]), 1
    )
    attended = jnp.transpose(col_sums, (1, 0, 2)).reshape(rows_here, -1).astype(jnp.bfloat16)
    hidden_sum = (residual.astype(jnp.float32) + attended.astype(jnp.float32)).astype(jnp.bfloat16)
    hidden32 = hidden_sum.astype(jnp.float32)
    normed = (
        hidden32
        * lax.rsqrt(jnp.mean(hidden32 * hidden32, -1, keepdims=True) + 1e-06)
        * norm_gain.astype(jnp.float32)
    ).astype(jnp.bfloat16)
    gate_probs = jax.nn.sigmoid(jnp.dot(normed, router, preferred_element_type=jnp.float32))
    expert_count = router.shape[1]
    top_count = expert_ids.shape[1]
    one_hot = (expert_ids[:, :, None] == jnp.arange(expert_count, dtype=jnp.int32)).astype(
        jnp.int32
    )
    pair_hot = one_hot.reshape(rows_here * top_count, expert_count)
    slot_index = jnp.sum((jnp.cumsum(pair_hot, 0) - pair_hot) * pair_hot, -1)
    slot_hot = (slot_index[:, None] == jnp.arange(rows_here, dtype=jnp.int32)).astype(jnp.int32)
    placement = (pair_hot[:, :, None] * slot_hot[:, None, :]).reshape(
        rows_here, top_count, expert_count * rows_here
    )
    chosen = jnp.sum(one_hot.astype(jnp.float32) * gate_probs[:, None, :], -1)
    gate_weights = chosen / jnp.sum(chosen, -1, keepdims=True) * 2.5
    dispatch = jnp.sum(placement, 1).astype(jnp.bfloat16)
    outgoing = jnp.dot(dispatch.T, normed, preferred_element_type=jnp.float32).astype(jnp.bfloat16)
    outgoing = outgoing.reshape(expert_count, rows_here, outgoing.shape[1])
    combine = jnp.sum(gate_weights[:, :, None] * placement.astype(jnp.float32), 1)
    copies = lax.axis_size("seq") * exp_count
    fanned = jnp.broadcast_to(outgoing[:, None], (expert_count, copies) + outgoing.shape[1:])
    fanned = fanned.reshape((expert_count * copies,) + outgoing.shape[1:])
    returned = lax.all_to_all(
        expert_rows(
            lax.all_to_all(fanned, ("req", "seq", "exp"), split_axis=0, concat_axis=0, tiled=True),
            w_gate,
            w_up,
            w_down,
        ),
        ("req", "seq", "exp"),
        split_axis=0,
        concat_axis=0,
        tiled=True,
    )
    returned = returned.reshape((expert_count, copies) + outgoing.shape[1:]).astype(jnp.float32)
    expert_out = jnp.sum(returned, 1).astype(jnp.bfloat16)
    slot_rows = expert_out.reshape(expert_count * rows_here, expert_out.shape[2]).astype(
        jnp.float32
    )
    routed = jnp.dot(combine, slot_rows, precision=lax.Precision.HIGHEST)
    return (hidden32 + routed).astype(jnp.bfloat16)


MESH = pl.DeviceIdType.MESH


def column_cuts(width):
    return [(0, width - 256), (width - 256, width)]


def column_groups(width):
    cuts = column_cuts(width)
    return [(lo, min(lo + 256, cuts[0][1])) for lo in range(0, cuts[0][1], 256)] + cuts[1:]


def flipped(index, mask):
    bit = 1
    while bit <= mask:
        if mask & bit:
            index = index + bit - 2 * bit * lax.rem(lax.div(index, bit), 2)
        bit *= 2
    return index


def fused_kernel(
    dims,
    residual_ref,
    queries_hbm,
    cache_hbm,
    blocks_ref,
    lengths_ref,
    value_up_hbm,
    out_proj_hbm,
    gain_ref,
    router_hbm,
    ids_ref,
    w_gate_hbm,
    w_up_hbm,
    w_down_hbm,
    out_ref,
    q_v,
    vu_v,
    op_v,
    rt_v,
    wg_v,
    wu_v,
    wd_v,
    keys_own,
    keys_rx,
    marks,
    res_tx,
    res_rx,
    gains,
    lat,
    hv,
    acc,
    res_sum,
    hots,
    ys,
    parts_tx,
    parts_rx,
    xs,
    y_tx,
    y_rx,
    both,
    mid_tx,
    mid_rx,
    mid_sum,
    end_tx,
    end_rx,
    load_sem,
    key_sem,
    mark_sem,
    res_ssem,
    res_rsem,
    hz_sem,
    hs_sem,
    hot_sem,
    ps_sem,
    first_sem,
    second_sem,
    across_sem,
    ys_sem,
    mid_sem,
    end_sem,
):
    R, S, E = dims
    f32, b16 = jnp.float32, jnp.bfloat16
    r, s, e = lax.axis_index("req"), lax.axis_index("seq"), lax.axis_index("exp")
    other = 1 - s
    sibling = (r, other, e)
    drafts, half_heads, _ = q_v.shape
    keys_len = cache_hbm.shape[0]
    width = op_v.shape[1]
    chunks = R * S
    nt = residual_ref.shape[0]
    devices = R * S * E
    mine = r * S + s
    at_home = (e == r).astype(jnp.int32)

    head_from = pl.multiple_of(s * half_heads, half_heads)
    loads = [
        pltpu.make_async_copy(queries_hbm.at[:, pl.ds(head_from, half_heads), :], q_v, load_sem.at[0]),
        pltpu.make_async_copy(value_up_hbm.at[pl.ds(head_from, half_heads)], vu_v, load_sem.at[1]),
        pltpu.make_async_copy(out_proj_hbm, op_v, load_sem.at[2]),
        pltpu.make_async_copy(router_hbm, rt_v, load_sem.at[3]),
        pltpu.make_async_copy(w_gate_hbm, wg_v, load_sem.at[4]),
        pltpu.make_async_copy(w_up_hbm, wu_v, load_sem.at[5]),
        pltpu.make_async_copy(w_down_hbm, wd_v, load_sem.at[6]),
    ]
    keys_copy = pltpu.make_async_copy(cache_hbm, keys_own, load_sem.at[7])
    keys_copy.start()
    for load in loads[:2]:
        load.start()

    def z_peer(d):
        return (flipped(r, d), s, e)

    def e_peer(d):
        return (r, s, flipped(e, d))

    barrier = pltpu.get_barrier_semaphore()
    for peer in [sibling] + [z_peer(d) for d in range(1, R)] + [e_peer(d) for d in range(1, E)]:
        pl.semaphore_signal(barrier, inc=1, device_id=peer, device_id_type=MESH)
    for ss in range(S):
        for ee in range(E):

            @pl.when(jnp.logical_not((e == r) & (s == ss) & (e == ee)))
            def _():
                pl.semaphore_signal(barrier, inc=1, device_id=(e, ss, ee), device_id_type=MESH)

    block_of = lax.broadcasted_iota(jnp.int32, marks.shape[1:], 1) // BLOCK
    hit = block_of == blocks_ref[0]
    for i in range(1, blocks_ref.shape[0]):
        hit = hit | (block_of == blocks_ref[i])
    marks[0] = hit.astype(f32)
    pl.semaphore_wait(barrier, 1 + (R - 1) + (E - 1) + S * E - at_home)

    def remote(src, dst, ssem, rsem, peer):
        return pltpu.make_async_remote_copy(
            src_ref=src, dst_ref=dst, send_sem=ssem, recv_sem=rsem, device_id=peer, device_id_type=MESH
        )

    sent = []
    key_copy = remote(cache_hbm, keys_rx, key_sem.at[0], key_sem.at[1], sibling)
    mark_copy = remote(marks.at[0], marks.at[1], mark_sem.at[0], mark_sem.at[1], sibling)
    key_copy.start()
    mark_copy.start()
    sent += [key_copy, mark_copy]
    loads[0].wait()
    keys_copy.wait()
    q2 = q_v[...].reshape(drafts * half_heads, q_v.shape[2])
    rows = drafts * half_heads
    limit = lengths_ref[0] - (drafts - 1) + lax.broadcasted_iota(jnp.int32, (rows, 1), 0) // half_heads

    def scores_of(keys, mark, shard):
        sc = lax.dot_general(q2, keys, (((1,), (1,)), ((), ())), preferred_element_type=f32)
        pos = shard * keys_len + lax.broadcasted_iota(jnp.int32, (rows, keys_len), 1)
        usable = (pos < limit) & (mark > 0)
        return jnp.where(usable, sc * (DV + DR) ** (-0.5), -1e30), usable

    near, near_ok = scores_of(keys_own[...], marks[0, :1, :keys_len], s)
    for load in loads[2:]:
        load.start()
    key_copy.wait_recv()
    mark_copy.wait_recv()
    far, far_ok = scores_of(keys_rx[...], marks[1, :1, :keys_len], other)
    top = jnp.maximum(jnp.max(near, -1, keepdims=True), jnp.max(far, -1, keepdims=True))
    near_p = jnp.where(near_ok, jnp.exp(near - top), 0.0).astype(b16)
    far_p = jnp.where(far_ok, jnp.exp(far - top), 0.0).astype(b16)
    total = jnp.sum(near_p.astype(f32), -1, keepdims=True) + jnp.sum(far_p.astype(f32), -1, keepdims=True)
    weighted = jnp.dot(near_p, keys_own[:, :DL], preferred_element_type=f32)
    weighted += jnp.dot(far_p, keys_rx[:, :DL], preferred_element_type=f32)
    latent = weighted / total
    for k in range(lat.shape[0]):
        lat[k] = latent[:, k * 128 : (k + 1) * 128]

    pieces = hv.shape[1]
    piece_heads = half_heads // pieces
    depth = piece_heads * DV
    loads[1].wait()
    hz = []
    for p in range(pieces):
        for n in range(piece_heads):
            h = p * piece_heads + n
            one = [lat[k, pl.ds(h, drafts, stride=half_heads), :] for k in range(lat.shape[0])]
            one = jnp.concatenate(one, axis=1).astype(b16)
            value = jnp.dot(one, vu_v[h], preferred_element_type=f32)
            hv[s, p, r, :, n * DV : (n + 1) * DV] = value.astype(b16)
        block = hv.at[s, p, r]
        hz.append(
            [remote(block, block, hz_sem.at[0, p, d - 1], hz_sem.at[1, p, d - 1], z_peer(d)) for d in range(1, R)]
        )
        for copy in hz[p]:
            copy.start()
        sent += hz[p]

    gains[...] = gain_ref[...].astype(f32).reshape(gains.shape)
    lane = lax.broadcasted_iota(jnp.int32, (1, 128), 1)
    for t in range(nt):
        hot = lane == ids_ref[t, 0]
        for k in range(1, ids_ref.shape[1]):
            hot = hot | (lane == ids_ref[t, k])
        for c in range(chunks):
            res_tx[c, t : t + 1, width:] = hot.astype(f32)
    for c in range(chunks):
        res_tx[c, :, :width] = residual_ref[:, c * width : (c + 1) * width].astype(f32)
    slot = s * E + e
    for c in range(chunks):
        to = (c // S, c % S, r)
        here = (r == c // S) & (s == c % S) & (e == r)

        @pl.when(jnp.logical_not(here))
        def _():
            remote(res_tx.at[c], res_rx.at[slot], res_ssem.at[c], res_rsem.at[slot], to).start()

        @pl.when(here)
        def _():
            pltpu.make_async_copy(res_tx.at[c], res_rx.at[slot], res_rsem.at[slot]).start()

    cuts = column_cuts(width)
    loads[2].wait()

    def out_part(side, p, lo, hi):
        head_rows = hv[side, p].reshape(R * drafts, depth)
        at = pl.ds(pl.multiple_of((side * pieces + p) * depth, depth), depth)
        part = jnp.dot(head_rows, op_v[at, lo:hi], preferred_element_type=f32)
        return part.reshape(E, drafts, hi - lo)

    hs = []
    for p in range(pieces):
        for copy in hz[p]:
            copy.wait_recv()
        whole = hv.at[s, p]
        hs.append(remote(whole, whole, hs_sem.at[0, p], hs_sem.at[1, p], sibling))
        hs[p].start()
        part = out_part(s, p, 0, width)
        if p:
            hs[p - 1].wait_recv()
            part += out_part(other, p - 1, 0, width)
            acc[...] += part
        else:
            acc[...] = part
    sent += hs
    for j in range(S * E):
        pltpu.make_async_copy(res_rx.at[j], res_rx.at[j], res_rsem.at[j]).wait()
        res_sum[j * nt : (j + 1) * nt, :] = res_rx[j]
    hots[e] = res_sum[:, width:].astype(b16)
    hot_copies = [
        remote(hots.at[e], hots.at[e], hot_sem.at[0, d - 1], hot_sem.at[1, d - 1], e_peer(d)) for d in range(1, E)
    ]
    for copy in hot_copies:
        copy.start()
    sent += hot_copies
    hs[-1].wait_recv()
    ps = [None, None]
    for i in (1, 0):
        lo, hi = cuts[i]
        acc[:, :, lo:hi] += out_part(other, pieces - 1, lo, hi)
        parts_tx[i][...] = acc[:, :, lo:hi].astype(b16)
        ps[i] = [
            remote(
                parts_tx[i].at[flipped(e, d)],
                parts_rx[i].at[d - 1],
                ps_sem.at[0, i, d - 1],
                ps_sem.at[1, i, d - 1],
                e_peer(d),
            )
            for d in range(1, E)
        ]
        for copy in ps[i]:
            copy.start()
        sent += ps[i]

    def chunk_at(d):
        return flipped(r, d) * S + s

    def group_at(d):
        return flipped(e, d)

    first = [None, None]
    for i in (1, 0):
        lo, hi = cuts[i]
        attended = acc[e, :, lo:hi]
        for d in range(1, E):
            ps[i][d - 1].wait_recv()
            attended += parts_rx[i][d - 1].astype(f32)
        xs[i][mine, e] = (res_sum[:, lo:hi] + attended.astype(b16).astype(f32)).astype(b16)
        block = xs[i].at[mine, e]
        first[i] = [
            remote(block, block, first_sem.at[0, i, d - 1], first_sem.at[1, i, d - 1], (e_peer if i else z_peer)(d))
            for d in range(1, E if i else R)
        ]
        for copy in first[i]:
            copy.start()
        sent += first[i]
    second = [[], []]
    for hop in range(max(R, E)):
        for i in (1, 0):
            if hop >= (E if i else R):
                continue
            if hop:
                first[i][hop - 1].wait_recv()
            block = xs[i].at[mine, group_at(hop)] if i else xs[i].at[chunk_at(hop), e]
            row = [
                remote(
                    block,
                    block,
                    second_sem.at[0, i, hop, d - 1],
                    second_sem.at[1, i, hop, d - 1],
                    (z_peer if i else e_peer)(d),
                )
                for d in range(1, R if i else E)
            ]
            for copy in row:
                copy.start()
            second[i].append(row)
            sent += row
    for load in loads[3:6]:
        load.wait()

    tokens = E * drafts

    def expert_part(state, chunk, i):
        squares, gate, up, logits = state
        lo, hi = cuts[i]
        hid = xs[i][chunk].reshape(tokens, hi - lo).astype(f32)
        cols = pl.ds(pl.multiple_of(chunk * width + lo, 128), hi - lo)
        scaled = (hid * gains[:, cols]).astype(b16)
        return (
            squares + jnp.sum(hid * hid, -1, keepdims=True),
            gate + jnp.dot(scaled, wg_v[cols, :], preferred_element_type=f32),
            up + jnp.dot(scaled, wu_v[cols, :], preferred_element_type=f32),
            logits + lax.dot_general(scaled, rt_v[:, cols], (((1,), (1,)), ((), ())), preferred_element_type=f32),
        )

    state = (
        jnp.zeros((tokens, 1), f32),
        jnp.zeros((tokens, wg_v.shape[1]), f32),
        jnp.zeros((tokens, wg_v.shape[1]), f32),
        jnp.zeros((tokens, rt_v.shape[0]), f32),
    )
    across = []

    def arrived(state, d):
        for i in (0, 1):
            across[2 * d + i].wait_recv()
            state = expert_part(state, flipped(r, d) * S + other, i)
        return state

    for d in range(R):
        for i in (0, 1):
            if i == 0:
                waits = second[0][d]
            elif d == 0:
                waits = []
            else:
                waits = [row[d - 1] for row in second[1]]
            for copy in waits:
                copy.wait_recv()
            whole = xs[i].at[chunk_at(d)]
            copy = remote(whole, whole, across_sem.at[0, i, d], across_sem.at[1, i, d], sibling)
            copy.start()
            across.append(copy)
            state = expert_part(state, chunk_at(d), i)
        if d:
            state = arrived(state, d - 1)
    state = arrived(state, R - 1)
    sent += across
    squares, gate, up, logits = state
    scale = lax.rsqrt(squares / (chunks * width) + 1e-06)
    experts = rt_v.shape[0]
    for copy in hot_copies:
        copy.wait_recv()
    chosen = hots[...].reshape(tokens, 128)[:, :experts].astype(f32) * jax.nn.sigmoid(logits * scale)
    this_expert = lax.broadcasted_iota(jnp.int32, (1, experts), 1) == r
    weight = jnp.sum(jnp.where(this_expert, chosen, 0.0), -1, keepdims=True)
    weight = weight / jnp.sum(chosen, -1, keepdims=True) * 2.5
    activated = (jax.nn.silu(gate * scale) * (up * scale) * weight).astype(b16)

    to_row = lax.broadcasted_iota(jnp.int32, (tokens, tokens), 0)
    from_row = lax.broadcasted_iota(jnp.int32, (tokens, tokens), 1)
    owner = to_row % devices
    wanted = ((owner % R) * (S * E) + owner // R) * nt + to_row // devices
    ordered = jnp.dot((wanted == from_row).astype(b16), activated, preferred_element_type=f32).astype(b16)
    loads[6].wait()
    per_owner = nt * chunks
    groups = column_groups(width)
    order = [len(groups) - 1] + list(range(len(groups) - 1))
    half_rows = R * E * per_owner

    def summed(side, lo, hi):
        at = pl.ds(pl.multiple_of(side * half_rows, half_rows), half_rows)
        part = jnp.concatenate([ys[k, at, :] for k in range(lo // 128, hi // 128)], axis=1)
        return part.reshape(E, R, per_owner, hi - lo)

    with_core, mid, end = {}, {}, {}

    def peers_of(g):
        return (z_peer, r, R, e_peer, e, E) if g == len(groups) - 1 else (e_peer, e, E, z_peer, r, R)

    def begin(g):
        lo, hi = groups[g]
        for c in range(chunks):
            down = jnp.dot(ordered, wd_v[:, c * width + lo : c * width + hi], preferred_element_type=f32)
            for t in range(nt):
                part = down[t * devices : (t + 1) * devices]
                for k in range(lo // 128, hi // 128):
                    column = part[:, k * 128 - lo : (k + 1) * 128 - lo]
                    ys[k, pl.ds(c * nt + t, devices, stride=per_owner), :] = column
        y_tx[g][...] = summed(other, lo, hi).astype(b16)
        with_core[g] = remote(y_tx[g], y_rx[g], ys_sem.at[0, g], ys_sem.at[1, g], sibling)
        with_core[g].start()

    def middle(g):
        lo, hi = groups[g]
        peer, me, count = peers_of(g)[:3]
        with_core[g].wait_recv()
        both[g][...] = summed(s, lo, hi) + y_rx[g][...].astype(f32)
        mid[g] = []
        for d in range(1, count):
            to = flipped(me, d)
            block = both[g][:, to] if g == len(groups) - 1 else both[g][to]
            mid_tx[g][d - 1] = block.astype(b16)
            copy = remote(
                mid_tx[g].at[d - 1], mid_rx[g].at[d - 1], mid_sem.at[0, g, d - 1], mid_sem.at[1, g, d - 1], peer(d)
            )
            copy.start()
            mid[g].append(copy)

    for n, g in enumerate(order):
        begin(g)
        if n:
            middle(order[n - 1])
    middle(order[-1])
    for g in order:
        peer, me, count = peers_of(g)[3:]
        total_g = both[g][:, r] if g == len(groups) - 1 else both[g][e]
        for d, copy in enumerate(mid[g]):
            copy.wait_recv()
            total_g += mid_rx[g][d].astype(f32)
        mid_sum[g][...] = total_g
        end_tx[g][...] = total_g.astype(b16)
        end[g] = []
        for d in range(1, count):
            to = flipped(me, d)
            copy = remote(
                end_tx[g].at[to], end_rx[g].at[d - 1], end_sem.at[0, g, d - 1], end_sem.at[1, g, d - 1], peer(d)
            )
            copy.start()
            end[g].append(copy)
        sent += [with_core[g]] + mid[g] + end[g]
    pick = lax.broadcasted_iota(jnp.int32, (8, tokens), 0) + (mine * E + e) * nt
    pick = (pick == lax.broadcasted_iota(jnp.int32, (8, tokens), 1)).astype(b16)
    own = []
    for c in range(chunks):
        sides = [
            jnp.dot(pick, xs[i][c].reshape(tokens, hi - lo), preferred_element_type=f32)
            for i, (lo, hi) in enumerate(cuts)
        ]
        own.append(jnp.concatenate(sides, axis=1))
    for g in order:
        lo, hi = groups[g]
        routed = mid_sum[g][peers_of(g)[4]]
        for d, copy in enumerate(end[g]):
            copy.wait_recv()
            routed += end_rx[g][d].astype(f32)
        for c in range(chunks):
            value = own[c][:nt, lo:hi] + routed[c * nt : (c + 1) * nt]
            out_ref[:, c * width + lo : c * width + hi] = value.astype(b16)

    for copy in sent:
        copy.wait_send()
    for c in range(chunks):
        here = (r == c // S) & (s == c % S) & (e == r)

        @pl.when(jnp.logical_not(here))
        def _():
            remote(res_tx.at[c], res_rx.at[slot], res_ssem.at[c], res_rsem.at[slot], (c // S, c % S, r)).wait_send()


def fused(
    dims, residual, queries, cache, blocks, lengths, value_up, out_proj, gain, router, ids, w_gate, w_up, w_down
):
    R, S, E = dims
    f32, b16 = jnp.float32, jnp.bfloat16
    drafts, heads, qk = queries.shape
    half_heads = heads // S
    width = out_proj.shape[1]
    nt, model = residual.shape
    keys_len = cache.shape[0]
    chunks = R * S
    lanes = -(-keys_len // 128) * 128
    ff = w_gate.shape[1]
    per_owner = nt * chunks
    cuts, groups = column_cuts(width), column_groups(width)
    pieces = 4
    dma = pltpu.SemaphoreType.DMA
    vmem, smem, hbm = (pl.BlockSpec(memory_space=m) for m in (pltpu.VMEM, pltpu.SMEM, pl.ANY))
    scratch = [
        pltpu.VMEM((drafts, half_heads, qk), b16),
        pltpu.VMEM((half_heads,) + value_up.shape[1:], b16),
        pltpu.VMEM(out_proj.shape, b16),
        pltpu.VMEM(router.shape, b16),
        pltpu.VMEM(w_gate.shape, b16),
        pltpu.VMEM(w_up.shape, b16),
        pltpu.VMEM(w_down.shape, b16),
        pltpu.VMEM(cache.shape, b16),
        pltpu.VMEM(cache.shape, b16),
        pltpu.VMEM((2, 8, lanes), f32),
        pltpu.VMEM((chunks, nt, width + 128), f32),
        pltpu.VMEM((S * E, nt, width + 128), f32),
        pltpu.VMEM((1, model), f32),
        pltpu.VMEM((DL // 128, drafts * half_heads, 128), f32),
        pltpu.VMEM((S, pieces, R, drafts, half_heads // pieces * DV), b16),
        pltpu.VMEM((E, drafts, width), f32),
        pltpu.VMEM((drafts, width + 128), f32),
        pltpu.VMEM((E, drafts, 128), b16),
        pltpu.VMEM((width // 128, R * S * E * per_owner, 128), f32),
        [pltpu.VMEM((E, drafts, hi - lo), b16) for lo, hi in cuts],
        [pltpu.VMEM((E - 1, drafts, hi - lo), b16) for lo, hi in cuts],
        [pltpu.VMEM((chunks, E, drafts, hi - lo), b16) for lo, hi in cuts],
        [pltpu.VMEM((E, R, per_owner, hi - lo), b16) for lo, hi in groups],
        [pltpu.VMEM((E, R, per_owner, hi - lo), b16) for lo, hi in groups],
        [pltpu.VMEM((E, R, per_owner, hi - lo), f32) for lo, hi in groups],
        [pltpu.VMEM((E - 1, R, per_owner, hi - lo), b16) for lo, hi in groups],
        [pltpu.VMEM((E - 1, R, per_owner, hi - lo), b16) for lo, hi in groups],
        [pltpu.VMEM((R, per_owner, hi - lo), f32) for lo, hi in groups],
        [pltpu.VMEM((R, per_owner, hi - lo), b16) for lo, hi in groups],
        [pltpu.VMEM((R - 1, per_owner, hi - lo), b16) for lo, hi in groups],
        dma((8,)),
        dma((2,)),
        dma((2,)),
        dma((chunks,)),
        dma((S * E,)),
        dma((2, pieces, R - 1)),
        dma((2, pieces)),
        dma((2, E - 1)),
        dma((2, 2, E - 1)),
        dma((2, 2, R - 1)),
        dma((2, 2, R, E - 1)),
        dma((2, 2, R)),
        dma((2, len(groups))),
        dma((2, len(groups), E - 1)),
        dma((2, len(groups), E - 1)),
    ]
    return pl.pallas_call(
        functools.partial(fused_kernel, dims),
        out_shape=jax.ShapeDtypeStruct((nt, model), b16),
        in_specs=[vmem, hbm, hbm, smem, smem, hbm, hbm, vmem, hbm, smem, hbm, hbm, hbm],
        out_specs=vmem,
        scratch_shapes=scratch,
        compiler_params=pltpu.CompilerParams(
            collective_id=0, has_side_effects=True, vmem_limit_bytes=56 * 1024 * 1024
        ),
        cost_estimate=pl.CostEstimate(
            flops=2 * R * drafts * (out_proj.size + 3 * w_gate.size),
            bytes_accessed=2 * (value_up.size + out_proj.size + 3 * w_gate.size),
            transcendentals=0,
        ),
    )(residual, queries, cache, blocks, lengths, value_up, out_proj, gain, router, ids, w_gate, w_up, w_down)


def per_device_fused(dims, *args):
    (residual, queries, cache, blocks, lengths, value_up, out_proj, gain, router, ids, w_gate, w_up, w_down) = args
    return fused(
        dims,
        residual,
        queries[0],
        cache[0],
        blocks[0, 0],
        lengths,
        value_up,
        out_proj,
        gain,
        router.T,
        ids,
        w_gate[0],
        w_up[0],
        w_down[0],
    )


def fits_fused(dims, shapes):
    R, S, E = dims
    residual, queries, cache, router = shapes[0], shapes[1], shapes[2], shapes[8]
    drafts, heads, model = queries[1], queries[2], residual[1]
    return (
        S == 2
        and R == E
        and R & (R - 1) == 0
        and queries[0] == R
        and router[1] == R
        and drafts % 16 == 0
        and residual[0] == R * drafts
        and heads % (E * S * 16) == 0
        and model % (R * S * 128) == 0
        and model // (R * S) >= 384
        and (residual[0] // E) % 16 == 0
        and (drafts // (S * E) * R * S) % 16 == 0
        and cache[1] // S % BLOCK == 0
    )


def solution(mesh):
    in_specs = (
        P(("req", "seq", "exp"), None),
        P("req", None, "exp", None),
        P("req", "seq", None),
        P("req", "seq", None),
        P("req"),
        P("exp", None, None),
        P("exp", ("req", "seq")),
        P(),
        P(),
        P(("req", "seq", "exp"), None),
        P("req", None, ("seq", "exp")),
        P("req", None, ("seq", "exp")),
        P("req", ("seq", "exp"), None),
    )
    out_specs = P(("req", "seq", "exp"), None)
    dims = (mesh.shape["req"], mesh.shape["seq"], mesh.shape["exp"])

    def layer(*args):
        fast = fits_fused(dims, [a.shape for a in args])
        body = functools.partial(per_device_fused, dims) if fast else per_device
        return jax.shard_map(body, mesh=mesh, in_specs=in_specs, out_specs=out_specs, check_vma=False)(*args)

    return layer
```

```python
import functools

import jax
import jax.numpy as jnp
from jax import lax
from jax.experimental import pallas as pl
from jax.experimental.pallas import tpu as pltpu
from jax.sharding import PartitionSpec as P

DL = 512
DR = 64
DV = 128
BLOCK = 64


def merge_parts(former, latter):
    row_max = jnp.maximum(former[0], latter[0])
    left_scale = jnp.exp(former[0] - row_max)
    right_scale = jnp.exp(latter[0] - row_max)
    return (
        row_max,
        left_scale * former[1] + right_scale * latter[1],
        left_scale[..., None] * former[2] + right_scale[..., None] * latter[2],
    )


def pick_rows(block_rows, picks):
    return block_rows[picks]


def shard_softmax(queries, picked, usable):
    scores = jnp.einsum("bqhk,bjk->bqhj", queries, picked, preferred_element_type=jnp.float32) * (
        DV + DR
    ) ** (-0.5)
    row_max = jnp.max(jnp.where(usable, scores, -1e30), axis=-1)
    weights = jnp.where(usable, jnp.exp(scores - row_max[..., None]), 0.0).astype(jnp.bfloat16)
    row_sum = jnp.sum(weights.astype(jnp.float32), -1)
    weighted = jnp.einsum(
        "bqhj,bjd->bqhd", weights, picked[..., :DL], preferred_element_type=jnp.float32
    )
    return (row_max, row_sum, weighted)


def expert_rows(arrived, w_gate, w_up, w_down):
    model_width = w_gate.shape[1]
    flat_rows = arrived.reshape(-1, model_width)
    gate_act = jnp.dot(flat_rows, w_gate[0], preferred_element_type=jnp.float32)
    up_act = jnp.dot(flat_rows, w_up[0], preferred_element_type=jnp.float32)
    activated = (jax.nn.silu(gate_act) * up_act).astype(jnp.bfloat16)
    partial_value = jnp.dot(activated, w_down[0], preferred_element_type=jnp.float32).astype(
        jnp.bfloat16
    )
    return partial_value.reshape(arrived.shape)


def per_device(
    residual,
    queries,
    latent_cache,
    blocks,
    lengths,
    value_up,
    out_proj,
    norm_gain,
    router,
    expert_ids,
    w_gate,
    w_up,
    w_down,
):
    local_reqs, drafts, head_count, qk_width = queries.shape
    shard_len = latent_cache.shape[1]
    picks_count = blocks.shape[2]
    seq_index = lax.axis_index("seq")
    block_view = latent_cache.reshape(local_reqs, shard_len // BLOCK, BLOCK, qk_width)
    picked = jax.vmap(pick_rows)(block_view, blocks[:, 0]).reshape(
        local_reqs, picks_count * BLOCK, qk_width
    )
    positions = (
        seq_index * shard_len + blocks[:, 0, :, None] * BLOCK + jnp.arange(BLOCK, dtype=jnp.int32)
    )
    positions = positions.reshape(local_reqs, picks_count * BLOCK)
    limits = lengths[:, None] - (drafts - 1) + jnp.arange(drafts, dtype=jnp.int32)[None, :]
    usable = positions[:, None, None, :] < limits[:, :, None, None]
    usable_mark = usable[:, :, 0, :].astype(jnp.bfloat16)
    all_keys, all_marks = (
        lax.all_gather(picked[None], "seq", axis=0, tiled=True),
        lax.all_gather(usable_mark[None], "seq", axis=0, tiled=True),
    )
    combined = None
    for shard in range(lax.axis_size("seq")):
        shard_usable = (all_marks[shard] > 0)[:, :, None, :]
        partial_value = shard_softmax(queries, all_keys[shard], shard_usable)
        combined = partial_value if combined is None else merge_parts(combined, partial_value)
    latent = (combined[2] / combined[1][..., None]).astype(jnp.bfloat16)
    head_values = jnp.einsum(
        "bqhd,hdv->bqhv", latent, value_up, preferred_element_type=jnp.float32
    ).astype(jnp.bfloat16)
    flat_values = head_values.reshape(local_reqs * drafts, head_count * DV)
    col_terms = jnp.dot(
        lax.all_gather(flat_values, "req", axis=0, tiled=True),
        out_proj,
        preferred_element_type=jnp.float32,
    )
    token_terms = lax.all_to_all(
        col_terms[None].astype(jnp.bfloat16),
        ("req", "seq", "exp"),
        split_axis=1,
        concat_axis=0,
        tiled=True,
    ).astype(jnp.float32)
    exp_count = lax.axis_size("exp")
    col_blocks = token_terms.shape[0] // exp_count
    rows_here = token_terms.shape[1]
    col_sums = jnp.sum(
        token_terms.reshape(col_blocks, exp_count, rows_here, token_terms.shape[2]), 1
    )
    attended = jnp.transpose(col_sums, (1, 0, 2)).reshape(rows_here, -1).astype(jnp.bfloat16)
    hidden_sum = (residual.astype(jnp.float32) + attended.astype(jnp.float32)).astype(jnp.bfloat16)
    hidden32 = hidden_sum.astype(jnp.float32)
    normed = (
        hidden32
        * lax.rsqrt(jnp.mean(hidden32 * hidden32, -1, keepdims=True) + 1e-06)
        * norm_gain.astype(jnp.float32)
    ).astype(jnp.bfloat16)
    gate_probs = jax.nn.sigmoid(jnp.dot(normed, router, preferred_element_type=jnp.float32))
    expert_count = router.shape[1]
    top_count = expert_ids.shape[1]
    one_hot = (expert_ids[:, :, None] == jnp.arange(expert_count, dtype=jnp.int32)).astype(
        jnp.int32
    )
    pair_hot = one_hot.reshape(rows_here * top_count, expert_count)
    slot_index = jnp.sum((jnp.cumsum(pair_hot, 0) - pair_hot) * pair_hot, -1)
    slot_hot = (slot_index[:, None] == jnp.arange(rows_here, dtype=jnp.int32)).astype(jnp.int32)
    placement = (pair_hot[:, :, None] * slot_hot[:, None, :]).reshape(
        rows_here, top_count, expert_count * rows_here
    )
    chosen = jnp.sum(one_hot.astype(jnp.float32) * gate_probs[:, None, :], -1)
    gate_weights = chosen / jnp.sum(chosen, -1, keepdims=True) * 2.5
    dispatch = jnp.sum(placement, 1).astype(jnp.bfloat16)
    outgoing = jnp.dot(dispatch.T, normed, preferred_element_type=jnp.float32).astype(jnp.bfloat16)
    outgoing = outgoing.reshape(expert_count, rows_here, outgoing.shape[1])
    combine = jnp.sum(gate_weights[:, :, None] * placement.astype(jnp.float32), 1)
    copies = lax.axis_size("seq") * exp_count
    fanned = jnp.broadcast_to(outgoing[:, None], (expert_count, copies) + outgoing.shape[1:])
    fanned = fanned.reshape((expert_count * copies,) + outgoing.shape[1:])
    returned = lax.all_to_all(
        expert_rows(
            lax.all_to_all(fanned, ("req", "seq", "exp"), split_axis=0, concat_axis=0, tiled=True),
            w_gate,
            w_up,
            w_down,
        ),
        ("req", "seq", "exp"),
        split_axis=0,
        concat_axis=0,
        tiled=True,
    )
    returned = returned.reshape((expert_count, copies) + outgoing.shape[1:]).astype(jnp.float32)
    expert_out = jnp.sum(returned, 1).astype(jnp.bfloat16)
    slot_rows = expert_out.reshape(expert_count * rows_here, expert_out.shape[2]).astype(
        jnp.float32
    )
    routed = jnp.dot(combine, slot_rows, precision=lax.Precision.HIGHEST)
    return (hidden32 + routed).astype(jnp.bfloat16)


MESH = pl.DeviceIdType.MESH


def column_cuts(width):
    return [(0, width - 256), (width - 256, width)]


def column_groups(width):
    cuts = column_cuts(width)
    return [(lo, min(lo + 256, cuts[0][1])) for lo in range(0, cuts[0][1], 256)] + cuts[1:]


def fused_kernel(
    dims,
    residual_ref,
    queries_hbm,
    cache_ref,
    blocks_ref,
    lengths_ref,
    value_up_hbm,
    out_proj_hbm,
    gain_ref,
    router_hbm,
    ids_ref,
    w_gate_hbm,
    w_up_hbm,
    w_down_hbm,
    out_ref,
    q_v,
    vu_v,
    op_v,
    rt_v,
    wg_v,
    wu_v,
    wd_v,
    keys_rx,
    marks,
    res_tx,
    res_rx,
    gains,
    squares,
    gate_up,
    logits,
    lat,
    hv,
    acc,
    res_sum,
    hots,
    ys,
    parts_tx,
    parts_rx,
    xs,
    y_tx,
    y_rx,
    both,
    mid_tx,
    mid_rx,
    mid_sum,
    end_tx,
    end_rx,
    load_sem,
    key_sem,
    mark_sem,
    res_ssem,
    res_rsem,
    hz_sem,
    hs_sem,
    hot_sem,
    ps_sem,
    first_sem,
    second_sem,
    across_sem,
    ys_sem,
    mid_sem,
    end_sem,
):
    R, S, E = dims
    f32, b16 = jnp.float32, jnp.bfloat16
    r, s, e = lax.axis_index("req"), lax.axis_index("seq"), lax.axis_index("exp")
    other = 1 - s
    sibling = (r, other, e)
    drafts, half_heads, _ = q_v.shape
    keys_len = cache_ref.shape[0]
    width = op_v.shape[1]
    chunks = R * S
    nt = residual_ref.shape[0]
    devices = R * S * E
    mine = r * S + s
    at_home = (e == r).astype(jnp.int32)

    head_from = pl.multiple_of(s * half_heads, half_heads)
    loads = [
        pltpu.make_async_copy(queries_hbm.at[:, pl.ds(head_from, half_heads), :], q_v, load_sem.at[0]),
        pltpu.make_async_copy(value_up_hbm.at[pl.ds(head_from, half_heads)], vu_v, load_sem.at[1]),
        pltpu.make_async_copy(out_proj_hbm, op_v, load_sem.at[2]),
        pltpu.make_async_copy(router_hbm, rt_v, load_sem.at[3]),
        pltpu.make_async_copy(w_gate_hbm, wg_v, load_sem.at[4]),
        pltpu.make_async_copy(w_up_hbm, wu_v, load_sem.at[5]),
        pltpu.make_async_copy(w_down_hbm, wd_v, load_sem.at[6]),
    ]
    for load in loads:
        load.start()

    def z_peer(d):
        return (lax.rem(r + d, R), s, e)

    def e_peer(d):
        return (r, s, lax.rem(e + d, E))

    barrier = pltpu.get_barrier_semaphore()
    for peer in [sibling] + [z_peer(d) for d in range(1, R)] + [e_peer(d) for d in range(1, E)]:
        pl.semaphore_signal(barrier, inc=1, device_id=peer, device_id_type=MESH)
    for ss in range(S):
        for ee in range(E):

            @pl.when(jnp.logical_not((e == r) & (s == ss) & (e == ee)))
            def _():
                pl.semaphore_signal(barrier, inc=1, device_id=(e, ss, ee), device_id_type=MESH)

    gains[...] = gain_ref[...].astype(f32).reshape(gains.shape)
    block_of = lax.broadcasted_iota(jnp.int32, marks.shape[1:], 1) // BLOCK
    hit = block_of == blocks_ref[0]
    for i in range(1, blocks_ref.shape[0]):
        hit = hit | (block_of == blocks_ref[i])
    marks[0] = hit.astype(f32)
    lane = lax.broadcasted_iota(jnp.int32, (1, 128), 1)
    for t in range(nt):
        hot = lane == ids_ref[t, 0]
        for k in range(1, ids_ref.shape[1]):
            hot = hot | (lane == ids_ref[t, k])
        for c in range(chunks):
            res_tx[c, t : t + 1, width:] = hot.astype(f32)
    for c in range(chunks):
        res_tx[c, :, :width] = residual_ref[:, c * width : (c + 1) * width].astype(f32)

    pl.semaphore_wait(barrier, 1 + (R - 1) + (E - 1) + S * E - at_home)

    def remote(src, dst, ssem, rsem, peer):
        return pltpu.make_async_remote_copy(
            src_ref=src, dst_ref=dst, send_sem=ssem, recv_sem=rsem, device_id=peer, device_id_type=MESH
        )

    sent = []
    key_copy = remote(cache_ref, keys_rx, key_sem.at[0], key_sem.at[1], sibling)
    mark_copy = remote(marks.at[0], marks.at[1], mark_sem.at[0], mark_sem.at[1], sibling)
    key_copy.start()
    mark_copy.start()
    sent += [key_copy, mark_copy]
    slot = s * E + e
    for c in range(chunks):
        to = (c // S, c % S, r)
        here = (r == c // S) & (s == c % S) & (e == r)

        @pl.when(jnp.logical_not(here))
        def _():
            remote(res_tx.at[c], res_rx.at[slot], res_ssem.at[c], res_rsem.at[slot], to).start()

        @pl.when(here)
        def _():
            pltpu.make_async_copy(res_tx.at[c], res_rx.at[slot], res_rsem.at[slot]).start()

    loads[0].wait()
    q2 = q_v[...].reshape(drafts * half_heads, q_v.shape[2])
    rows = drafts * half_heads
    limit = lengths_ref[0] - (drafts - 1) + lax.broadcasted_iota(jnp.int32, (rows, 1), 0) // half_heads

    def scores_of(keys, mark, shard):
        sc = lax.dot_general(q2, keys, (((1,), (1,)), ((), ())), preferred_element_type=f32)
        pos = shard * keys_len + lax.broadcasted_iota(jnp.int32, (rows, keys_len), 1)
        usable = (pos < limit) & (mark > 0)
        return jnp.where(usable, sc * (DV + DR) ** (-0.5), -1e30), usable

    near, near_ok = scores_of(cache_ref[...], marks[0, :1, :keys_len], s)
    key_copy.wait_recv()
    mark_copy.wait_recv()
    far, far_ok = scores_of(keys_rx[...], marks[1, :1, :keys_len], other)
    top = jnp.maximum(jnp.max(near, -1, keepdims=True), jnp.max(far, -1, keepdims=True))
    near_p = jnp.where(near_ok, jnp.exp(near - top), 0.0).astype(b16)
    far_p = jnp.where(far_ok, jnp.exp(far - top), 0.0).astype(b16)
    total = jnp.sum(near_p.astype(f32), -1, keepdims=True) + jnp.sum(far_p.astype(f32), -1, keepdims=True)
    weighted = jnp.dot(near_p, cache_ref[:, :DL], preferred_element_type=f32)
    weighted += jnp.dot(far_p, keys_rx[:, :DL], preferred_element_type=f32)
    latent = weighted / total
    for k in range(lat.shape[0]):
        lat[k] = latent[:, k * 128 : (k + 1) * 128]

    pieces = hv.shape[1]
    piece_heads = half_heads // pieces
    depth = piece_heads * DV
    loads[1].wait()

    def hz_copy(p, d):
        block = hv.at[s, p, r]
        return remote(block, block, hz_sem.at[0, p, d - 1], hz_sem.at[1, p, d - 1], z_peer(d))

    def hs_copy(p):
        whole = hv.at[s, p]
        return remote(whole, whole, hs_sem.at[0, p], hs_sem.at[1, p], sibling)

    @pl.loop(0, pieces)
    def _(p):
        for n in range(piece_heads):
            h = p * piece_heads + n
            one = [lat[k, pl.ds(h, drafts, stride=half_heads), :] for k in range(lat.shape[0])]
            one = jnp.concatenate(one, axis=1).astype(b16)
            value = jnp.dot(one, vu_v[h], preferred_element_type=f32)
            hv[s, p, r, :, n * DV : (n + 1) * DV] = value.astype(b16)
        for d in range(1, R):
            hz_copy(p, d).start()

    sent += [hz_copy(p, d) for p in range(pieces) for d in range(1, R)] + [hs_copy(p) for p in range(pieces)]

    cuts = column_cuts(width)
    loads[2].wait()
    acc[...] = jnp.zeros_like(acc)

    @pl.loop(0, 2 * pieces)
    def _(step):
        p = step // 2
        near_turn = step % 2 == 0

        @pl.when(near_turn)
        def _():
            for d in range(1, R):
                hz_copy(p, d).wait_recv()
            hs_copy(p).start()

        @pl.when(jnp.logical_not(near_turn))
        def _():
            hs_copy(p).wait_recv()

        side = lax.rem(s + step, 2)
        head_rows = hv[side, p].reshape(R * drafts, depth)
        at = pl.ds(pl.multiple_of((side * pieces + p) * depth, depth), depth)
        part = jnp.dot(head_rows, op_v[at, :], preferred_element_type=f32)
        acc[...] += part.reshape(E, drafts, width)

    for j in range(S * E):
        pltpu.make_async_copy(res_rx.at[j], res_rx.at[j], res_rsem.at[j]).wait()
        res_sum[j * nt : (j + 1) * nt, :] = res_rx[j]
    hots[e] = res_sum[:, width:].astype(b16)
    hot_copies = [
        remote(hots.at[e], hots.at[e], hot_sem.at[0, d - 1], hot_sem.at[1, d - 1], e_peer(d)) for d in range(1, E)
    ]
    for copy in hot_copies:
        copy.start()
    sent += hot_copies
    ps = [None, None]
    for i in (1, 0):
        lo, hi = cuts[i]
        parts_tx[i][...] = acc[:, :, lo:hi].astype(b16)
        ps[i] = [
            remote(
                parts_tx[i].at[lax.rem(e + d, E)],
                parts_rx[i].at[d - 1],
                ps_sem.at[0, i, d - 1],
                ps_sem.at[1, i, d - 1],
                e_peer(d),
            )
            for d in range(1, E)
        ]
        for copy in ps[i]:
            copy.start()
        sent += ps[i]

    def chunk_at(d):
        return lax.rem(r + R - d, R) * S + s

    def group_at(d):
        return lax.rem(e + E - d, E)

    first = [None, None]
    for i in (1, 0):
        lo, hi = cuts[i]
        attended = acc[e, :, lo:hi]
        for d in range(1, E):
            ps[i][d - 1].wait_recv()
            attended += parts_rx[i][d - 1].astype(f32)
        xs[i][mine, e] = (res_sum[:, lo:hi] + attended.astype(b16).astype(f32)).astype(b16)
        block = xs[i].at[mine, e]
        first[i] = [
            remote(block, block, first_sem.at[0, i, d - 1], first_sem.at[1, i, d - 1], (e_peer if i else z_peer)(d))
            for d in range(1, E if i else R)
        ]
        for copy in first[i]:
            copy.start()
        sent += first[i]
    second = [[], []]
    for hop in range(max(R, E)):
        for i in (1, 0):
            if hop >= (E if i else R):
                continue
            if hop:
                first[i][hop - 1].wait_recv()
            block = xs[i].at[mine, group_at(hop)] if i else xs[i].at[chunk_at(hop), e]
            row = [
                remote(
                    block,
                    block,
                    second_sem.at[0, i, hop, d - 1],
                    second_sem.at[1, i, hop, d - 1],
                    (z_peer if i else e_peer)(d),
                )
                for d in range(1, R if i else E)
            ]
            for copy in row:
                copy.start()
            second[i].append(row)
            sent += row
    for load in loads[3:6]:
        load.wait()

    tokens = E * drafts
    squares[...] = jnp.zeros_like(squares)
    gate_up[...] = jnp.zeros_like(gate_up)
    logits[...] = jnp.zeros_like(logits)

    def second_copy(i, hop, d):
        block = xs[i].at[mine, group_at(hop)] if i else xs[i].at[chunk_at(hop), e]
        peer = (z_peer if i else e_peer)(d)
        return remote(block, block, second_sem.at[0, i, hop, d - 1], second_sem.at[1, i, hop, d - 1], peer)

    def across_copy(i, hop):
        whole = xs[i].at[chunk_at(hop)]
        return remote(whole, whole, across_sem.at[0, i, hop], across_sem.at[1, i, hop], sibling)

    @pl.loop(0, 2 * R)
    def _(step):
        hop = step // 2
        near_turn = step % 2 == 0

        @pl.when(near_turn)
        def _():
            for d in range(1, E):
                second_copy(0, hop, d).wait_recv()
            across_copy(0, hop).start()

            @pl.when(hop > 0)
            def _():
                for n in range(E):
                    second_copy(1, n, hop).wait_recv()

            across_copy(1, hop).start()

        @pl.when(jnp.logical_not(near_turn))
        def _():
            for i in (0, 1):
                across_copy(i, hop).wait_recv()

        chunk = lax.rem(r + R - hop, R) * S + lax.rem(s + step, 2)
        for i in (0, 1):
            lo, hi = cuts[i]
            hid = xs[i][chunk].reshape(tokens, hi - lo).astype(f32)
            cols = pl.ds(pl.multiple_of(chunk * width + lo, 128), hi - lo)
            scaled = (hid * gains[:, cols]).astype(b16)
            squares[...] += jnp.sum(hid * hid, -1, keepdims=True)
            gate_up[0] += jnp.dot(scaled, wg_v[cols, :], preferred_element_type=f32)
            gate_up[1] += jnp.dot(scaled, wu_v[cols, :], preferred_element_type=f32)
            logits[...] += lax.dot_general(
                scaled, rt_v[:, cols], (((1,), (1,)), ((), ())), preferred_element_type=f32
            )

    sent += [across_copy(i, hop) for i in (0, 1) for hop in range(R)]
    gate, up = gate_up[0], gate_up[1]
    scale = lax.rsqrt(squares[...] / (chunks * width) + 1e-06)
    experts = rt_v.shape[0]
    for copy in hot_copies:
        copy.wait_recv()
    chosen = hots[...].reshape(tokens, 128)[:, :experts].astype(f32) * jax.nn.sigmoid(logits[...] * scale)
    this_expert = lax.broadcasted_iota(jnp.int32, (1, experts), 1) == r
    weight = jnp.sum(jnp.where(this_expert, chosen, 0.0), -1, keepdims=True)
    weight = weight / jnp.sum(chosen, -1, keepdims=True) * 2.5
    activated = (jax.nn.silu(gate * scale) * (up * scale) * weight).astype(b16)

    to_row = lax.broadcasted_iota(jnp.int32, (tokens, tokens), 0)
    from_row = lax.broadcasted_iota(jnp.int32, (tokens, tokens), 1)
    owner = to_row % devices
    wanted = ((owner % R) * (S * E) + owner // R) * nt + to_row // devices
    ordered = jnp.dot((wanted == from_row).astype(b16), activated, preferred_element_type=f32).astype(b16)
    loads[6].wait()
    per_owner = nt * chunks
    groups = column_groups(width)
    order = [len(groups) - 1] + list(range(len(groups) - 1))
    half_rows = R * E * per_owner

    def summed(side, lo, hi):
        at = pl.ds(pl.multiple_of(side * half_rows, half_rows), half_rows)
        part = jnp.concatenate([ys[k, at, :] for k in range(lo // 128, hi // 128)], axis=1)
        return part.reshape(E, R, per_owner, hi - lo)

    with_core, mid, end = {}, {}, {}

    def peers_of(g):
        return (z_peer, r, R, e_peer, e, E) if g == len(groups) - 1 else (e_peer, e, E, z_peer, r, R)

    def begin(g):
        lo, hi = groups[g]
        for c in range(chunks):
            down = jnp.dot(ordered, wd_v[:, c * width + lo : c * width + hi], preferred_element_type=f32)
            for t in range(nt):
                part = down[t * devices : (t + 1) * devices]
                for k in range(lo // 128, hi // 128):
                    column = part[:, k * 128 - lo : (k + 1) * 128 - lo]
                    ys[k, pl.ds(c * nt + t, devices, stride=per_owner), :] = column
        y_tx[g][...] = summed(other, lo, hi).astype(b16)
        with_core[g] = remote(y_tx[g], y_rx[g], ys_sem.at[0, g], ys_sem.at[1, g], sibling)
        with_core[g].start()

    def middle(g):
        lo, hi = groups[g]
        peer, me, count = peers_of(g)[:3]
        with_core[g].wait_recv()
        both[g][...] = summed(s, lo, hi) + y_rx[g][...].astype(f32)
        mid[g] = []
        for d in range(1, count):
            to = lax.rem(me + d, count)
            block = both[g][:, to] if g == len(groups) - 1 else both[g][to]
            mid_tx[g][d - 1] = block.astype(b16)
            copy = remote(
                mid_tx[g].at[d - 1], mid_rx[g].at[d - 1], mid_sem.at[0, g, d - 1], mid_sem.at[1, g, d - 1], peer(d)
            )
            copy.start()
            mid[g].append(copy)

    for n, g in enumerate(order):
        begin(g)
        if n:
            middle(order[n - 1])
    middle(order[-1])
    for g in order:
        peer, me, count = peers_of(g)[3:]
        total_g = both[g][:, r] if g == len(groups) - 1 else both[g][e]
        for d, copy in enumerate(mid[g]):
            copy.wait_recv()
            total_g += mid_rx[g][d].astype(f32)
        mid_sum[g][...] = total_g
        end_tx[g][...] = total_g.astype(b16)
        end[g] = []
        for d in range(1, count):
            to = lax.rem(me + d, count)
            copy = remote(
                end_tx[g].at[to], end_rx[g].at[d - 1], end_sem.at[0, g, d - 1], end_sem.at[1, g, d - 1], peer(d)
            )
            copy.start()
            end[g].append(copy)
        sent += [with_core[g]] + mid[g] + end[g]
    pick = lax.broadcasted_iota(jnp.int32, (8, tokens), 0) + (mine * E + e) * nt
    pick = (pick == lax.broadcasted_iota(jnp.int32, (8, tokens), 1)).astype(b16)
    own = []
    for c in range(chunks):
        sides = [
            jnp.dot(pick, xs[i][c].reshape(tokens, hi - lo), preferred_element_type=f32)
            for i, (lo, hi) in enumerate(cuts)
        ]
        own.append(jnp.concatenate(sides, axis=1))
    for g in order:
        lo, hi = groups[g]
        routed = mid_sum[g][peers_of(g)[4]]
        for d, copy in enumerate(end[g]):
            copy.wait_recv()
            routed += end_rx[g][d].astype(f32)
        for c in range(chunks):
            value = own[c][:nt, lo:hi] + routed[c * nt : (c + 1) * nt]
            out_ref[:, c * width + lo : c * width + hi] = value.astype(b16)

    for copy in sent:
        copy.wait_send()
    for c in range(chunks):
        here = (r == c // S) & (s == c % S) & (e == r)

        @pl.when(jnp.logical_not(here))
        def _():
            remote(res_tx.at[c], res_rx.at[slot], res_ssem.at[c], res_rsem.at[slot], (c // S, c % S, r)).wait_send()


def fused(
    dims, residual, queries, cache, blocks, lengths, value_up, out_proj, gain, router, ids, w_gate, w_up, w_down
):
    R, S, E = dims
    f32, b16 = jnp.float32, jnp.bfloat16
    drafts, heads, qk = queries.shape
    half_heads = heads // S
    width = out_proj.shape[1]
    nt, model = residual.shape
    keys_len = cache.shape[0]
    chunks = R * S
    lanes = -(-keys_len // 128) * 128
    ff = w_gate.shape[1]
    per_owner = nt * chunks
    cuts, groups = column_cuts(width), column_groups(width)
    pieces = 4
    dma = pltpu.SemaphoreType.DMA
    vmem, smem, hbm = (pl.BlockSpec(memory_space=m) for m in (pltpu.VMEM, pltpu.SMEM, pl.ANY))
    scratch = [
        pltpu.VMEM((drafts, half_heads, qk), b16),
        pltpu.VMEM((half_heads,) + value_up.shape[1:], b16),
        pltpu.VMEM(out_proj.shape, b16),
        pltpu.VMEM(router.shape, b16),
        pltpu.VMEM(w_gate.shape, b16),
        pltpu.VMEM(w_up.shape, b16),
        pltpu.VMEM(w_down.shape, b16),
        pltpu.VMEM(cache.shape, b16),
        pltpu.VMEM((2, 8, lanes), f32),
        pltpu.VMEM((chunks, nt, width + 128), f32),
        pltpu.VMEM((S * E, nt, width + 128), f32),
        pltpu.VMEM((1, model), f32),
        pltpu.VMEM((R * drafts, 1), f32),
        pltpu.VMEM((2, R * drafts, ff), f32),
        pltpu.VMEM((R * drafts, router.shape[0]), f32),
        pltpu.VMEM((DL // 128, drafts * half_heads, 128), f32),
        pltpu.VMEM((S, pieces, R, drafts, half_heads // pieces * DV), b16),
        pltpu.VMEM((E, drafts, width), f32),
        pltpu.VMEM((drafts, width + 128), f32),
        pltpu.VMEM((E, drafts, 128), b16),
        pltpu.VMEM((width // 128, R * S * E * per_owner, 128), f32),
        [pltpu.VMEM((E, drafts, hi - lo), b16) for lo, hi in cuts],
        [pltpu.VMEM((E - 1, drafts, hi - lo), b16) for lo, hi in cuts],
        [pltpu.VMEM((chunks, E, drafts, hi - lo), b16) for lo, hi in cuts],
        [pltpu.VMEM((E, R, per_owner, hi - lo), b16) for lo, hi in groups],
        [pltpu.VMEM((E, R, per_owner, hi - lo), b16) for lo, hi in groups],
        [pltpu.VMEM((E, R, per_owner, hi - lo), f32) for lo, hi in groups],
        [pltpu.VMEM((E - 1, R, per_owner, hi - lo), b16) for lo, hi in groups],
        [pltpu.VMEM((E - 1, R, per_owner, hi - lo), b16) for lo, hi in groups],
        [pltpu.VMEM((R, per_owner, hi - lo), f32) for lo, hi in groups],
        [pltpu.VMEM((R, per_owner, hi - lo), b16) for lo, hi in groups],
        [pltpu.VMEM((R - 1, per_owner, hi - lo), b16) for lo, hi in groups],
        dma((7,)),
        dma((2,)),
        dma((2,)),
        dma((chunks,)),
        dma((S * E,)),
        dma((2, pieces, R - 1)),
        dma((2, pieces)),
        dma((2, E - 1)),
        dma((2, 2, E - 1)),
        dma((2, 2, R - 1)),
        dma((2, 2, R, E - 1)),
        dma((2, 2, R)),
        dma((2, len(groups))),
        dma((2, len(groups), E - 1)),
        dma((2, len(groups), E - 1)),
    ]
    return pl.pallas_call(
        functools.partial(fused_kernel, dims),
        out_shape=jax.ShapeDtypeStruct((nt, model), b16),
        in_specs=[vmem, hbm, vmem, smem, smem, hbm, hbm, vmem, hbm, smem, hbm, hbm, hbm],
        out_specs=vmem,
        scratch_shapes=scratch,
        compiler_params=pltpu.CompilerParams(
            collective_id=0, has_side_effects=True, vmem_limit_bytes=56 * 1024 * 1024
        ),
        cost_estimate=pl.CostEstimate(
            flops=2 * R * drafts * (out_proj.size + 3 * w_gate.size),
            bytes_accessed=2 * (value_up.size + out_proj.size + 3 * w_gate.size),
            transcendentals=0,
        ),
    )(residual, queries, cache, blocks, lengths, value_up, out_proj, gain, router, ids, w_gate, w_up, w_down)


def per_device_fused(dims, *args):
    (residual, queries, cache, blocks, lengths, value_up, out_proj, gain, router, ids, w_gate, w_up, w_down) = args
    return fused(
        dims,
        residual,
        queries[0],
        cache[0],
        blocks[0, 0],
        lengths,
        value_up,
        out_proj,
        gain,
        router.T,
        ids,
        w_gate[0],
        w_up[0],
        w_down[0],
    )


def fits_fused(dims, shapes):
    R, S, E = dims
    residual, queries, cache, router = shapes[0], shapes[1], shapes[2], shapes[8]
    drafts, heads, model = queries[1], queries[2], residual[1]
    return (
        S == 2
        and R == E
        and queries[0] == R
        and router[1] == R
        and drafts % 16 == 0
        and residual[0] == R * drafts
        and heads % (E * S * 16) == 0
        and model % (R * S * 128) == 0
        and model // (R * S) >= 384
        and (residual[0] // E) % 16 == 0
        and (drafts // (S * E) * R * S) % 16 == 0
        and cache[1] // S % BLOCK == 0
    )


def solution(mesh):
    in_specs = (
        P(("req", "seq", "exp"), None),
        P("req", None, "exp", None),
        P("req", "seq", None),
        P("req", "seq", None),
        P("req"),
        P("exp", None, None),
        P("exp", ("req", "seq")),
        P(),
        P(),
        P(("req", "seq", "exp"), None),
        P("req", None, ("seq", "exp")),
        P("req", None, ("seq", "exp")),
        P("req", ("seq", "exp"), None),
    )
    out_specs = P(("req", "seq", "exp"), None)
    dims = (mesh.shape["req"], mesh.shape["seq"], mesh.shape["exp"])

    def layer(*args):
        fast = fits_fused(dims, [a.shape for a in args])
        body = functools.partial(per_device_fused, dims) if fast else per_device
        return jax.shard_map(body, mesh=mesh, in_specs=in_specs, out_specs=out_specs, check_vma=False)(*args)

    return layer
```

```python
import functools

import jax
import jax.numpy as jnp
from jax import lax
from jax.experimental import pallas as pl
from jax.experimental.pallas import tpu as pltpu
from jax.sharding import PartitionSpec as P

DL = 512
DR = 64
DV = 128
BLOCK = 64


def merge_parts(former, latter):
    row_max = jnp.maximum(former[0], latter[0])
    left_scale = jnp.exp(former[0] - row_max)
    right_scale = jnp.exp(latter[0] - row_max)
    return (
        row_max,
        left_scale * former[1] + right_scale * latter[1],
        left_scale[..., None] * former[2] + right_scale[..., None] * latter[2],
    )


def pick_rows(block_rows, picks):
    return block_rows[picks]


def shard_softmax(queries, picked, usable):
    scores = jnp.einsum("bqhk,bjk->bqhj", queries, picked, preferred_element_type=jnp.float32) * (
        DV + DR
    ) ** (-0.5)
    row_max = jnp.max(jnp.where(usable, scores, -1e30), axis=-1)
    weights = jnp.where(usable, jnp.exp(scores - row_max[..., None]), 0.0).astype(jnp.bfloat16)
    row_sum = jnp.sum(weights.astype(jnp.float32), -1)
    weighted = jnp.einsum(
        "bqhj,bjd->bqhd", weights, picked[..., :DL], preferred_element_type=jnp.float32
    )
    return (row_max, row_sum, weighted)


def expert_rows(arrived, w_gate, w_up, w_down):
    model_width = w_gate.shape[1]
    flat_rows = arrived.reshape(-1, model_width)
    gate_act = jnp.dot(flat_rows, w_gate[0], preferred_element_type=jnp.float32)
    up_act = jnp.dot(flat_rows, w_up[0], preferred_element_type=jnp.float32)
    activated = (jax.nn.silu(gate_act) * up_act).astype(jnp.bfloat16)
    partial_value = jnp.dot(activated, w_down[0], preferred_element_type=jnp.float32).astype(
        jnp.bfloat16
    )
    return partial_value.reshape(arrived.shape)


def per_device(
    residual,
    queries,
    latent_cache,
    blocks,
    lengths,
    value_up,
    out_proj,
    norm_gain,
    router,
    expert_ids,
    w_gate,
    w_up,
    w_down,
):
    local_reqs, drafts, head_count, qk_width = queries.shape
    shard_len = latent_cache.shape[1]
    picks_count = blocks.shape[2]
    seq_index = lax.axis_index("seq")
    block_view = latent_cache.reshape(local_reqs, shard_len // BLOCK, BLOCK, qk_width)
    picked = jax.vmap(pick_rows)(block_view, blocks[:, 0]).reshape(
        local_reqs, picks_count * BLOCK, qk_width
    )
    positions = (
        seq_index * shard_len + blocks[:, 0, :, None] * BLOCK + jnp.arange(BLOCK, dtype=jnp.int32)
    )
    positions = positions.reshape(local_reqs, picks_count * BLOCK)
    limits = lengths[:, None] - (drafts - 1) + jnp.arange(drafts, dtype=jnp.int32)[None, :]
    usable = positions[:, None, None, :] < limits[:, :, None, None]
    usable_mark = usable[:, :, 0, :].astype(jnp.bfloat16)
    all_keys, all_marks = (
        lax.all_gather(picked[None], "seq", axis=0, tiled=True),
        lax.all_gather(usable_mark[None], "seq", axis=0, tiled=True),
    )
    combined = None
    for shard in range(lax.axis_size("seq")):
        shard_usable = (all_marks[shard] > 0)[:, :, None, :]
        partial_value = shard_softmax(queries, all_keys[shard], shard_usable)
        combined = partial_value if combined is None else merge_parts(combined, partial_value)
    latent = (combined[2] / combined[1][..., None]).astype(jnp.bfloat16)
    head_values = jnp.einsum(
        "bqhd,hdv->bqhv", latent, value_up, preferred_element_type=jnp.float32
    ).astype(jnp.bfloat16)
    flat_values = head_values.reshape(local_reqs * drafts, head_count * DV)
    col_terms = jnp.dot(
        lax.all_gather(flat_values, "req", axis=0, tiled=True),
        out_proj,
        preferred_element_type=jnp.float32,
    )
    token_terms = lax.all_to_all(
        col_terms[None].astype(jnp.bfloat16),
        ("req", "seq", "exp"),
        split_axis=1,
        concat_axis=0,
        tiled=True,
    ).astype(jnp.float32)
    exp_count = lax.axis_size("exp")
    col_blocks = token_terms.shape[0] // exp_count
    rows_here = token_terms.shape[1]
    col_sums = jnp.sum(
        token_terms.reshape(col_blocks, exp_count, rows_here, token_terms.shape[2]), 1
    )
    attended = jnp.transpose(col_sums, (1, 0, 2)).reshape(rows_here, -1).astype(jnp.bfloat16)
    hidden_sum = (residual.astype(jnp.float32) + attended.astype(jnp.float32)).astype(jnp.bfloat16)
    hidden32 = hidden_sum.astype(jnp.float32)
    normed = (
        hidden32
        * lax.rsqrt(jnp.mean(hidden32 * hidden32, -1, keepdims=True) + 1e-06)
        * norm_gain.astype(jnp.float32)
    ).astype(jnp.bfloat16)
    gate_probs = jax.nn.sigmoid(jnp.dot(normed, router, preferred_element_type=jnp.float32))
    expert_count = router.shape[1]
    top_count = expert_ids.shape[1]
    one_hot = (expert_ids[:, :, None] == jnp.arange(expert_count, dtype=jnp.int32)).astype(
        jnp.int32
    )
    pair_hot = one_hot.reshape(rows_here * top_count, expert_count)
    slot_index = jnp.sum((jnp.cumsum(pair_hot, 0) - pair_hot) * pair_hot, -1)
    slot_hot = (slot_index[:, None] == jnp.arange(rows_here, dtype=jnp.int32)).astype(jnp.int32)
    placement = (pair_hot[:, :, None] * slot_hot[:, None, :]).reshape(
        rows_here, top_count, expert_count * rows_here
    )
    chosen = jnp.sum(one_hot.astype(jnp.float32) * gate_probs[:, None, :], -1)
    gate_weights = chosen / jnp.sum(chosen, -1, keepdims=True) * 2.5
    dispatch = jnp.sum(placement, 1).astype(jnp.bfloat16)
    outgoing = jnp.dot(dispatch.T, normed, preferred_element_type=jnp.float32).astype(jnp.bfloat16)
    outgoing = outgoing.reshape(expert_count, rows_here, outgoing.shape[1])
    combine = jnp.sum(gate_weights[:, :, None] * placement.astype(jnp.float32), 1)
    copies = lax.axis_size("seq") * exp_count
    fanned = jnp.broadcast_to(outgoing[:, None], (expert_count, copies) + outgoing.shape[1:])
    fanned = fanned.reshape((expert_count * copies,) + outgoing.shape[1:])
    returned = lax.all_to_all(
        expert_rows(
            lax.all_to_all(fanned, ("req", "seq", "exp"), split_axis=0, concat_axis=0, tiled=True),
            w_gate,
            w_up,
            w_down,
        ),
        ("req", "seq", "exp"),
        split_axis=0,
        concat_axis=0,
        tiled=True,
    )
    returned = returned.reshape((expert_count, copies) + outgoing.shape[1:]).astype(jnp.float32)
    expert_out = jnp.sum(returned, 1).astype(jnp.bfloat16)
    slot_rows = expert_out.reshape(expert_count * rows_here, expert_out.shape[2]).astype(
        jnp.float32
    )
    routed = jnp.dot(combine, slot_rows, precision=lax.Precision.HIGHEST)
    return (hidden32 + routed).astype(jnp.bfloat16)


MESH = pl.DeviceIdType.MESH


def column_cuts(width):
    return [(0, width - 256), (width - 256, width)]


def column_groups(width):
    cuts = column_cuts(width)
    first = min(256, cuts[0][1])
    return [(0, first)] + [(first, cuts[0][1])] * (cuts[0][1] > first) + cuts[1:]


def fused_kernel(
    dims,
    residual_ref,
    queries_hbm,
    cache_ref,
    blocks_ref,
    lengths_ref,
    value_up_hbm,
    out_proj_hbm,
    gain_ref,
    router_hbm,
    ids_ref,
    w_gate_hbm,
    w_up_hbm,
    w_down_hbm,
    out_ref,
    q_v,
    vu_v,
    op_v,
    rt_v,
    wg_v,
    wu_v,
    wd_v,
    keys_rx,
    marks,
    res_tx,
    res_rx,
    gains,
    lat,
    hv,
    acc,
    res_sum,
    hots,
    ys,
    parts_tx,
    parts_rx,
    xs,
    y_tx,
    y_rx,
    both,
    mid_tx,
    mid_rx,
    mid_sum,
    end_tx,
    end_rx,
    load_sem,
    key_sem,
    mark_sem,
    res_ssem,
    res_rsem,
    hz_sem,
    hs_sem,
    hot_sem,
    ps_sem,
    first_sem,
    second_sem,
    across_sem,
    ys_sem,
    mid_sem,
    end_sem,
):
    R, S, E = dims
    f32, b16 = jnp.float32, jnp.bfloat16
    r, s, e = lax.axis_index("req"), lax.axis_index("seq"), lax.axis_index("exp")
    other = 1 - s
    sibling = (r, other, e)
    drafts, half_heads, _ = q_v.shape
    keys_len = cache_ref.shape[0]
    width = op_v.shape[1]
    chunks = R * S
    nt = residual_ref.shape[0]
    devices = R * S * E
    mine = r * S + s
    at_home = (e == r).astype(jnp.int32)

    head_from = pl.multiple_of(s * half_heads, half_heads)
    loads = [
        pltpu.make_async_copy(queries_hbm.at[:, pl.ds(head_from, half_heads), :], q_v, load_sem.at[0]),
        pltpu.make_async_copy(value_up_hbm.at[pl.ds(head_from, half_heads)], vu_v, load_sem.at[1]),
        pltpu.make_async_copy(out_proj_hbm, op_v, load_sem.at[2]),
        pltpu.make_async_copy(router_hbm, rt_v, load_sem.at[3]),
        pltpu.make_async_copy(w_gate_hbm, wg_v, load_sem.at[4]),
        pltpu.make_async_copy(w_up_hbm, wu_v, load_sem.at[5]),
        pltpu.make_async_copy(w_down_hbm, wd_v, load_sem.at[6]),
    ]
    for load in loads:
        load.start()

    def z_peer(d):
        return (lax.rem(r + d, R), s, e)

    def e_peer(d):
        return (r, s, lax.rem(e + d, E))

    barrier = pltpu.get_barrier_semaphore()
    for peer in [sibling] + [z_peer(d) for d in range(1, R)] + [e_peer(d) for d in range(1, E)]:
        pl.semaphore_signal(barrier, inc=1, device_id=peer, device_id_type=MESH)
    for ss in range(S):
        for ee in range(E):

            @pl.when(jnp.logical_not((e == r) & (s == ss) & (e == ee)))
            def _():
                pl.semaphore_signal(barrier, inc=1, device_id=(e, ss, ee), device_id_type=MESH)

    gains[...] = gain_ref[...].astype(f32).reshape(gains.shape)
    block_of = lax.broadcasted_iota(jnp.int32, marks.shape[1:], 1) // BLOCK
    hit = block_of == blocks_ref[0]
    for i in range(1, blocks_ref.shape[0]):
        hit = hit | (block_of == blocks_ref[i])
    marks[0] = hit.astype(f32)
    lane = lax.broadcasted_iota(jnp.int32, (1, 128), 1)
    for t in range(nt):
        hot = lane == ids_ref[t, 0]
        for k in range(1, ids_ref.shape[1]):
            hot = hot | (lane == ids_ref[t, k])
        for c in range(chunks):
            res_tx[c, t : t + 1, width:] = hot.astype(f32)
    for c in range(chunks):
        res_tx[c, :, :width] = residual_ref[:, c * width : (c + 1) * width].astype(f32)

    pl.semaphore_wait(barrier, 1 + (R - 1) + (E - 1) + S * E - at_home)

    def remote(src, dst, ssem, rsem, peer):
        return pltpu.make_async_remote_copy(
            src_ref=src, dst_ref=dst, send_sem=ssem, recv_sem=rsem, device_id=peer, device_id_type=MESH
        )

    sent = []
    key_copy = remote(cache_ref, keys_rx, key_sem.at[0], key_sem.at[1], sibling)
    mark_copy = remote(marks.at[0], marks.at[1], mark_sem.at[0], mark_sem.at[1], sibling)
    key_copy.start()
    mark_copy.start()
    sent += [key_copy, mark_copy]
    slot = s * E + e
    for c in range(chunks):
        to = (c // S, c % S, r)
        here = (r == c // S) & (s == c % S) & (e == r)

        @pl.when(jnp.logical_not(here))
        def _():
            remote(res_tx.at[c], res_rx.at[slot], res_ssem.at[c], res_rsem.at[slot], to).start()

        @pl.when(here)
        def _():
            pltpu.make_async_copy(res_tx.at[c], res_rx.at[slot], res_rsem.at[slot]).start()

    loads[0].wait()
    q2 = q_v[...].reshape(drafts * half_heads, q_v.shape[2])
    rows = drafts * half_heads
    limit = lengths_ref[0] - (drafts - 1) + lax.broadcasted_iota(jnp.int32, (rows, 1), 0) // half_heads

    def scores_of(keys, mark, shard):
        sc = lax.dot_general(q2, keys, (((1,), (1,)), ((), ())), preferred_element_type=f32)
        pos = shard * keys_len + lax.broadcasted_iota(jnp.int32, (rows, keys_len), 1)
        usable = (pos < limit) & (mark > 0)
        return jnp.where(usable, sc * (DV + DR) ** (-0.5), -1e30), usable

    near, near_ok = scores_of(cache_ref[...], marks[0, :1, :keys_len], s)
    key_copy.wait_recv()
    mark_copy.wait_recv()
    far, far_ok = scores_of(keys_rx[...], marks[1, :1, :keys_len], other)
    top = jnp.maximum(jnp.max(near, -1, keepdims=True), jnp.max(far, -1, keepdims=True))
    near_p = jnp.where(near_ok, jnp.exp(near - top), 0.0).astype(b16)
    far_p = jnp.where(far_ok, jnp.exp(far - top), 0.0).astype(b16)
    total = jnp.sum(near_p.astype(f32), -1, keepdims=True) + jnp.sum(far_p.astype(f32), -1, keepdims=True)
    weighted = jnp.dot(near_p, cache_ref[:, :DL], preferred_element_type=f32)
    weighted += jnp.dot(far_p, keys_rx[:, :DL], preferred_element_type=f32)
    latent = weighted / total
    for k in range(lat.shape[0]):
        lat[k] = latent[:, k * 128 : (k + 1) * 128]

    pieces = hv.shape[1]
    piece_heads = half_heads // pieces
    depth = piece_heads * DV
    loads[1].wait()
    hz = []
    for p in range(pieces):
        for n in range(piece_heads):
            h = p * piece_heads + n
            one = [lat[k, pl.ds(h, drafts, stride=half_heads), :] for k in range(lat.shape[0])]
            one = jnp.concatenate(one, axis=1).astype(b16)
            value = jnp.dot(one, vu_v[h], preferred_element_type=f32)
            hv[s, p, r, :, n * DV : (n + 1) * DV] = value.astype(b16)
        block = hv.at[s, p, r]
        hz.append(
            [remote(block, block, hz_sem.at[0, p, d - 1], hz_sem.at[1, p, d - 1], z_peer(d)) for d in range(1, R)]
        )
        for copy in hz[p]:
            copy.start()
        sent += hz[p]

    cuts = column_cuts(width)
    loads[2].wait()

    def out_part(side, p, lo, hi):
        head_rows = hv[side, p].reshape(R * drafts, depth)
        at = pl.ds(pl.multiple_of((side * pieces + p) * depth, depth), depth)
        part = jnp.dot(head_rows, op_v[at, lo:hi], preferred_element_type=f32)
        return part.reshape(E, drafts, hi - lo)

    hs = []
    for p in range(pieces):
        for copy in hz[p]:
            copy.wait_recv()
        whole = hv.at[s, p]
        hs.append(remote(whole, whole, hs_sem.at[0, p], hs_sem.at[1, p], sibling))
        hs[p].start()
        part = out_part(s, p, 0, width)
        if p:
            hs[p - 1].wait_recv()
            part += out_part(other, p - 1, 0, width)
            acc[...] += part
        else:
            acc[...] = part
    sent += hs
    for j in range(S * E):
        pltpu.make_async_copy(res_rx.at[j], res_rx.at[j], res_rsem.at[j]).wait()
        res_sum[j * nt : (j + 1) * nt, :] = res_rx[j]
    hots[e] = res_sum[:, width:].astype(b16)
    hot_copies = [
        remote(hots.at[e], hots.at[e], hot_sem.at[0, d - 1], hot_sem.at[1, d - 1], e_peer(d)) for d in range(1, E)
    ]
    for copy in hot_copies:
        copy.start()
    sent += hot_copies
    hs[-1].wait_recv()
    ps = [None, None]
    for i in (1, 0):
        lo, hi = cuts[i]
        acc[:, :, lo:hi] += out_part(other, pieces - 1, lo, hi)
        parts_tx[i][...] = acc[:, :, lo:hi].astype(b16)
        ps[i] = [
            remote(
                parts_tx[i].at[lax.rem(e + d, E)],
                parts_rx[i].at[d - 1],
                ps_sem.at[0, i, d - 1],
                ps_sem.at[1, i, d - 1],
                e_peer(d),
            )
            for d in range(1, E)
        ]
        for copy in ps[i]:
            copy.start()
        sent += ps[i]

    def chunk_at(d):
        return lax.rem(r + R - d, R) * S + s

    first = [None, None]
    for i in (1, 0):
        lo, hi = cuts[i]
        attended = acc[e, :, lo:hi]
        for d in range(1, E):
            ps[i][d - 1].wait_recv()
            attended += parts_rx[i][d - 1].astype(f32)
        xs[i][mine, e] = (res_sum[:, lo:hi] + attended.astype(b16).astype(f32)).astype(b16)
        block = xs[i].at[mine, e]
        first[i] = [
            remote(block, block, first_sem.at[0, i, d - 1], first_sem.at[1, i, d - 1], (e_peer if i else z_peer)(d))
            for d in range(1, E if i else R)
        ]
        for copy in first[i]:
            copy.start()
        sent += first[i]
    second = [[], []]
    for hop in range(R):
        if hop:
            first[0][hop - 1].wait_recv()
        block = xs[0].at[chunk_at(hop), e]
        row = [
            remote(block, block, second_sem.at[0, 0, hop, d - 1], second_sem.at[1, 0, hop, d - 1], e_peer(d))
            for d in range(1, E)
        ]
        for copy in row:
            copy.start()
        second[0].append(row)
        sent += row
        if hop == 1:
            for copy in first[1]:
                copy.wait_recv()
            whole = xs[1].at[mine]
            second[1] = [
                remote(whole, whole, second_sem.at[0, 1, 0, d - 1], second_sem.at[1, 1, 0, d - 1], z_peer(d))
                for d in range(1, R)
            ]
            for copy in second[1]:
                copy.start()
            sent += second[1]
    for load in loads[3:6]:
        load.wait()

    tokens = E * drafts

    def expert_part(state, chunk, i):
        squares, gate, up, logits = state
        lo, hi = cuts[i]
        hid = xs[i][chunk].reshape(tokens, hi - lo).astype(f32)
        cols = pl.ds(pl.multiple_of(chunk * width + lo, 128), hi - lo)
        scaled = (hid * gains[:, cols]).astype(b16)
        return (
            squares + jnp.sum(hid * hid, -1, keepdims=True),
            gate + jnp.dot(scaled, wg_v[cols, :], preferred_element_type=f32),
            up + jnp.dot(scaled, wu_v[cols, :], preferred_element_type=f32),
            logits + lax.dot_general(scaled, rt_v[:, cols], (((1,), (1,)), ((), ())), preferred_element_type=f32),
        )

    state = (
        jnp.zeros((tokens, 1), f32),
        jnp.zeros((tokens, wg_v.shape[1]), f32),
        jnp.zeros((tokens, wg_v.shape[1]), f32),
        jnp.zeros((tokens, rt_v.shape[0]), f32),
    )
    across = []

    def arrived(state, d):
        for i in (0, 1):
            across[2 * d + i].wait_recv()
            state = expert_part(state, lax.rem(r + R - d, R) * S + other, i)
        return state

    for d in range(R):
        for i in (0, 1):
            if i == 0:
                waits = second[0][d]
            elif d == 0:
                waits = []
            else:
                waits = [second[1][d - 1]]
            for copy in waits:
                copy.wait_recv()
            whole = xs[i].at[chunk_at(d)]
            copy = remote(whole, whole, across_sem.at[0, i, d], across_sem.at[1, i, d], sibling)
            copy.start()
            across.append(copy)
            state = expert_part(state, chunk_at(d), i)
        if d:
            state = arrived(state, d - 1)
    state = arrived(state, R - 1)
    sent += across
    squares, gate, up, logits = state
    scale = lax.rsqrt(squares / (chunks * width) + 1e-06)
    experts = rt_v.shape[0]
    for copy in hot_copies:
        copy.wait_recv()
    chosen = hots[...].reshape(tokens, 128)[:, :experts].astype(f32) * jax.nn.sigmoid(logits * scale)
    this_expert = lax.broadcasted_iota(jnp.int32, (1, experts), 1) == r
    weight = jnp.sum(jnp.where(this_expert, chosen, 0.0), -1, keepdims=True)
    weight = weight / jnp.sum(chosen, -1, keepdims=True) * 2.5
    activated = (jax.nn.silu(gate * scale) * (up * scale) * weight).astype(b16)

    to_row = lax.broadcasted_iota(jnp.int32, (tokens, tokens), 0)
    from_row = lax.broadcasted_iota(jnp.int32, (tokens, tokens), 1)
    owner = to_row % devices
    wanted = ((owner % R) * (S * E) + owner // R) * nt + to_row // devices
    ordered = jnp.dot((wanted == from_row).astype(b16), activated, preferred_element_type=f32).astype(b16)
    loads[6].wait()
    per_owner = nt * chunks
    groups = column_groups(width)
    order = [len(groups) - 1] + list(range(len(groups) - 1))
    half_rows = R * E * per_owner

    def summed(side, lo, hi):
        at = pl.ds(pl.multiple_of(side * half_rows, half_rows), half_rows)
        part = jnp.concatenate([ys[k, at, :] for k in range(lo // 128, hi // 128)], axis=1)
        return part.reshape(E, R, per_owner, hi - lo)

    with_core, mid, end = {}, {}, {}

    def peers_of(g):
        return (z_peer, r, R, e_peer, e, E) if g == len(groups) - 1 else (e_peer, e, E, z_peer, r, R)

    def begin(g):
        lo, hi = groups[g]
        for c in range(chunks):
            down = jnp.dot(ordered, wd_v[:, c * width + lo : c * width + hi], preferred_element_type=f32)
            for t in range(nt):
                part = down[t * devices : (t + 1) * devices]
                for k in range(lo // 128, hi // 128):
                    column = part[:, k * 128 - lo : (k + 1) * 128 - lo]
                    ys[k, pl.ds(c * nt + t, devices, stride=per_owner), :] = column
        y_tx[g][...] = summed(other, lo, hi).astype(b16)
        with_core[g] = remote(y_tx[g], y_rx[g], ys_sem.at[0, g], ys_sem.at[1, g], sibling)
        with_core[g].start()

    def middle(g):
        lo, hi = groups[g]
        peer, me, count = peers_of(g)[:3]
        with_core[g].wait_recv()
        both[g][...] = summed(s, lo, hi) + y_rx[g][...].astype(f32)
        mid[g] = []
        for d in range(1, count):
            to = lax.rem(me + d, count)
            block = both[g][:, to] if g == len(groups) - 1 else both[g][to]
            mid_tx[g][d - 1] = block.astype(b16)
            copy = remote(
                mid_tx[g].at[d - 1], mid_rx[g].at[d - 1], mid_sem.at[0, g, d - 1], mid_sem.at[1, g, d - 1], peer(d)
            )
            copy.start()
            mid[g].append(copy)

    for n, g in enumerate(order):
        begin(g)
        if n:
            middle(order[n - 1])
    middle(order[-1])
    for g in order:
        peer, me, count = peers_of(g)[3:]
        total_g = both[g][:, r] if g == len(groups) - 1 else both[g][e]
        for d, copy in enumerate(mid[g]):
            copy.wait_recv()
            total_g += mid_rx[g][d].astype(f32)
        mid_sum[g][...] = total_g
        end_tx[g][...] = total_g.astype(b16)
        end[g] = []
        for d in range(1, count):
            to = lax.rem(me + d, count)
            copy = remote(
                end_tx[g].at[to], end_rx[g].at[d - 1], end_sem.at[0, g, d - 1], end_sem.at[1, g, d - 1], peer(d)
            )
            copy.start()
            end[g].append(copy)
        sent += [with_core[g]] + mid[g]
    pick = lax.broadcasted_iota(jnp.int32, (8, tokens), 0) + (mine * E + e) * nt
    pick = (pick == lax.broadcasted_iota(jnp.int32, (8, tokens), 1)).astype(b16)
    own = []
    for c in range(chunks):
        sides = [
            jnp.dot(pick, xs[i][c].reshape(tokens, hi - lo), preferred_element_type=f32)
            for i, (lo, hi) in enumerate(cuts)
        ]
        own.append(jnp.concatenate(sides, axis=1))
    for copy in sent:
        copy.wait_send()
    for c in range(chunks):
        here = (r == c // S) & (s == c % S) & (e == r)

        @pl.when(jnp.logical_not(here))
        def _():
            remote(res_tx.at[c], res_rx.at[slot], res_ssem.at[c], res_rsem.at[slot], (c // S, c % S, r)).wait_send()
    for g in order:
        lo, hi = groups[g]
        routed = mid_sum[g][peers_of(g)[4]]
        for d, copy in enumerate(end[g]):
            copy.wait_recv()
            routed += end_rx[g][d].astype(f32)
        for c in range(chunks):
            value = own[c][:nt, lo:hi] + routed[c * nt : (c + 1) * nt]
            out_ref[:, c * width + lo : c * width + hi] = value.astype(b16)

    for g in order:
        for copy in end[g]:
            copy.wait_send()


def fused(
    dims, residual, queries, cache, blocks, lengths, value_up, out_proj, gain, router, ids, w_gate, w_up, w_down
):
    R, S, E = dims
    f32, b16 = jnp.float32, jnp.bfloat16
    drafts, heads, qk = queries.shape
    half_heads = heads // S
    width = out_proj.shape[1]
    nt, model = residual.shape
    keys_len = cache.shape[0]
    chunks = R * S
    lanes = -(-keys_len // 128) * 128
    ff = w_gate.shape[1]
    per_owner = nt * chunks
    cuts, groups = column_cuts(width), column_groups(width)
    pieces = 2
    dma = pltpu.SemaphoreType.DMA
    vmem, smem, hbm = (pl.BlockSpec(memory_space=m) for m in (pltpu.VMEM, pltpu.SMEM, pl.ANY))
    scratch = [
        pltpu.VMEM((drafts, half_heads, qk), b16),
        pltpu.VMEM((half_heads,) + value_up.shape[1:], b16),
        pltpu.VMEM(out_proj.shape, b16),
        pltpu.VMEM(router.shape, b16),
        pltpu.VMEM(w_gate.shape, b16),
        pltpu.VMEM(w_up.shape, b16),
        pltpu.VMEM(w_down.shape, b16),
        pltpu.VMEM(cache.shape, b16),
        pltpu.VMEM((2, 8, lanes), f32),
        pltpu.VMEM((chunks, nt, width + 128), f32),
        pltpu.VMEM((S * E, nt, width + 128), f32),
        pltpu.VMEM((1, model), f32),
        pltpu.VMEM((DL // 128, drafts * half_heads, 128), f32),
        pltpu.VMEM((S, pieces, R, drafts, half_heads // pieces * DV), b16),
        pltpu.VMEM((E, drafts, width), f32),
        pltpu.VMEM((drafts, width + 128), f32),
        pltpu.VMEM((E, drafts, 128), b16),
        pltpu.VMEM((width // 128, R * S * E * per_owner, 128), f32),
        [pltpu.VMEM((E, drafts, hi - lo), b16) for lo, hi in cuts],
        [pltpu.VMEM((E - 1, drafts, hi - lo), b16) for lo, hi in cuts],
        [pltpu.VMEM((chunks, E, drafts, hi - lo), b16) for lo, hi in cuts],
        [pltpu.VMEM((E, R, per_owner, hi - lo), b16) for lo, hi in groups],
        [pltpu.VMEM((E, R, per_owner, hi - lo), b16) for lo, hi in groups],
        [pltpu.VMEM((E, R, per_owner, hi - lo), f32) for lo, hi in groups],
        [pltpu.VMEM((E - 1, R, per_owner, hi - lo), b16) for lo, hi in groups],
        [pltpu.VMEM((E - 1, R, per_owner, hi - lo), b16) for lo, hi in groups],
        [pltpu.VMEM((R, per_owner, hi - lo), f32) for lo, hi in groups],
        [pltpu.VMEM((R, per_owner, hi - lo), b16) for lo, hi in groups],
        [pltpu.VMEM((R - 1, per_owner, hi - lo), b16) for lo, hi in groups],
        dma((7,)),
        dma((2,)),
        dma((2,)),
        dma((chunks,)),
        dma((S * E,)),
        dma((2, pieces, R - 1)),
        dma((2, pieces)),
        dma((2, E - 1)),
        dma((2, 2, E - 1)),
        dma((2, 2, R - 1)),
        dma((2, 2, R, E - 1)),
        dma((2, 2, R)),
        dma((2, len(groups))),
        dma((2, len(groups), E - 1)),
        dma((2, len(groups), E - 1)),
    ]
    return pl.pallas_call(
        functools.partial(fused_kernel, dims),
        out_shape=jax.ShapeDtypeStruct((nt, model), b16),
        in_specs=[vmem, hbm, vmem, smem, smem, hbm, hbm, vmem, hbm, smem, hbm, hbm, hbm],
        out_specs=vmem,
        scratch_shapes=scratch,
        compiler_params=pltpu.CompilerParams(
            collective_id=0, has_side_effects=True, vmem_limit_bytes=56 * 1024 * 1024
        ),
        cost_estimate=pl.CostEstimate(
            flops=2 * R * drafts * (out_proj.size + 3 * w_gate.size),
            bytes_accessed=2 * (value_up.size + out_proj.size + 3 * w_gate.size),
            transcendentals=0,
        ),
    )(residual, queries, cache, blocks, lengths, value_up, out_proj, gain, router, ids, w_gate, w_up, w_down)


def per_device_fused(dims, *args):
    (residual, queries, cache, blocks, lengths, value_up, out_proj, gain, router, ids, w_gate, w_up, w_down) = args
    return fused(
        dims,
        residual,
        queries[0],
        cache[0],
        blocks[0, 0],
        lengths,
        value_up,
        out_proj,
        gain,
        router.T,
        ids,
        w_gate[0],
        w_up[0],
        w_down[0],
    )


def fits_fused(dims, shapes):
    R, S, E = dims
    residual, queries, cache, router = shapes[0], shapes[1], shapes[2], shapes[8]
    drafts, heads, model = queries[1], queries[2], residual[1]
    return (
        S == 2
        and R == E
        and queries[0] == R
        and router[1] == R
        and drafts % 16 == 0
        and residual[0] == R * drafts
        and heads % (E * S * 16) == 0
        and model % (R * S * 128) == 0
        and model // (R * S) >= 384
        and (residual[0] // E) % 16 == 0
        and (drafts // (S * E) * R * S) % 16 == 0
        and cache[1] // S % BLOCK == 0
    )


def solution(mesh):
    in_specs = (
        P(("req", "seq", "exp"), None),
        P("req", None, "exp", None),
        P("req", "seq", None),
        P("req", "seq", None),
        P("req"),
        P("exp", None, None),
        P("exp", ("req", "seq")),
        P(),
        P(),
        P(("req", "seq", "exp"), None),
        P("req", None, ("seq", "exp")),
        P("req", None, ("seq", "exp")),
        P("req", ("seq", "exp"), None),
    )
    out_specs = P(("req", "seq", "exp"), None)
    dims = (mesh.shape["req"], mesh.shape["seq"], mesh.shape["exp"])

    def layer(*args):
        fast = fits_fused(dims, [a.shape for a in args])
        body = functools.partial(per_device_fused, dims) if fast else per_device
        return jax.shard_map(body, mesh=mesh, in_specs=in_specs, out_specs=out_specs, check_vma=False)(*args)

    return layer
```

```python
import functools

import jax
import jax.numpy as jnp
from jax import lax
from jax.experimental import pallas as pl
from jax.experimental.pallas import tpu as pltpu
from jax.sharding import PartitionSpec as P

DL = 512
DR = 64
DV = 128
BLOCK = 64


def merge_parts(former, latter):
    row_max = jnp.maximum(former[0], latter[0])
    left_scale = jnp.exp(former[0] - row_max)
    right_scale = jnp.exp(latter[0] - row_max)
    return (
        row_max,
        left_scale * former[1] + right_scale * latter[1],
        left_scale[..., None] * former[2] + right_scale[..., None] * latter[2],
    )


def pick_rows(block_rows, picks):
    return block_rows[picks]


def shard_softmax(queries, picked, usable):
    scores = jnp.einsum("bqhk,bjk->bqhj", queries, picked, preferred_element_type=jnp.float32) * (
        DV + DR
    ) ** (-0.5)
    row_max = jnp.max(jnp.where(usable, scores, -1e30), axis=-1)
    weights = jnp.where(usable, jnp.exp(scores - row_max[..., None]), 0.0).astype(jnp.bfloat16)
    row_sum = jnp.sum(weights.astype(jnp.float32), -1)
    weighted = jnp.einsum(
        "bqhj,bjd->bqhd", weights, picked[..., :DL], preferred_element_type=jnp.float32
    )
    return (row_max, row_sum, weighted)


def expert_rows(arrived, w_gate, w_up, w_down):
    model_width = w_gate.shape[1]
    flat_rows = arrived.reshape(-1, model_width)
    gate_act = jnp.dot(flat_rows, w_gate[0], preferred_element_type=jnp.float32)
    up_act = jnp.dot(flat_rows, w_up[0], preferred_element_type=jnp.float32)
    activated = (jax.nn.silu(gate_act) * up_act).astype(jnp.bfloat16)
    partial_value = jnp.dot(activated, w_down[0], preferred_element_type=jnp.float32).astype(
        jnp.bfloat16
    )
    return partial_value.reshape(arrived.shape)


def per_device(
    residual,
    queries,
    latent_cache,
    blocks,
    lengths,
    value_up,
    out_proj,
    norm_gain,
    router,
    expert_ids,
    w_gate,
    w_up,
    w_down,
):
    local_reqs, drafts, head_count, qk_width = queries.shape
    shard_len = latent_cache.shape[1]
    picks_count = blocks.shape[2]
    seq_index = lax.axis_index("seq")
    block_view = latent_cache.reshape(local_reqs, shard_len // BLOCK, BLOCK, qk_width)
    picked = jax.vmap(pick_rows)(block_view, blocks[:, 0]).reshape(
        local_reqs, picks_count * BLOCK, qk_width
    )
    positions = (
        seq_index * shard_len + blocks[:, 0, :, None] * BLOCK + jnp.arange(BLOCK, dtype=jnp.int32)
    )
    positions = positions.reshape(local_reqs, picks_count * BLOCK)
    limits = lengths[:, None] - (drafts - 1) + jnp.arange(drafts, dtype=jnp.int32)[None, :]
    usable = positions[:, None, None, :] < limits[:, :, None, None]
    usable_mark = usable[:, :, 0, :].astype(jnp.bfloat16)
    all_keys, all_marks = (
        lax.all_gather(picked[None], "seq", axis=0, tiled=True),
        lax.all_gather(usable_mark[None], "seq", axis=0, tiled=True),
    )
    combined = None
    for shard in range(lax.axis_size("seq")):
        shard_usable = (all_marks[shard] > 0)[:, :, None, :]
        partial_value = shard_softmax(queries, all_keys[shard], shard_usable)
        combined = partial_value if combined is None else merge_parts(combined, partial_value)
    latent = (combined[2] / combined[1][..., None]).astype(jnp.bfloat16)
    head_values = jnp.einsum(
        "bqhd,hdv->bqhv", latent, value_up, preferred_element_type=jnp.float32
    ).astype(jnp.bfloat16)
    flat_values = head_values.reshape(local_reqs * drafts, head_count * DV)
    col_terms = jnp.dot(
        lax.all_gather(flat_values, "req", axis=0, tiled=True),
        out_proj,
        preferred_element_type=jnp.float32,
    )
    token_terms = lax.all_to_all(
        col_terms[None].astype(jnp.bfloat16),
        ("req", "seq", "exp"),
        split_axis=1,
        concat_axis=0,
        tiled=True,
    ).astype(jnp.float32)
    exp_count = lax.axis_size("exp")
    col_blocks = token_terms.shape[0] // exp_count
    rows_here = token_terms.shape[1]
    col_sums = jnp.sum(
        token_terms.reshape(col_blocks, exp_count, rows_here, token_terms.shape[2]), 1
    )
    attended = jnp.transpose(col_sums, (1, 0, 2)).reshape(rows_here, -1).astype(jnp.bfloat16)
    hidden_sum = (residual.astype(jnp.float32) + attended.astype(jnp.float32)).astype(jnp.bfloat16)
    hidden32 = hidden_sum.astype(jnp.float32)
    normed = (
        hidden32
        * lax.rsqrt(jnp.mean(hidden32 * hidden32, -1, keepdims=True) + 1e-06)
        * norm_gain.astype(jnp.float32)
    ).astype(jnp.bfloat16)
    gate_probs = jax.nn.sigmoid(jnp.dot(normed, router, preferred_element_type=jnp.float32))
    expert_count = router.shape[1]
    top_count = expert_ids.shape[1]
    one_hot = (expert_ids[:, :, None] == jnp.arange(expert_count, dtype=jnp.int32)).astype(
        jnp.int32
    )
    pair_hot = one_hot.reshape(rows_here * top_count, expert_count)
    slot_index = jnp.sum((jnp.cumsum(pair_hot, 0) - pair_hot) * pair_hot, -1)
    slot_hot = (slot_index[:, None] == jnp.arange(rows_here, dtype=jnp.int32)).astype(jnp.int32)
    placement = (pair_hot[:, :, None] * slot_hot[:, None, :]).reshape(
        rows_here, top_count, expert_count * rows_here
    )
    chosen = jnp.sum(one_hot.astype(jnp.float32) * gate_probs[:, None, :], -1)
    gate_weights = chosen / jnp.sum(chosen, -1, keepdims=True) * 2.5
    dispatch = jnp.sum(placement, 1).astype(jnp.bfloat16)
    outgoing = jnp.dot(dispatch.T, normed, preferred_element_type=jnp.float32).astype(jnp.bfloat16)
    outgoing = outgoing.reshape(expert_count, rows_here, outgoing.shape[1])
    combine = jnp.sum(gate_weights[:, :, None] * placement.astype(jnp.float32), 1)
    copies = lax.axis_size("seq") * exp_count
    fanned = jnp.broadcast_to(outgoing[:, None], (expert_count, copies) + outgoing.shape[1:])
    fanned = fanned.reshape((expert_count * copies,) + outgoing.shape[1:])
    returned = lax.all_to_all(
        expert_rows(
            lax.all_to_all(fanned, ("req", "seq", "exp"), split_axis=0, concat_axis=0, tiled=True),
            w_gate,
            w_up,
            w_down,
        ),
        ("req", "seq", "exp"),
        split_axis=0,
        concat_axis=0,
        tiled=True,
    )
    returned = returned.reshape((expert_count, copies) + outgoing.shape[1:]).astype(jnp.float32)
    expert_out = jnp.sum(returned, 1).astype(jnp.bfloat16)
    slot_rows = expert_out.reshape(expert_count * rows_here, expert_out.shape[2]).astype(
        jnp.float32
    )
    routed = jnp.dot(combine, slot_rows, precision=lax.Precision.HIGHEST)
    return (hidden32 + routed).astype(jnp.bfloat16)


MESH = pl.DeviceIdType.MESH


def column_cuts(width):
    return [(0, width - 256), (width - 256, width)]


def column_groups(width):
    cuts = column_cuts(width)
    return [(lo, min(lo + 256, cuts[0][1])) for lo in range(0, cuts[0][1], 256)] + cuts[1:]


def fused_kernel(
    dims,
    residual_ref,
    queries_hbm,
    cache_ref,
    blocks_ref,
    lengths_ref,
    value_up_hbm,
    out_proj_hbm,
    gain_ref,
    router_hbm,
    ids_ref,
    w_gate_hbm,
    w_up_hbm,
    w_down_hbm,
    out_ref,
    q_v,
    vu_v,
    op_v,
    rt_v,
    wg_v,
    wu_v,
    wd_v,
    keys_rx,
    marks,
    res_tx,
    res_rx,
    gains,
    lat,
    hv,
    acc,
    res_sum,
    hots,
    ys,
    parts_tx,
    parts_rx,
    xs,
    y_tx,
    y_rx,
    both,
    mid_tx,
    mid_rx,
    mid_sum,
    end_tx,
    end_rx,
    load_sem,
    key_sem,
    mark_sem,
    res_ssem,
    res_rsem,
    hz_sem,
    hs_sem,
    hot_sem,
    ps_sem,
    first_sem,
    second_sem,
    across_sem,
    ys_sem,
    mid_sem,
    end_sem,
):
    R, S, E = dims
    f32, b16 = jnp.float32, jnp.bfloat16
    r, s, e = lax.axis_index("req"), lax.axis_index("seq"), lax.axis_index("exp")
    other = 1 - s
    sibling = (r, other, e)
    drafts, half_heads, _ = q_v.shape
    keys_len = cache_ref.shape[0]
    width = op_v.shape[1]
    chunks = R * S
    nt = residual_ref.shape[0]
    devices = R * S * E
    mine = r * S + s
    at_home = (e == r).astype(jnp.int32)

    head_from = pl.multiple_of(s * half_heads, half_heads)
    loads = [
        pltpu.make_async_copy(queries_hbm.at[:, pl.ds(head_from, half_heads), :], q_v, load_sem.at[0]),
        pltpu.make_async_copy(value_up_hbm.at[pl.ds(head_from, half_heads)], vu_v, load_sem.at[1]),
        pltpu.make_async_copy(out_proj_hbm, op_v, load_sem.at[2]),
        pltpu.make_async_copy(router_hbm, rt_v, load_sem.at[3]),
        pltpu.make_async_copy(w_gate_hbm, wg_v, load_sem.at[4]),
        pltpu.make_async_copy(w_up_hbm, wu_v, load_sem.at[5]),
        pltpu.make_async_copy(w_down_hbm, wd_v, load_sem.at[6]),
    ]
    for load in loads:
        load.start()

    def z_peer(d):
        return (lax.rem(r + d, R), s, e)

    def e_peer(d):
        return (r, s, lax.rem(e + d, E))

    barrier = pltpu.get_barrier_semaphore()
    for peer in [sibling] + [z_peer(d) for d in range(1, R)] + [e_peer(d) for d in range(1, E)]:
        pl.semaphore_signal(barrier, inc=1, device_id=peer, device_id_type=MESH)
    for ss in range(S):
        for ee in range(E):

            @pl.when(jnp.logical_not((e == r) & (s == ss) & (e == ee)))
            def _():
                pl.semaphore_signal(barrier, inc=1, device_id=(e, ss, ee), device_id_type=MESH)

    gains[...] = gain_ref[...].astype(f32).reshape(gains.shape)
    block_of = lax.broadcasted_iota(jnp.int32, marks.shape[1:], 1) // BLOCK
    hit = block_of == blocks_ref[0]
    for i in range(1, blocks_ref.shape[0]):
        hit = hit | (block_of == blocks_ref[i])
    marks[0] = hit.astype(f32)
    lane = lax.broadcasted_iota(jnp.int32, (1, 128), 1)
    for t in range(nt):
        hot = lane == ids_ref[t, 0]
        for k in range(1, ids_ref.shape[1]):
            hot = hot | (lane == ids_ref[t, k])
        for c in range(chunks):
            res_tx[c, t : t + 1, width:] = hot.astype(f32)
    for c in range(chunks):
        res_tx[c, :, :width] = residual_ref[:, c * width : (c + 1) * width].astype(f32)

    pl.semaphore_wait(barrier, 1 + (R - 1) + (E - 1) + S * E - at_home)

    def remote(src, dst, ssem, rsem, peer):
        return pltpu.make_async_remote_copy(
            src_ref=src, dst_ref=dst, send_sem=ssem, recv_sem=rsem, device_id=peer, device_id_type=MESH
        )

    sent = []
    key_copy = remote(cache_ref, keys_rx, key_sem.at[0], key_sem.at[1], sibling)
    mark_copy = remote(marks.at[0], marks.at[1], mark_sem.at[0], mark_sem.at[1], sibling)
    key_copy.start()
    mark_copy.start()
    sent += [key_copy, mark_copy]
    slot = s * E + e
    for c in range(chunks):
        to = (c // S, c % S, r)
        here = (r == c // S) & (s == c % S) & (e == r)

        @pl.when(jnp.logical_not(here))
        def _():
            remote(res_tx.at[c], res_rx.at[slot], res_ssem.at[c], res_rsem.at[slot], to).start()

        @pl.when(here)
        def _():
            pltpu.make_async_copy(res_tx.at[c], res_rx.at[slot], res_rsem.at[slot]).start()

    loads[0].wait()
    q2 = q_v[...].reshape(drafts * half_heads, q_v.shape[2])
    rows = drafts * half_heads
    limit = lengths_ref[0] - (drafts - 1) + lax.broadcasted_iota(jnp.int32, (rows, 1), 0) // half_heads

    def scores_of(keys, mark, shard):
        sc = lax.dot_general(q2, keys, (((1,), (1,)), ((), ())), preferred_element_type=f32)
        pos = shard * keys_len + lax.broadcasted_iota(jnp.int32, (rows, keys_len), 1)
        usable = (pos < limit) & (mark > 0)
        return jnp.where(usable, sc * (DV + DR) ** (-0.5), -1e30), usable

    near, near_ok = scores_of(cache_ref[...], marks[0, :1, :keys_len], s)
    key_copy.wait_recv()
    mark_copy.wait_recv()
    far, far_ok = scores_of(keys_rx[...], marks[1, :1, :keys_len], other)
    top = jnp.maximum(jnp.max(near, -1, keepdims=True), jnp.max(far, -1, keepdims=True))
    near_p = jnp.where(near_ok, jnp.exp(near - top), 0.0).astype(b16)
    far_p = jnp.where(far_ok, jnp.exp(far - top), 0.0).astype(b16)
    total = jnp.sum(near_p.astype(f32), -1, keepdims=True) + jnp.sum(far_p.astype(f32), -1, keepdims=True)
    weighted = jnp.dot(near_p, cache_ref[:, :DL], preferred_element_type=f32)
    weighted += jnp.dot(far_p, keys_rx[:, :DL], preferred_element_type=f32)
    latent = weighted / total
    for k in range(lat.shape[0]):
        lat[k] = latent[:, k * 128 : (k + 1) * 128]

    pieces = hv.shape[1]
    piece_heads = half_heads // pieces
    depth = piece_heads * DV
    loads[1].wait()
    hz = []
    for p in range(pieces):
        for n in range(piece_heads):
            h = p * piece_heads + n
            one = [lat[k, pl.ds(h, drafts, stride=half_heads), :] for k in range(lat.shape[0])]
            one = jnp.concatenate(one, axis=1).astype(b16)
            value = jnp.dot(one, vu_v[h], preferred_element_type=f32)
            hv[s, p, r, :, n * DV : (n + 1) * DV] = value.astype(b16)
        block = hv.at[s, p, r]
        hz.append(
            [remote(block, block, hz_sem.at[0, p, d - 1], hz_sem.at[1, p, d - 1], z_peer(d)) for d in range(1, R)]
        )
        for copy in hz[p]:
            copy.start()
        sent += hz[p]

    cuts = column_cuts(width)
    loads[2].wait()

    def out_part(side, p, lo, hi):
        head_rows = hv[side, p].reshape(R * drafts, depth)
        at = pl.ds(pl.multiple_of((side * pieces + p) * depth, depth), depth)
        part = jnp.dot(head_rows, op_v[at, lo:hi], preferred_element_type=f32)
        return part.reshape(E, drafts, hi - lo)

    hs = []
    for p in range(pieces):
        for copy in hz[p]:
            copy.wait_recv()
        whole = hv.at[s, p]
        hs.append(remote(whole, whole, hs_sem.at[0, p], hs_sem.at[1, p], sibling))
        hs[p].start()
        part = out_part(s, p, 0, width)
        if p:
            hs[p - 1].wait_recv()
            part += out_part(other, p - 1, 0, width)
            acc[...] += part
        else:
            acc[...] = part
    sent += hs
    for j in range(S * E):
        pltpu.make_async_copy(res_rx.at[j], res_rx.at[j], res_rsem.at[j]).wait()
        res_sum[j * nt : (j + 1) * nt, :] = res_rx[j]
    hots[e] = res_sum[:, width:].astype(b16)
    hot_copies = [
        remote(hots.at[e], hots.at[e], hot_sem.at[0, d - 1], hot_sem.at[1, d - 1], e_peer(d)) for d in range(1, E)
    ]
    for copy in hot_copies:
        copy.start()
    sent += hot_copies
    hs[-1].wait_recv()
    ps = [None, None]
    for i in (1, 0):
        lo, hi = cuts[i]
        acc[:, :, lo:hi] += out_part(other, pieces - 1, lo, hi)
        parts_tx[i][...] = acc[:, :, lo:hi].astype(b16)
        ps[i] = [
            remote(
                parts_tx[i].at[lax.rem(e + d, E)],
                parts_rx[i].at[d - 1],
                ps_sem.at[0, i, d - 1],
                ps_sem.at[1, i, d - 1],
                e_peer(d),
            )
            for d in range(1, E)
        ]
        for copy in ps[i]:
            copy.start()
        sent += ps[i]

    def chunk_at(d):
        return lax.rem(r + R - d, R) * S + s

    def group_at(d):
        return lax.rem(e + E - d, E)

    first = [None, None]
    for i in (1, 0):
        lo, hi = cuts[i]
        attended = acc[e, :, lo:hi]
        for d in range(1, E):
            ps[i][d - 1].wait_recv()
            attended += parts_rx[i][d - 1].astype(f32)
        xs[i][mine, e] = (res_sum[:, lo:hi] + attended.astype(b16).astype(f32)).astype(b16)
        block = xs[i].at[mine, e]
        first[i] = [
            remote(block, block, first_sem.at[0, i, d - 1], first_sem.at[1, i, d - 1], (e_peer if i else z_peer)(d))
            for d in range(1, E if i else R)
        ]
        for copy in first[i]:
            copy.start()
        sent += first[i]
    second = [[], []]
    for hop in range(max(R, E)):
        for i in (1, 0):
            if hop >= (E if i else R):
                continue
            if hop:
                first[i][hop - 1].wait_recv()
            block = xs[i].at[mine, group_at(hop)] if i else xs[i].at[chunk_at(hop), e]
            row = [
                remote(
                    block,
                    block,
                    second_sem.at[0, i, hop, d - 1],
                    second_sem.at[1, i, hop, d - 1],
                    (z_peer if i else e_peer)(d),
                )
                for d in range(1, R if i else E)
            ]
            for copy in row:
                copy.start()
            second[i].append(row)
            sent += row
    for load in loads[3:6]:
        load.wait()

    tokens = E * drafts

    def expert_part(state, chunk, i):
        squares, gate, up, logits = state
        lo, hi = cuts[i]
        hid = xs[i][chunk].reshape(tokens, hi - lo).astype(f32)
        cols = pl.ds(pl.multiple_of(chunk * width + lo, 128), hi - lo)
        scaled = (hid * gains[:, cols]).astype(b16)
        return (
            squares + jnp.sum(hid * hid, -1, keepdims=True),
            gate + jnp.dot(scaled, wg_v[cols, :], preferred_element_type=f32),
            up + jnp.dot(scaled, wu_v[cols, :], preferred_element_type=f32),
            logits + lax.dot_general(scaled, rt_v[:, cols], (((1,), (1,)), ((), ())), preferred_element_type=f32),
        )

    state = (
        jnp.zeros((tokens, 1), f32),
        jnp.zeros((tokens, wg_v.shape[1]), f32),
        jnp.zeros((tokens, wg_v.shape[1]), f32),
        jnp.zeros((tokens, rt_v.shape[0]), f32),
    )
    across = []

    def arrived(state, d):
        for i in (0, 1):
            across[2 * d + i].wait_recv()
            state = expert_part(state, lax.rem(r + R - d, R) * S + other, i)
        return state

    for d in range(R):
        for i in (0, 1):
            if i == 0:
                waits = second[0][d]
            elif d == 0:
                waits = []
            else:
                waits = [row[d - 1] for row in second[1]]
            for copy in waits:
                copy.wait_recv()
            whole = xs[i].at[chunk_at(d)]
            copy = remote(whole, whole, across_sem.at[0, i, d], across_sem.at[1, i, d], sibling)
            copy.start()
            across.append(copy)
            state = expert_part(state, chunk_at(d), i)
        if d:
            state = arrived(state, d - 1)
    state = arrived(state, R - 1)
    sent += across
    squares, gate, up, logits = state
    scale = lax.rsqrt(squares / (chunks * width) + 1e-06)
    experts = rt_v.shape[0]
    for copy in hot_copies:
        copy.wait_recv()
    chosen = hots[...].reshape(tokens, 128)[:, :experts].astype(f32) * jax.nn.sigmoid(logits * scale)
    this_expert = lax.broadcasted_iota(jnp.int32, (1, experts), 1) == r
    weight = jnp.sum(jnp.where(this_expert, chosen, 0.0), -1, keepdims=True)
    weight = weight / jnp.sum(chosen, -1, keepdims=True) * 2.5
    activated = (jax.nn.silu(gate * scale) * (up * scale) * weight).astype(b16)

    to_row = lax.broadcasted_iota(jnp.int32, (tokens, tokens), 0)
    from_row = lax.broadcasted_iota(jnp.int32, (tokens, tokens), 1)
    owner = to_row % devices
    wanted = ((owner % R) * (S * E) + owner // R) * nt + to_row // devices
    ordered = jnp.dot((wanted == from_row).astype(b16), activated, preferred_element_type=f32).astype(b16)
    loads[6].wait()
    per_owner = nt * chunks
    groups = column_groups(width)
    order = [len(groups) - 1] + list(range(len(groups) - 1))
    half_rows = R * E * per_owner

    def summed(side, lo, hi):
        at = pl.ds(pl.multiple_of(side * half_rows, half_rows), half_rows)
        part = jnp.concatenate([ys[k, at, :] for k in range(lo // 128, hi // 128)], axis=1)
        return part.reshape(E, R, per_owner, hi - lo)

    with_core, mid, end = {}, {}, {}

    def peers_of(g):
        return (z_peer, r, R, e_peer, e, E) if g == len(groups) - 1 else (e_peer, e, E, z_peer, r, R)

    def begin(g):
        lo, hi = groups[g]
        for c in range(chunks):
            down = jnp.dot(ordered, wd_v[:, c * width + lo : c * width + hi], preferred_element_type=f32)
            for t in range(nt):
                part = down[t * devices : (t + 1) * devices]
                for k in range(lo // 128, hi // 128):
                    column = part[:, k * 128 - lo : (k + 1) * 128 - lo]
                    ys[k, pl.ds(c * nt + t, devices, stride=per_owner), :] = column
        y_tx[g][...] = summed(other, lo, hi).astype(b16)
        with_core[g] = remote(y_tx[g], y_rx[g], ys_sem.at[0, g], ys_sem.at[1, g], sibling)
        with_core[g].start()

    def middle(g):
        lo, hi = groups[g]
        peer, me, count = peers_of(g)[:3]
        with_core[g].wait_recv()
        both[g][...] = summed(s, lo, hi) + y_rx[g][...].astype(f32)
        mid[g] = []
        for d in range(1, count):
            to = lax.rem(me + d, count)
            block = both[g][:, to] if g == len(groups) - 1 else both[g][to]
            mid_tx[g][d - 1] = block.astype(b16)
            copy = remote(
                mid_tx[g].at[d - 1], mid_rx[g].at[d - 1], mid_sem.at[0, g, d - 1], mid_sem.at[1, g, d - 1], peer(d)
            )
            copy.start()
            mid[g].append(copy)

    for n, g in enumerate(order):
        begin(g)
        if n:
            middle(order[n - 1])
    middle(order[-1])
    pick = lax.broadcasted_iota(jnp.int32, (8, tokens), 0) + (mine * E + e) * nt
    pick = (pick == lax.broadcasted_iota(jnp.int32, (8, tokens), 1)).astype(b16)
    own = []
    for c in range(chunks):
        sides = [
            jnp.dot(pick, xs[i][c].reshape(tokens, hi - lo), preferred_element_type=f32)
            for i, (lo, hi) in enumerate(cuts)
        ]
        own.append(jnp.concatenate(sides, axis=1))
    for g in order:
        peer, me, count = peers_of(g)[3:]
        total_g = both[g][:, r] if g == len(groups) - 1 else both[g][e]
        for d, copy in enumerate(mid[g]):
            copy.wait_recv()
            total_g += mid_rx[g][d].astype(f32)
        mid_sum[g][...] = total_g
        end_tx[g][...] = total_g.astype(b16)
        end[g] = []
        for d in range(1, count):
            to = lax.rem(me + d, count)
            copy = remote(
                end_tx[g].at[to], end_rx[g].at[d - 1], end_sem.at[0, g, d - 1], end_sem.at[1, g, d - 1], peer(d)
            )
            copy.start()
            end[g].append(copy)
        sent += [with_core[g]] + mid[g]
    for copy in sent:
        copy.wait_send()
    for c in range(chunks):
        here = (r == c // S) & (s == c % S) & (e == r)

        @pl.when(jnp.logical_not(here))
        def _():
            remote(res_tx.at[c], res_rx.at[slot], res_ssem.at[c], res_rsem.at[slot], (c // S, c % S, r)).wait_send()
    for g in order:
        lo, hi = groups[g]
        routed = mid_sum[g][peers_of(g)[4]]
        for d, copy in enumerate(end[g]):
            copy.wait_recv()
            routed += end_rx[g][d].astype(f32)
        for c in range(chunks):
            value = own[c][:nt, lo:hi] + routed[c * nt : (c + 1) * nt]
            out_ref[:, c * width + lo : c * width + hi] = value.astype(b16)

    for g in order:
        for copy in end[g]:
            copy.wait_send()


def fused(
    dims, residual, queries, cache, blocks, lengths, value_up, out_proj, gain, router, ids, w_gate, w_up, w_down
):
    R, S, E = dims
    f32, b16 = jnp.float32, jnp.bfloat16
    drafts, heads, qk = queries.shape
    half_heads = heads // S
    width = out_proj.shape[1]
    nt, model = residual.shape
    keys_len = cache.shape[0]
    chunks = R * S
    lanes = -(-keys_len // 128) * 128
    ff = w_gate.shape[1]
    per_owner = nt * chunks
    cuts, groups = column_cuts(width), column_groups(width)
    pieces = 4
    dma = pltpu.SemaphoreType.DMA
    vmem, smem, hbm = (pl.BlockSpec(memory_space=m) for m in (pltpu.VMEM, pltpu.SMEM, pl.ANY))
    scratch = [
        pltpu.VMEM((drafts, half_heads, qk), b16),
        pltpu.VMEM((half_heads,) + value_up.shape[1:], b16),
        pltpu.VMEM(out_proj.shape, b16),
        pltpu.VMEM(router.shape, b16),
        pltpu.VMEM(w_gate.shape, b16),
        pltpu.VMEM(w_up.shape, b16),
        pltpu.VMEM(w_down.shape, b16),
        pltpu.VMEM(cache.shape, b16),
        pltpu.VMEM((2, 8, lanes), f32),
        pltpu.VMEM((chunks, nt, width + 128), f32),
        pltpu.VMEM((S * E, nt, width + 128), f32),
        pltpu.VMEM((1, model), f32),
        pltpu.VMEM((DL // 128, drafts * half_heads, 128), f32),
        pltpu.VMEM((S, pieces, R, drafts, half_heads // pieces * DV), b16),
        pltpu.VMEM((E, drafts, width), f32),
        pltpu.VMEM((drafts, width + 128), f32),
        pltpu.VMEM((E, drafts, 128), b16),
        pltpu.VMEM((width // 128, R * S * E * per_owner, 128), f32),
        [pltpu.VMEM((E, drafts, hi - lo), b16) for lo, hi in cuts],
        [pltpu.VMEM((E - 1, drafts, hi - lo), b16) for lo, hi in cuts],
        [pltpu.VMEM((chunks, E, drafts, hi - lo), b16) for lo, hi in cuts],
        [pltpu.VMEM((E, R, per_owner, hi - lo), b16) for lo, hi in groups],
        [pltpu.VMEM((E, R, per_owner, hi - lo), b16) for lo, hi in groups],
        [pltpu.VMEM((E, R, per_owner, hi - lo), f32) for lo, hi in groups],
        [pltpu.VMEM((E - 1, R, per_owner, hi - lo), b16) for lo, hi in groups],
        [pltpu.VMEM((E - 1, R, per_owner, hi - lo), b16) for lo, hi in groups],
        [pltpu.VMEM((R, per_owner, hi - lo), f32) for lo, hi in groups],
        [pltpu.VMEM((R, per_owner, hi - lo), b16) for lo, hi in groups],
        [pltpu.VMEM((R - 1, per_owner, hi - lo), b16) for lo, hi in groups],
        dma((7,)),
        dma((2,)),
        dma((2,)),
        dma((chunks,)),
        dma((S * E,)),
        dma((2, pieces, R - 1)),
        dma((2, pieces)),
        dma((2, E - 1)),
        dma((2, 2, E - 1)),
        dma((2, 2, R - 1)),
        dma((2, 2, R, E - 1)),
        dma((2, 2, R)),
        dma((2, len(groups))),
        dma((2, len(groups), E - 1)),
        dma((2, len(groups), E - 1)),
    ]
    return pl.pallas_call(
        functools.partial(fused_kernel, dims),
        out_shape=jax.ShapeDtypeStruct((nt, model), b16),
        in_specs=[vmem, hbm, vmem, smem, smem, hbm, hbm, vmem, hbm, smem, hbm, hbm, hbm],
        out_specs=vmem,
        scratch_shapes=scratch,
        compiler_params=pltpu.CompilerParams(
            collective_id=0, has_side_effects=True, vmem_limit_bytes=56 * 1024 * 1024
        ),
        cost_estimate=pl.CostEstimate(
            flops=2 * R * drafts * (out_proj.size + 3 * w_gate.size),
            bytes_accessed=2 * (value_up.size + out_proj.size + 3 * w_gate.size),
            transcendentals=0,
        ),
    )(residual, queries, cache, blocks, lengths, value_up, out_proj, gain, router, ids, w_gate, w_up, w_down)


def per_device_fused(dims, *args):
    (residual, queries, cache, blocks, lengths, value_up, out_proj, gain, router, ids, w_gate, w_up, w_down) = args
    return fused(
        dims,
        residual,
        queries[0],
        cache[0],
        blocks[0, 0],
        lengths,
        value_up,
        out_proj,
        gain,
        router.T,
        ids,
        w_gate[0],
        w_up[0],
        w_down[0],
    )


def fits_fused(dims, shapes):
    R, S, E = dims
    residual, queries, cache, router = shapes[0], shapes[1], shapes[2], shapes[8]
    drafts, heads, model = queries[1], queries[2], residual[1]
    return (
        S == 2
        and R == E
        and queries[0] == R
        and router[1] == R
        and drafts % 16 == 0
        and residual[0] == R * drafts
        and heads % (E * S * 16) == 0
        and model % (R * S * 128) == 0
        and model // (R * S) >= 384
        and (residual[0] // E) % 16 == 0
        and (drafts // (S * E) * R * S) % 16 == 0
        and cache[1] // S % BLOCK == 0
    )


def solution(mesh):
    in_specs = (
        P(("req", "seq", "exp"), None),
        P("req", None, "exp", None),
        P("req", "seq", None),
        P("req", "seq", None),
        P("req"),
        P("exp", None, None),
        P("exp", ("req", "seq")),
        P(),
        P(),
        P(("req", "seq", "exp"), None),
        P("req", None, ("seq", "exp")),
        P("req", None, ("seq", "exp")),
        P("req", ("seq", "exp"), None),
    )
    out_specs = P(("req", "seq", "exp"), None)
    dims = (mesh.shape["req"], mesh.shape["seq"], mesh.shape["exp"])

    def layer(*args):
        fast = fits_fused(dims, [a.shape for a in args])
        body = functools.partial(per_device_fused, dims) if fast else per_device
        return jax.shard_map(body, mesh=mesh, in_specs=in_specs, out_specs=out_specs, check_vma=False)(*args)

    return layer
```
